32 devices in a mesh: clip: 8 (over z, y), frame: 4 (over x, core).
Axes of the slice: x: 2, y: 2, z: 4, core: 2. Of those that a mesh axis runs over, the one named last changes fastest.
Arguments:
- inputs: bfloat16 [16, 8, 196, 768], P('clip', 'frame'), may hold values from -6 to 6
- out_grad: bfloat16 [16, 8, 196, 768], P('clip', 'frame'), may hold values from -6 to 6
- adapter_index: int32 [16], P('clip'), may hold values from 0 to 7, as said below
- norm_gain: bfloat16 [3, 768], P(None, 'clip'), may hold values from 0.5 to 1.5
- norm_bias: bfloat16 [3, 768], P(None, 'clip'), may hold values from -4 to 4
- qkv_weight: bfloat16 [2, 768, 2304], P(None, 'clip'), may hold values from -0.21875 to 0.21875
- proj_weight: bfloat16 [3, 768, 768], P(None, 'clip'), may hold values from -0.3125 to 0.3125
- mlp_in: bfloat16 [768, 3072], P('clip'), may hold values from -0.21875 to 0.21875
- mlp_out: bfloat16 [3072, 768], P('clip'), may hold values from -0.109375 to 0.109375
- adapt_down: bfloat16 [6, 8, 768, 16], P(None, None, 'clip'), may hold values from -0.21875 to 0.21875
- adapt_down_wide: bfloat16 [8, 3072, 16], P(None, 'clip'), may hold values from -0.109375 to 0.109375
- adapt_up_qkv: bfloat16 [2, 8, 16, 2304], P(None, None, None, 'clip'), may hold values from -1.5 to 1.5
- adapt_up: bfloat16 [4, 8, 16, 768], P(None, None, None, 'clip'), may hold values from -1.5 to 1.5
- adapt_up_wide: bfloat16 [8, 16, 3072], P(None, None, 'clip'), may hold values from -1.5 to 1.5
Outputs:
- output: bfloat16 [16, 8, 196, 768], P('clip', 'frame')
- input_grad: bfloat16 [16, 8, 196, 768], P('clip', 'frame')
- grad_down: float32 [6, 8, 768, 16], P(None, None, 'clip')
- grad_down_wide: float32 [8, 3072, 16], P(None, 'clip')
- grad_up_qkv: float32 [2, 8, 16, 2304], P(None, None, None, 'clip')
- grad_up: float32 [4, 8, 16, 768], P(None, None, None, 'clip')
- grad_up_wide: float32 [8, 16, 3072], P(None, None, 'clip')
The draws below stay inside these ranges and needn't reach their ends.
Inputs may be any that keep to these rules, and one draw needn't show every extreme that they name: `adapter_index`: every one of the 8 adapters is chosen by at least one clip.
All inputs are finite; a program needn't handle non-finite values.
Results may differ from the reference program's by a relative error of at most 0.025.
Values may be sent and summed in bfloat16 or wider, within the bound.
A program may use at most 256 MiB of HBM per device.

```python
import jax
import jax.numpy as jnp
from jax import lax

D = 768
HEADS = 12
HD = 64
FF = 3072
PATCHES = 196
RANK = 16
NADP = 8
FRAMES = 8
CLIPS = 16


def draw_adapter_index(key, part):
    key = jax.random.fold_in(key, 11)
    first_key, second_key = jax.random.split(key)
    chosen = jax.random.randint(first_key, (CLIPS,), 0, NADP)
    every = jax.random.permutation(second_key, NADP)
    return chosen.at[:NADP].set(every).astype(jnp.int32)


def block_levels(own_key, extent, shards, smallest, top_value):
    level = 1.0
    for position, parts in shards:
        draws = jax.random.uniform(jax.random.fold_in(jax.random.fold_in(own_key, 6), position), (parts,), jnp.float32, smallest / len(shards), top_value / len(shards))
        level = level * jnp.repeat(jnp.exp(draws), extent[position] // parts).reshape((-1,) + (1,) * (len(extent) - 1 - position))
    return level


def bell_draw(rng, dims, deviation, limit, cuts=(), dtype=jnp.bfloat16):
    factor_of = block_levels(rng, dims, cuts, -0.22, 0.18) if cuts else 1.0
    drawn = jax.random.normal(rng, dims, jnp.float32) * deviation * factor_of
    return jnp.minimum(jnp.maximum(drawn, -limit), limit).astype(dtype)


def setup_inputs(seed: int = 0) -> dict:
    arg_keys = jax.random.split(jax.random.key(seed), 15)
    inputs = bell_draw(arg_keys[0], (CLIPS, FRAMES, PATCHES, D), 1.0, 6.0, ((0, 8), (1, 4)))
    out_grad = bell_draw(arg_keys[1], (CLIPS, FRAMES, PATCHES, D), 1.0, 6.0, ((0, 8), (1, 4)))
    adapter_index = draw_adapter_index(jax.random.fold_in(arg_keys[14], 71), 0)
    norm_gain = jnp.clip(1.0 + 0.1 * jax.random.normal(arg_keys[3], (3, D), jnp.float32), 0.5, 1.5).astype(jnp.bfloat16)
    norm_bias = bell_draw(arg_keys[4], (3, D), 0.3, 4.0, ((1, 8),))
    qkv_weight = bell_draw(arg_keys[5], (2, D, 3 * D), D ** -0.5, 0.21875, ((1, 8),))
    proj_weight = bell_draw(arg_keys[6], (3, D, D), (D // 2) ** -0.5, 0.3125, ((1, 8),))
    mlp_in = bell_draw(arg_keys[7], (D, FF), D ** -0.5, 0.21875, ((0, 8),))
    mlp_out = bell_draw(arg_keys[8], (FF, D), FF ** -0.5, 0.109375, ((0, 8),))
    adapt_down = bell_draw(arg_keys[9], (6, NADP, D, RANK), D ** -0.5, 0.21875, ((2, 8),))
    adapt_down_wide = bell_draw(arg_keys[10], (NADP, FF, RANK), FF ** -0.5, 0.109375, ((1, 8),))
    adapt_up_qkv = bell_draw(arg_keys[11], (2, NADP, RANK, 3 * D), RANK ** -0.5, 1.5, ((3, 8),))
    adapt_up = bell_draw(arg_keys[12], (4, NADP, RANK, D), RANK ** -0.5, 1.5, ((3, 8),))
    adapt_up_wide = bell_draw(arg_keys[13], (NADP, RANK, FF), RANK ** -0.5, 1.5, ((2, 8),))
    return {"inputs": inputs, "out_grad": out_grad, "adapter_index": adapter_index, "norm_gain": norm_gain, "norm_bias": norm_bias, "qkv_weight": qkv_weight, "proj_weight": proj_weight, "mlp_in": mlp_in, "mlp_out": mlp_out, "adapt_down": adapt_down, "adapt_down_wide": adapt_down_wide, "adapt_up_qkv": adapt_up_qkv, "adapt_up": adapt_up, "adapt_up_wide": adapt_up_wide}


@jax.custom_vjp
def low(v):
    return lax.optimization_barrier(v.astype(jnp.bfloat16)).astype(jnp.float32)

@jax.custom_vjp
def low_back(v):
    return v

def low_keep(v):
    return (low(v), None)

def low_pass(kept, grad):
    return (grad,)

def back_keep(v):
    return (v, None)

def back_low(kept, grad):
    return (low(grad),)
low.defvjp(low_keep, low_pass)
low_back.defvjp(back_keep, back_low)
score_scale = 0.125
eps_norm = 1e-06

def layer_norm(values, gains, shifts):
    row_mean = lax.optimization_barrier(jnp.mean(values, axis=-1, keepdims=True))
    centred = values - row_mean
    spread = lax.optimization_barrier(jnp.mean(centred * centred, axis=-1, keepdims=True))
    return centred * lax.rsqrt(spread + eps_norm) * gains + shifts

def product(left, right):
    return jnp.einsum('...i,io->...o', left, right, precision=lax.Precision.HIGHEST)

def adapted(hidden, weight, down_factor, up_factor):
    inner_rank = low_back(low(product(hidden, down_factor)))
    return product(hidden, weight) + product(inner_rank, up_factor)

def attend(queries, key_rows, value_rows):
    scores = low_back(jnp.einsum('bshd,bthd->bhst', queries, key_rows, precision=lax.Precision.HIGHEST) * score_scale)
    attn_probs = low(jax.nn.softmax(scores, axis=-1))
    result = jnp.einsum('bhst,bthd->bshd', attn_probs, value_rows, precision=lax.Precision.HIGHEST)
    return low_back(low(result))

def reference(inputs, out_grad, adapter_index, norm_gain, norm_bias, qkv_weight, proj_weight, mlp_in, mlp_out, adapt_down, adapt_down_wide, adapt_up_qkv, adapt_up, adapt_up_wide):
    gains = norm_gain.astype(jnp.float32)
    shifts = norm_bias.astype(jnp.float32)
    w_qkv = qkv_weight.astype(jnp.float32)
    w_proj = proj_weight.astype(jnp.float32)
    w_in = mlp_in.astype(jnp.float32)
    w_out = mlp_out.astype(jnp.float32)

    def forward(stream, down_all, down_wide, up_qkv_all, up_all, up_wide):

        def one_clip(clip_item):
            clip_rows, which = clip_item
            pick_down = down_all[:, which]
            pick_down_wide = down_wide[which]
            pick_qkv = up_qkv_all[:, which]
            pick_up = up_all[:, which]
            pick_up_wide = up_wide[which]
            temporal_in = low_back(clip_rows)
            hidden_t = low(layer_norm(temporal_in, gains[0], shifts[0]))
            qkv_t = low_back(low(adapted(hidden_t, w_qkv[0], pick_down[0], pick_qkv[0])))
            qkv_t = qkv_t.reshape(FRAMES, PATCHES, 3, HEADS, HD).transpose(1, 0, 2, 3, 4)
            att_t = attend(qkv_t[:, :, 0], qkv_t[:, :, 1], qkv_t[:, :, 2])
            att_t = att_t.transpose(1, 0, 2, 3).reshape(FRAMES, PATCHES, D)
            mid_t = low_back(low(adapted(att_t, w_proj[0], pick_down[1], pick_up[0])))
            branch_t = low_back(low(adapted(mid_t, w_proj[1], pick_down[2], pick_up[1])))
            stream_one = clip_rows + branch_t
            hidden_s = low(layer_norm(stream_one, gains[1], shifts[1]))
            qkv_s = low_back(low(adapted(hidden_s, w_qkv[1], pick_down[3], pick_qkv[1])))
            qkv_s = qkv_s.reshape(FRAMES, PATCHES, 3, HEADS, HD)
            att_s = attend(qkv_s[:, :, 0], qkv_s[:, :, 1], qkv_s[:, :, 2]).reshape(FRAMES, PATCHES, D)
            branch_s = low_back(adapted(att_s, w_proj[2], pick_down[4], pick_up[2]))
            stream_two = stream_one + branch_s
            hidden_m = low(layer_norm(stream_two, gains[2], shifts[2]))
            pre_act = low_back(adapted(hidden_m, w_in, pick_down[5], pick_up_wide))
            activ = low_back(low(jax.nn.gelu(pre_act, approximate=False)))
            branch_m = low_back(adapted(activ, w_out, pick_down_wide, pick_up[3]))
            return stream_two + branch_m
        return lax.map(jax.checkpoint(one_clip), (stream, adapter_index))
    primals = (inputs.astype(jnp.float32), adapt_down.astype(jnp.float32), adapt_down_wide.astype(jnp.float32), adapt_up_qkv.astype(jnp.float32), adapt_up.astype(jnp.float32), adapt_up_wide.astype(jnp.float32))
    result, pullback = jax.vjp(forward, *primals)
    gradients = pullback(out_grad.astype(jnp.float32))
    return (result.astype(jnp.bfloat16), gradients[0].astype(jnp.bfloat16), gradients[1], gradients[2], gradients[3], gradients[4], gradients[5])
```

```python
import functools
import jax
import jax.numpy as jnp
from jax import lax
from jax.experimental import pallas as pl
from jax.experimental.pallas import tpu as pltpu
from jax.sharding import PartitionSpec as P

EPS = 1e-06
MESH = pl.DeviceIdType.MESH
f32 = jnp.float32
bf16 = jnp.bfloat16
D, FF, QKV, RANK = 768, 3072, 2304, 16
NP, GR, R = 196, 208, 832
DOWN = (0, 768, 1536, 2304, 3072, 3840, 4608)
UP = (7680, 12288, 13056, 9984, 13824, 15360, 14592)
ADW = 18432
BIG = 1e30


def dg(a, b, ca, cb):
    return lax.dot_general(a, b, (((ca,), (cb,)), ((), ())), preferred_element_type=f32)


def iota(shape, d):
    return lax.broadcasted_iota(jnp.int32, shape, d)


def cols(off, w):
    return pl.ds(off if isinstance(off, int) else pl.multiple_of(off, 128), w)


def normal_parts(v):
    e = jnp.exp(-0.5 * v * v)
    t = 1.0 / (1.0 + 0.2316419 * jnp.abs(v))
    poly = t * (
        0.127414796
        + t * (-0.142248368 + t * (0.7107068705 + t * (-0.7265760135 + t * 0.5307027145)))
    )
    tail = poly * e
    return jnp.where(v >= 0, 1.0 - tail, tail), e


def onehot(col, width):
    return jnp.where(iota((col.shape[0], width), 1) == col, 1.0, 0.0).astype(bf16)


def message_rows():
    m = iota((GR, 1), 0)
    c = jnp.where(m >= 98, 1, 0)
    rest = m - 98 * c
    f = jnp.where(rest >= 49, 1, 0)
    return m < 196, c, f, rest - 49 * f


def to_message(owner):
    ok, c, f, q = message_rows()
    return jnp.where(ok, (2 * c + f) * GR + 49 * owner + q, -1)


def from_patches(owner):
    ok, c, f, q = message_rows()
    return jnp.where(ok, 392 * c + 8 * q + 2 * owner + f, -1)


def to_patches(chunk):
    t = iota((GR, 1), 0) + chunk * GR
    c = jnp.where(t >= 392, 1, 0)
    u = t - 392 * c
    q, fr = u >> 3, u & 7
    return jnp.where(t < 784, (fr >> 1) * GR + c * 98 + (fr & 1) * 49 + q, -1)


def to_frames(g):
    p = iota((GR, 1), 0)
    d = jnp.where(p >= 49, 1, 0) + jnp.where(p >= 98, 1, 0) + jnp.where(p >= 147, 1, 0)
    return jnp.where(p < NP, d * GR + (g // 2) * 98 + (g % 2) * 49 + p - 49 * d, -1)


def clip_mask(first):
    return (iota((R, 32), 0) >= first) == (iota((R, 32), 1) >= 16)


class Part:
    def __init__(self, ref, c0=0, width=None):
        self.ref, self.c0 = ref, c0
        self.width = ref.shape[1] - c0 if width is None else width

    def get(self, rows=slice(None), off=0, width=None):
        return self.ref[rows, cols(self.c0 + off, self.width if width is None else width)]

    def put(self, val, rows=slice(None), off=0):
        self.ref[rows, cols(self.c0 + off, val.shape[1])] = val


def chunks(size, body):
    @pl.loop(0, R // size)
    def _(i):
        body(pl.ds(pl.multiple_of(i * size, size), size))


def tiles(total, tile, body):
    if total == tile:
        body(0)
    else:

        @pl.loop(0, total // tile)
        def _(i):
            body(i * tile)


def norm_rows(v):
    mean = jnp.mean(v, axis=-1, keepdims=True)
    cen = v - mean
    rstd = lax.rsqrt(jnp.mean(cen * cen, axis=-1, keepdims=True) + EPS)
    return cen * rstd, rstd


def norm_back_rows(v, gain, dh):
    hat, rstd = norm_rows(v)
    g = dh * gain
    m1 = jnp.mean(g, axis=-1, keepdims=True)
    m2 = jnp.mean(g * hat, axis=-1, keepdims=True)
    return rstd * (g - m1 - hat * m2)


def head_masks(n):
    first = iota((n, 128), 1) < 64
    one, zero = jnp.ones((n, 128), bf16), jnp.zeros((n, 128), bf16)
    return jnp.where(first, one, zero), jnp.where(first, zero, one)


def attend_pair(qkv, rows, n, off, bias, out):
    q = qkv.get(rows, off, 128)
    k = qkv.get(rows, D + off, 128)
    v = qkv.get(rows, 2 * D + off, 128)
    o = None
    for hm in head_masks(n):
        s = dg(q, k * (hm * 0.125).astype(bf16), 1, 1) + bias
        p = jnp.exp(s - jnp.max(s, axis=-1, keepdims=True))
        p = p * (1.0 / jnp.sum(p, axis=-1, keepdims=True))
        oh = dg(p.astype(bf16), v * hm, 1, 0)
        o = oh if o is None else o + oh
    out.put(o.astype(bf16), rows, off)


def attend_pair_back(qkv, rows, n, off, bias, dout):
    q = qkv.get(rows, off, 128)
    k = qkv.get(rows, D + off, 128)
    v = qkv.get(rows, 2 * D + off, 128)
    do = dout.get(rows, off, 128)
    dq, dks, dvs = None, [], []
    for hm in head_masks(n):
        kh = k * (hm * 0.125).astype(bf16)
        s = dg(q, kh, 1, 1) + bias
        p = jnp.exp(s - jnp.max(s, axis=-1, keepdims=True))
        p = p * (1.0 / jnp.sum(p, axis=-1, keepdims=True))
        dp = dg(do, v * hm, 1, 1)
        dvs.append(dg(p.astype(bf16), do, 0, 0))
        ds = (p * (dp - jnp.sum(dp * p, axis=-1, keepdims=True))).astype(bf16)
        dqh = dg(ds, kh, 1, 0)
        dq = dqh if dq is None else dq + dqh
        dks.append(dg(ds, q, 0, 0))
    first = iota((n, 128), 1) < 64
    qkv.put(dq.astype(bf16), rows, off)
    qkv.put((jnp.where(first, dks[0], dks[1]) * 0.125).astype(bf16), rows, D + off)
    qkv.put(jnp.where(first, dvs[0], dvs[1]).astype(bf16), rows, 2 * D + off)


def spatial_loop(body):
    bias = jnp.where(iota((1, GR), 1) < NP, 0.0, -BIG)

    @pl.loop(0, 24)
    def _(i):
        rows = pl.ds(pl.multiple_of((i // 6) * GR, 16), GR)
        body(rows, GR, (i % 6) * 128, bias)


def temporal_loop(body):
    def bias(n):
        return jnp.where((iota((n, n), 0) >> 3) == (iota((n, n), 1) >> 3), 0.0, -BIG)

    @pl.loop(0, 6)
    def _(i):
        for h in range(6):
            body(pl.ds(pl.multiple_of(i * 128, 128), 128), 128, h * 128, bias(128))

    for h in range(6):
        body(pl.ds(768, 64), 64, h * 128, bias(64))


def layer_kernel(
    x_ref, g_ref, ad, nm, hq, hp, hi, ho,
    out, ig, gd, spill,
    wq, wp, wi, wo, snd, rcv_a, rcv_b, buf_g, buf_d, x1, x2, tmp, o2, qkv2, a0, a1, us,
    wsem, ssem, rsem, psem,
):
    clip = lax.axis_index("clip")
    me = lax.axis_index("frame")
    nf = 4
    peers = [lax.rem(me + k, nf) for k in range(1, nf)]

    loads = {}
    for key, src, dst in (
        ("q0", hq.at[0], wq.at[0]), ("p0", hp.at[0], wp.at[0]), ("p1", hp.at[1], wp.at[1]),
        ("q1", hq.at[1], wq.at[1]), ("p2", hp.at[2], wp.at[2]), ("o", ho, wo), ("i", hi, wi),
    ):
        loads[key] = pltpu.make_async_copy(src, dst, wsem.at[len(loads)])
        loads[key].start()

    barrier = pltpu.get_barrier_semaphore()
    for d in peers:
        pl.semaphore_signal(barrier, inc=1, device_id={"clip": clip, "frame": d}, device_id_type=MESH)
    pl.semaphore_wait(barrier, nf - 1)

    def exchange(step, src, index, rcv):
        sent = []
        for k, d in enumerate(peers):
            slot = pl.ds(k * GR, GR)
            snd[slot, :] = dg(onehot(index(d), R), src.get(), 1, 0).astype(bf16)
            cp = pltpu.make_async_remote_copy(
                src_ref=snd.at[slot],
                dst_ref=rcv.at[pl.ds(pl.multiple_of(me * GR, 16), GR)],
                send_sem=ssem.at[step, k],
                recv_sem=rsem.at[step, k],
                device_id={"clip": clip, "frame": d},
                device_id_type=MESH,
            )
            cp.start()
            sent.append(cp)
        rcv[pl.ds(pl.multiple_of(me * GR, 16), GR), :] = dg(onehot(index(me), R), src.get(), 1, 0).astype(bf16)

        def finish():
            for cp in sent:
                cp.wait_recv()
            for cp in sent:
                cp.wait_send()

        return finish

    def gain(k):
        return nm[k : k + 1, :]

    def norm(k, read, put):
        def body(rows):
            hat, _ = norm_rows(read(rows))
            put(rows, (hat * gain(k) + gain(3 + k)).astype(bf16))

        chunks(64, body)

    def rank(h, at, mask, m):
        us[m] = jnp.where(mask, dg(h.get(), ad[:, pl.ds(at, h.width)], 1, 1), 0.0).astype(bf16)

    def forward(m, h, w, width, tile, mask, emit):
        rank(h, DOWN[m], mask, m)

        def body(c):
            acc = dg(h.get(), w[:, cols(c, tile)], 1, 0)
            acc = acc + dg(us[m], ad[:, cols(UP[m] + c, tile)], 1, 0)
            emit(c, acc)

        tiles(width, tile, body)

    def backward(m, dz, w, width, tile, mask, emit):
        du = jnp.where(mask, dg(dz.get(), ad[:, pl.ds(UP[m], dz.width)], 1, 1), 0.0).astype(bf16)
        us[7] = du

        def body(c):
            acc = dg(dz.get(), w[cols(c, tile), :], 1, 1)
            acc = acc + dg(us[7], ad[:, cols(DOWN[m] + c, tile)], 1, 0)
            emit(c, acc)

        tiles(width, tile, body)

    def adapter_grads(m, h, dz):
        gd[:, pl.ds(DOWN[m], h.width)] = dg(us[7], h.get(), 0, 0).astype(gd.dtype)
        gd[:, pl.ds(UP[m], dz.width)] = dg(us[m], dz.get(), 0, 0).astype(gd.dtype)

    p_a0, p_a1 = Part(a0), Part(a1)
    qkv1, h1 = Part(buf_g, 0, QKV), Part(buf_g, QKV, D)
    xt, o1, m1, spare = (Part(buf_d, D * i, D) for i in range(4))
    p_o2, p_qkv2, p_g, p_d = Part(o2), Part(qkv2), Part(buf_g), Part(buf_d)

    for src, dst in ((x_ref, a0), (g_ref, a1)):
        for g in range(4):
            dst[pl.ds(GR * g + 192, 16), :] = jnp.zeros((16, D), bf16)
            dst[pl.ds(GR * g, NP), :] = src[g // 2, g % 2]
        if dst is a0:
            arrive = exchange(0, p_a0, to_message, rcv_a)

    mask_t = clip_mask(392)
    mask_s = clip_mask(416)
    arrive()
    for i in range(4):
        xt.put(dg(onehot(to_patches(i), R), rcv_a[...], 1, 0).astype(bf16), pl.ds(i * GR, GR))
    norm(0, lambda rows: xt.get(rows).astype(f32), lambda rows, v: h1.put(v, rows))
    loads["q0"].wait()
    forward(0, h1, wq.at[0], QKV, 768, mask_t, lambda c, acc: qkv1.put(acc.astype(bf16), off=c))
    temporal_loop(lambda rows, n, off, bias: attend_pair(qkv1, rows, n, off, bias, o1))
    loads["p0"].wait()
    forward(1, o1, wp.at[0], D, 384, mask_t, lambda c, acc: m1.put(acc.astype(bf16), off=c))
    loads["p1"].wait()
    forward(2, m1, wp.at[1], D, 384, mask_t, lambda c, acc: spare.put(acc.astype(bf16), off=c))
    arrive = exchange(1, spare, from_patches, rcv_b)
    saves = [pltpu.make_async_copy(b, spill.at[i], psem.at[i]) for i, b in enumerate((buf_g, buf_d))]
    for cp in saves:
        cp.start()
    for cp in saves:
        cp.wait()

    loads["o"].wait()
    backward(6, p_a1, wo, FF, 768, mask_s, lambda c, acc: p_d.put(acc.astype(bf16), off=c))
    us[8] = us[7]
    arrive()

    for g in range(4):
        rows = pl.ds(g * GR, GR)
        tb = dg(onehot(to_frames(g), R), rcv_b[...], 1, 0)
        x1[rows, :] = a0[rows, :].astype(f32) + tb
    norm(1, lambda rows: x1[rows, :], lambda rows, v: p_o2.put(v, rows))
    loads["q1"].wait()
    forward(3, p_o2, wq.at[1], QKV, 768, mask_s, lambda c, acc: p_qkv2.put(acc.astype(bf16), off=c))
    spatial_loop(lambda rows, n, off, bias: attend_pair(p_qkv2, rows, n, off, bias, p_o2))
    loads["p2"].wait()

    def add_spatial(c, acc):
        x2[:, cols(c, 384)] = x1[:, cols(c, 384)] + acc

    forward(4, p_o2, wp.at[2], D, 384, mask_s, add_spatial)

    norm(2, lambda rows: x2[rows, :], lambda rows, v: p_a0.put(v, rows))
    loads["i"].wait()

    def activate(c, acc):
        tmp_w = acc.shape[1]
        tmp[:, pl.ds(0, tmp_w)] = acc
        @pl.loop(0, R // 32)
        def _(i):
            rows = pl.ds(pl.multiple_of(i * 32, 32), 32)
            v = tmp[rows, pl.ds(0, tmp_w)]
            phi, e = normal_parts(v)
            slope = phi + v * e * 0.3989422804014327
            p_g.put((v * phi).astype(bf16), rows, c)
            p_d.put((p_d.get(rows, c, tmp_w).astype(f32) * slope).astype(bf16), rows, c)

    forward(5, p_a0, wi, FF, 768, mask_s, activate)

    def emit_out(c, acc):
        y = (x2[:, cols(c, 384)] + acc).astype(bf16)
        for g in range(4):
            out[g // 2, g % 2, :, cols(c, 384)] = y[g * GR : g * GR + NP]

    forward(6, p_g, wo, D, 384, mask_s, emit_out)
    us[7] = us[8]
    adapter_grads(6, p_g, p_a1)

    def emit_tmp(c, acc):
        tmp[:, cols(c, 384)] = acc

    backward(5, p_d, wi, D, 384, mask_s, emit_tmp)
    adapter_grads(5, p_a0, p_d)
    loads_back = [pltpu.make_async_copy(spill.at[i], b, psem.at[i]) for i, b in enumerate((buf_g, buf_d))]
    for cp in loads_back:
        cp.start()

    def step_two(rows):
        dx = a1[rows, :].astype(f32) + norm_back_rows(x2[rows, :], gain(2), tmp[rows, :])
        x2[rows, :] = dx
        a0[rows, :] = dx.astype(bf16)

    chunks(64, step_two)

    backward(4, p_a0, wp.at[2], D, 384, mask_s, lambda c, acc: p_a1.put(acc.astype(bf16), off=c))
    adapter_grads(4, p_o2, p_a0)
    spatial_loop(lambda rows, n, off, bias: attend_pair_back(p_qkv2, rows, n, off, bias, p_a1))
    backward(3, p_qkv2, wq.at[1], D, 384, mask_s, emit_tmp)

    def step_one(rows):
        dx = x2[rows, :] + norm_back_rows(x1[rows, :], gain(1), tmp[rows, :])
        x2[rows, :] = dx
        a0[rows, :] = dx.astype(bf16)

    chunks(64, step_one)
    arrive = exchange(2, p_a0, to_message, rcv_a)
    norm(1, lambda rows: x1[rows, :], lambda rows, v: p_a1.put(v, rows))
    adapter_grads(3, p_a1, p_qkv2)
    for cp in loads_back:
        cp.wait()
    arrive()

    for i in range(4):
        p_a0.put(dg(onehot(to_patches(i), R), rcv_a[...], 1, 0).astype(bf16), pl.ds(i * GR, GR))
    backward(2, p_a0, wp.at[1], D, 384, mask_t, lambda c, acc: p_a1.put(acc.astype(bf16), off=c))
    adapter_grads(2, m1, p_a0)
    backward(1, p_a1, wp.at[0], D, 384, mask_t, lambda c, acc: spare.put(acc.astype(bf16), off=c))
    adapter_grads(1, o1, p_a1)
    temporal_loop(lambda rows, n, off, bias: attend_pair_back(qkv1, rows, n, off, bias, spare))
    backward(0, qkv1, wq.at[0], D, 384, mask_t, emit_tmp)

    def step_zero(rows):
        dx = norm_back_rows(xt.get(rows).astype(f32), gain(0), tmp[rows, :])
        a0[rows, :] = dx.astype(bf16)

    chunks(64, step_zero)
    arrive = exchange(3, p_a0, from_patches, rcv_b)
    adapter_grads(0, h1, qkv1)
    arrive()
    for g in range(4):
        dxt = dg(onehot(to_frames(g), R), rcv_b[...], 1, 0)
        total = x2[pl.ds(g * GR, GR), :] + dxt
        ig[g // 2, g % 2] = total.astype(bf16)[:NP]


def layer(x, g, ad, nm, hq, hp, hi, ho):
    vm = pl.BlockSpec(memory_space=pltpu.VMEM)
    hbm = pl.BlockSpec(memory_space=pl.ANY)
    dma = pltpu.SemaphoreType.DMA
    rows = lambda w, t=bf16: pltpu.VMEM((R, w), t)
    return pl.pallas_call(
        layer_kernel,
        out_shape=[
            jax.ShapeDtypeStruct(x.shape, bf16),
            jax.ShapeDtypeStruct(x.shape, bf16),
            jax.ShapeDtypeStruct((32, ADW), bf16),
            jax.ShapeDtypeStruct((2, R, FF), bf16),
        ],
        in_specs=[vm] * 4 + [hbm] * 4,
        out_specs=[vm] * 3 + [hbm],
        scratch_shapes=[
            pltpu.VMEM((2, D, QKV), bf16), pltpu.VMEM((3, D, D), bf16), pltpu.VMEM((D, FF), bf16), pltpu.VMEM((FF, D), bf16),
            pltpu.VMEM((3 * GR, D), bf16), rows(D), rows(D), rows(FF), rows(FF), rows(D, f32), rows(D, f32), rows(D, f32),
            rows(D), rows(QKV), rows(D), rows(D), pltpu.VMEM((9, R, 32), bf16),
            dma((7,)), dma((4, 3)), dma((4, 3)), dma((2,)),
        ],
        compiler_params=pltpu.CompilerParams(
            collective_id=1, has_side_effects=True, vmem_limit_bytes=64 * 2**20 - 2**17
        ),
        name="layer",
    )(x, g, ad, nm, hq, hp, hi, ho)


class Many:
    def __init__(self, cps):
        self.cps = cps

    def start(self):
        for cp in self.cps:
            cp.start()

    def wait_recv(self):
        for cp in self.cps:
            cp.wait_recv()

    def wait_send(self):
        for cp in self.cps:
            cp.wait_send()


def column_groups(a, lead, rows, total, width):
    return [(a, lead, 0, rows, c, width) for c in range(0, total, width)]


GROUPS = (
    [(4, None, 0, 96, 0, 1664), (4, None, 0, 96, 1664, 1536)]
    + column_groups(0, 0, 96, QKV, D)
    + [(1, 0, 0, 96, 0, D), (1, 1, 0, 96, 0, D)]
    + column_groups(0, 1, 96, QKV, D)
    + [(1, 2, 0, 96, 0, D)]
    + column_groups(2, None, 96, FF, D)
    + [(3, None, r, 96, 0, D) for r in range(0, 384, 96)]
)


def gather_kernel(n_in, *refs):
    ahead, lag = 3, 1
    groups = GROUPS
    ins = refs[:n_in]
    outs = refs[n_in : 2 * n_in]
    zs, zr, ys, yr, xs, xr, cs, cr, ls = refs[2 * n_in :]
    clip = lax.axis_index("clip")
    frame = lax.axis_index("frame")
    z, y, x, c = clip // 2, clip % 2, frame // 2, frame % 2

    def dev(zz, yy, xx, cc):
        return {"clip": zz * 2 + yy, "frame": xx * 2 + cc}

    zpeers = [lax.rem(z + k, 4) for k in (1, 2, 3)]
    ypeer, xpeer, cpeer = dev(z, 1 - y, x, c), dev(z, y, 1 - x, c), dev(z, y, x, 1 - c)
    barrier = pltpu.get_barrier_semaphore()
    for p in [dev(zz, y, x, c) for zz in zpeers] + [ypeer, xpeer, cpeer]:
        pl.semaphore_signal(barrier, inc=1, device_id=p, device_id_type=MESH)
    pl.semaphore_wait(barrier, 6)

    def src(g, off, n):
        a, lead, r0, rows, c0, width = groups[g]
        r = ins[a] if lead is None else ins[a].at[lead]
        return r.at[pl.ds(r0 + off, n), pl.ds(c0, width)]

    def dst(g, zz, yy, off, n):
        a, lead, r0, rows, c0, width = groups[g]
        r = outs[a] if lead is None else outs[a].at[lead]
        return r.at[zz, yy, pl.ds(r0 + off, n), pl.ds(c0, width)]

    def remote(s, d, ss, rs, p):
        return pltpu.make_async_remote_copy(
            src_ref=s, dst_ref=d, send_sem=ss, recv_sem=rs, device_id=p, device_id_type=MESH
        )

    def same(ref, ss, rs, p):
        return remote(ref, ref, ss, rs, p)

    ng = len(groups)
    local = []
    moved = {k: {} for k in ("z", "y", "x1", "x2", "c1", "c2")}
    for a in range(n_in):
        r, d = ins[a], outs[a]
        for s, t in (
            [(r.at[k], d.at[k, z, y]) for k in range(r.shape[0])]
            if len(r.shape) == 3
            else [(r, d.at[z, y])]
        ):
            local.append(pltpu.make_async_copy(s, t, ls.at[len(local)]))
    for cp in local:
        cp.start()
    two = pl.multiple_of(16 * (3 * c + x), 16)
    one = pl.multiple_of(16 * (3 * c + 2 * x), 16)
    half = pl.multiple_of(48 * c, 16)

    def start(kind, g, cps):
        moved[kind][g] = Many(cps)
        moved[kind][g].start()

    def start_z(g):
        start(
            "z",
            g,
            [
                remote(src(g, two, 32), dst(g, z, y, two, 32), zs.at[g, k], zr.at[g, k], dev(zpeers[k], y, x, c))
                for k in range(3)
            ],
        )

    def start_y(g):
        start("y", g, [same(dst(g, q, y, two, 32), ys.at[g, q], yr.at[g, q], ypeer) for q in range(4)])
        start(
            "x1",
            g,
            [same(dst(g, lax.rem(z + q, 4), y, one, 16), xs.at[g, 0, q], xr.at[g, 0, q], xpeer) for q in (1, 2, 3)],
        )

    def start_x(g):
        start("x2", g, [same(dst(g, q, 1 - y, one, 16), xs.at[g, 1, q], xr.at[g, 1, q], xpeer) for q in range(4)])

    def start_c(g, k):
        yy = y if k == 0 else 1 - y
        start(
            ("c1", "c2")[k],
            g,
            [
                same(dst(g, lax.rem(z + q, 4), yy, half, 48), cs.at[g, k, q], cr.at[g, k, q], cpeer)
                for q in range(1 - k, 4)
            ],
        )

    for g in range(min(ahead, ng)):
        start_z(g)
    for cp in local:
        cp.wait()
    for s in range(ng + 3 * lag):
        if s < ng:
            moved["z"][s].wait_recv()
            if s + ahead < ng:
                start_z(s + ahead)
            start_y(s)
        g = s - lag
        if 0 <= g < ng:
            moved["y"][g].wait_recv()
            start_x(g)
            moved["x1"][g].wait_recv()
            start_c(g, 0)
        g = s - 2 * lag
        if 0 <= g < ng:
            moved["x2"][g].wait_recv()
            start_c(g, 1)
        g = s - 3 * lag
        if 0 <= g < ng:
            moved["c1"][g].wait_recv()
            moved["c2"][g].wait_recv()
    for kind in moved.values():
        for m in kind.values():
            m.wait_send()


def gather(arrays):
    n, ng = len(arrays), len(GROUPS)
    shapes = []
    for a in arrays:
        lead = a.ndim == 3
        shapes.append((a.shape[0], 4, 2) + a.shape[1:] if lead else (4, 2) + a.shape)
    dma = pltpu.SemaphoreType.DMA
    return pl.pallas_call(
        functools.partial(gather_kernel, n),
        out_shape=[jax.ShapeDtypeStruct(s, a.dtype) for s, a in zip(shapes, arrays)],
        in_specs=[pl.BlockSpec(memory_space=pl.ANY)] * n,
        out_specs=[pl.BlockSpec(memory_space=pltpu.VMEM)] * n,
        scratch_shapes=[
            dma((ng, 3)), dma((ng, 3)), dma((ng, 4)), dma((ng, 4)),
            dma((ng, 2, 4)), dma((ng, 2, 4)), dma((ng, 2, 4)), dma((ng, 2, 4)), dma((8,)),
        ],
        compiler_params=pltpu.CompilerParams(
            collective_id=0, has_side_effects=True, vmem_limit_bytes=48 * 2**20
        ),
        name="gather",
    )(*arrays)


def piece_widths(w):
    return [w] * 6 + [4 * w] + [3 * w] * 2 + [w] * 4 + [4 * w]


def pack_adapters(adapt_down, adapt_down_wide, adapt_up_qkv, adapt_up, adapt_up_wide):
    adapters = adapt_down_wide.shape[0]

    def flat(v):
        return v.reshape(adapters, RANK, -1)

    return jnp.concatenate(
        [
            flat(adapt_down.transpose(1, 3, 0, 2)),
            flat(adapt_down_wide.transpose(0, 2, 1)),
            flat(adapt_up_qkv.transpose(1, 2, 0, 3)),
            flat(adapt_up.transpose(1, 2, 0, 3)),
            flat(adapt_up_wide),
        ],
        axis=-1,
    )


def join_pieces(parts, w):
    joined, at = [], 0
    for width in piece_widths(w):
        piece = parts[:, :, at : at + width]
        joined.append(piece.transpose(1, 0, 2).reshape(parts.shape[1], -1))
        at += width
    return jnp.concatenate(joined, axis=-1)


def split_pieces(rows, w, owners):
    parts, at = [], 0
    for width in piece_widths(w):
        piece = rows[:, at : at + width * owners]
        parts.append(piece.reshape(rows.shape[0], owners, width).transpose(1, 0, 2))
        at += width * owners
    return jnp.concatenate(parts, axis=-1)


def per_device(
    inputs,
    out_grad,
    adapter_index,
    norm_gain,
    norm_bias,
    qkv_weight,
    proj_weight,
    mlp_in,
    mlp_out,
    adapt_down,
    adapt_down_wide,
    adapt_up_qkv,
    adapt_up,
    adapt_up_wide,
):
    owners = lax.axis_size("clip")
    adapters = adapt_down_wide.shape[0]
    clips = inputs.shape[0]
    w = norm_gain.shape[1]
    packed = pack_adapters(adapt_down, adapt_down_wide, adapt_up_qkv, adapt_up, adapt_up_wide)
    norms = jnp.concatenate([norm_gain, norm_bias], axis=0)
    if owners == 8:
        small = jnp.concatenate(
            [packed.reshape(96, -1), jnp.pad(norms, ((0, 90), (0, 128 - w)))], axis=1
        )
        full_qkv, full_proj, full_in, full_out, table = gather(
            (qkv_weight, proj_weight, mlp_in, mlp_out, small)
        )
        full_qkv = full_qkv.reshape(2, D, QKV)
        full_proj = full_proj.reshape(3, D, D)
        full_in = full_in.reshape(D, FF)
        full_out = full_out.reshape(FF, D)
        table = table.reshape(owners, 96, -1)
        all_norms = table[:, :6, -128:][:, :, :w]
        table = table[:, :, :-128].reshape(owners, adapters, RANK, 24 * w)
    else:
        full_qkv = lax.all_gather(qkv_weight, "clip", axis=1, tiled=True)
        full_proj = lax.all_gather(proj_weight, "clip", axis=1, tiled=True)
        full_in = lax.all_gather(mlp_in, "clip", axis=0, tiled=True)
        full_out = lax.all_gather(mlp_out, "clip", axis=0, tiled=True)
        table = lax.all_gather(packed, "clip", axis=0)
        all_norms = lax.all_gather(norms, "clip", axis=0)
    nm = jnp.pad(all_norms.transpose(1, 0, 2).reshape(6, D).astype(f32), ((0, 2), (0, 0)))
    chosen = jnp.take(table, adapter_index, axis=1).reshape(owners, clips * RANK, 24 * w)
    ad = join_pieces(chosen, w)
    output, input_grad, grads, _ = layer(
        inputs, out_grad, ad, nm, full_qkv, full_proj, full_in, full_out
    )
    parts = split_pieces(grads, w, owners)
    parts = lax.all_to_all(parts, "clip", split_axis=0, concat_axis=0, tiled=True)
    every = lax.all_gather(adapter_index, "clip", axis=0, tiled=True)
    pick = (every[:, None] == jnp.arange(adapters, dtype=jnp.int32)[None, :]).astype(bf16)
    summed = jnp.einsum(
        "ca,crm->arm", pick, parts.reshape(owners * clips, RANK, 24 * w), preferred_element_type=f32
    )
    summed = lax.psum(summed.astype(bf16), "frame").astype(f32)
    return (output, input_grad) + unpack_grads(summed, w)


def unpack_grads(summed, w):
    adapters = summed.shape[0]
    down = summed[:, :, : 6 * w].reshape(adapters, RANK, 6, w).transpose(2, 0, 3, 1)
    down_wide = summed[:, :, 6 * w : 10 * w].transpose(0, 2, 1)
    up_qkv = summed[:, :, 10 * w : 16 * w].reshape(adapters, RANK, 2, 3 * w).transpose(2, 0, 1, 3)
    up = summed[:, :, 16 * w : 20 * w].reshape(adapters, RANK, 4, w).transpose(2, 0, 1, 3)
    return (down, down_wide, up_qkv, up, summed[:, :, 20 * w :])


def solution(mesh):
    return jax.shard_map(
        per_device,
        mesh=mesh,
        in_specs=(
            P("clip", "frame", None, None),
            P("clip", "frame", None, None),
            P("clip"),
            P(None, "clip"),
            P(None, "clip"),
            P(None, "clip", None),
            P(None, "clip", None),
            P("clip", None),
            P("clip", None),
            P(None, None, "clip", None),
            P(None, "clip", None),
            P(None, None, None, "clip"),
            P(None, None, None, "clip"),
            P(None, None, "clip"),
        ),
        out_specs=(
            P("clip", "frame", None, None),
            P("clip", "frame", None, None),
            P(None, None, "clip", None),
            P(None, "clip", None),
            P(None, None, None, "clip"),
            P(None, None, None, "clip"),
            P(None, None, "clip"),
        ),
        check_vma=False,
    )
```

```python
import functools
import jax
import jax.numpy as jnp
from jax import lax
from jax.experimental import pallas as pl
from jax.experimental.pallas import tpu as pltpu
from jax.sharding import PartitionSpec as P

EPS = 1e-06
MESH = pl.DeviceIdType.MESH
f32 = jnp.float32
bf16 = jnp.bfloat16
D, FF, QKV, RANK = 768, 3072, 2304, 16
NP, GR, R = 196, 208, 832
DOWN = (0, 768, 1536, 2304, 3072, 3840, 4608)
UP = (7680, 12288, 13056, 9984, 13824, 15360, 14592)
ADW = 18432
BIG = 1e30


def dg(a, b, ca, cb):
    return lax.dot_general(a, b, (((ca,), (cb,)), ((), ())), preferred_element_type=f32)


def iota(shape, d):
    return lax.broadcasted_iota(jnp.int32, shape, d)


def cols(off, w):
    return pl.ds(off if isinstance(off, int) else pl.multiple_of(off, 128), w)


def normal_parts(v):
    e = jnp.exp(-0.5 * v * v)
    t = 1.0 / (1.0 + 0.2316419 * jnp.abs(v))
    poly = t * (
        0.127414796
        + t * (-0.142248368 + t * (0.7107068705 + t * (-0.7265760135 + t * 0.5307027145)))
    )
    tail = poly * e
    return jnp.where(v >= 0, 1.0 - tail, tail), e


def onehot(col, width):
    return jnp.where(iota((col.shape[0], width), 1) == col, 1.0, 0.0).astype(bf16)


def message_rows():
    m = iota((GR, 1), 0)
    c = jnp.where(m >= 98, 1, 0)
    rest = m - 98 * c
    f = jnp.where(rest >= 49, 1, 0)
    return m < 196, c, f, rest - 49 * f


def to_message(owner):
    ok, c, f, q = message_rows()
    return jnp.where(ok, (2 * c + f) * GR + 49 * owner + q, -1)


def from_patches(owner):
    ok, c, f, q = message_rows()
    return jnp.where(ok, 392 * c + 8 * q + 2 * owner + f, -1)


def to_patches(chunk):
    t = iota((GR, 1), 0) + chunk * GR
    c = jnp.where(t >= 392, 1, 0)
    u = t - 392 * c
    q, fr = u >> 3, u & 7
    return jnp.where(t < 784, (fr >> 1) * GR + c * 98 + (fr & 1) * 49 + q, -1)


def to_frames(g):
    p = iota((GR, 1), 0)
    d = jnp.where(p >= 49, 1, 0) + jnp.where(p >= 98, 1, 0) + jnp.where(p >= 147, 1, 0)
    return jnp.where(p < NP, d * GR + (g // 2) * 98 + (g % 2) * 49 + p - 49 * d, -1)


def clip_mask(first):
    return (iota((R, 32), 0) >= first) == (iota((R, 32), 1) >= 16)


class Part:
    def __init__(self, ref, c0, width):
        self.ref, self.c0, self.width = ref, c0, width

    def get(self, rows=slice(None), off=0, width=None):
        return self.ref[rows, cols(self.c0 + off, self.width if width is None else width)]

    def put(self, val, rows=slice(None), off=0):
        self.ref[rows, cols(self.c0 + off, val.shape[1])] = val


def chunks(size, body):
    @pl.loop(0, R // size)
    def _(i):
        body(pl.ds(pl.multiple_of(i * size, size), size))


def tiles(total, tile, body, between):
    if total == tile:
        body(0)
    elif between is None:

        @pl.loop(0, total // tile)
        def _(i):
            body(i * tile)

    else:
        for c in range(0, total, tile):
            body(c)
            if c + tile < total:
                between()


def norm_rows(v):
    mean = jnp.mean(v, axis=-1, keepdims=True)
    cen = v - mean
    rstd = lax.rsqrt(jnp.mean(cen * cen, axis=-1, keepdims=True) + EPS)
    return cen * rstd, rstd


def norm_back_rows(v, gain, dh):
    hat, rstd = norm_rows(v)
    g = dh * gain
    m1 = jnp.mean(g, axis=-1, keepdims=True)
    m2 = jnp.mean(g * hat, axis=-1, keepdims=True)
    return rstd * (g - m1 - hat * m2)


def head_masks(n):
    first = iota((n, 128), 1) < 64
    one, zero = jnp.ones((n, 128), bf16), jnp.zeros((n, 128), bf16)
    return jnp.where(first, one, zero), jnp.where(first, zero, one)


def eye(n):
    return jnp.where(iota((n, n), 0) == iota((n, n), 1), 1.0, 0.0).astype(bf16)


def attend_pair(qkv, rows, n, off, bias, out):
    q = qkv.get(rows, off, 128)
    k = qkv.get(rows, D + off, 128)
    v_t = dg(eye(128), qkv.get(rows, 2 * D + off, 128), 1, 1).astype(bf16)
    parts = []
    for h, hm in enumerate(head_masks(n)):
        s = dg(k * (hm * 0.125).astype(bf16), q, 1, 1) + bias
        p = jnp.exp(s - jnp.max(s, axis=0, keepdims=True))
        total = jnp.sum(p, axis=0, keepdims=True)
        parts.append(dg(v_t[64 * h : 64 * h + 64], p.astype(bf16), 1, 0) * (1.0 / total))
    o_t = jnp.concatenate(parts, axis=0).astype(bf16)
    out.put(dg(eye(n), o_t, 1, 1).astype(bf16), rows, off)


def attend_pair_back(qkv, rows, n, off, bias, dout):
    q = qkv.get(rows, off, 128)
    k = qkv.get(rows, D + off, 128)
    v = qkv.get(rows, 2 * D + off, 128)
    do = dout.get(rows, off, 128)
    k_t = (dg(eye(128), k, 1, 1) * 0.125).astype(bf16)
    dq_t, dks, dvs = [], [], []
    for h, hm in enumerate(head_masks(n)):
        s = dg(k * (hm * 0.125).astype(bf16), q, 1, 1) + bias
        p = jnp.exp(s - jnp.max(s, axis=0, keepdims=True))
        p = p * (1.0 / jnp.sum(p, axis=0, keepdims=True))
        dp = dg(v * hm, do, 1, 1)
        dvs.append(dg(p.astype(bf16), do, 1, 0))
        ds = (p * (dp - jnp.sum(dp * p, axis=0, keepdims=True))).astype(bf16)
        dq_t.append(dg(k_t[64 * h : 64 * h + 64], ds, 1, 0))
        dks.append(dg(ds, q, 1, 0))
    first = iota((n, 128), 1) < 64
    dq = dg(eye(n), jnp.concatenate(dq_t, axis=0).astype(bf16), 1, 1)
    qkv.put(dq.astype(bf16), rows, off)
    qkv.put((jnp.where(first, dks[0], dks[1]) * 0.125).astype(bf16), rows, D + off)
    qkv.put(jnp.where(first, dvs[0], dvs[1]).astype(bf16), rows, 2 * D + off)


def spatial_loop(body, between=None):
    bias = jnp.where(iota((GR, 1), 0) < NP, 0.0, -BIG)

    def group(g):
        @pl.loop(0, 6)
        def _(i):
            body(pl.ds(g * GR if isinstance(g, int) else pl.multiple_of(g * GR, 16), GR), GR, i * 128, bias)

    if between is None:
        pl.loop(0, 4)(group)
    else:
        for g in range(4):
            group(g)
            between()


def temporal_loop(body, between=None):
    def bias(n):
        return jnp.where((iota((n, n), 0) >> 3) == (iota((n, n), 1) >> 3), 0.0, -BIG)

    def block(i, n):
        rows = pl.ds(i * 128 if isinstance(i, int) else pl.multiple_of(i * 128, 128), n)
        for u in range(6):
            body(rows, n, u * 128, bias(n))

    if between is None:
        pl.loop(0, 6)(lambda i: block(i, 128))
    else:
        for k in range(3):
            pl.loop(2 * k, 2 * k + 2)(lambda i: block(i, 128))
            between()
    block(6, 64)


class Many:
    def __init__(self, cps):
        self.cps = cps
        for cp in cps:
            cp.start()

    def wait_recv(self):
        for cp in self.cps:
            cp.wait_recv()

    def wait_send(self):
        for cp in self.cps:
            cp.wait_send()


def gather_groups():
    out = [("ad", "table", None, 32 * k, 32, 0, 0, FF) for k in range(4)]
    out += [("q0", "q", 0, 0, 96, 16, c, D) for c in range(0, QKV, D)]
    out += [("p0", "p", 0, 0, 96, 16, 0, D), ("p1", "p", 1, 0, 96, 16, 0, D)]
    out += [("q1", "q", 1, 0, 96, 16, c, D) for c in range(0, QKV, D)]
    out += [("p2", "p", 2, 0, 96, 16, 0, D)]
    out += [("o", "o", None, r, 96, 16, 0, D) for r in range(0, 384, 96)]
    out += [("i", "i", None, 0, 96, 16, c, D) for c in range(0, FF, D)]
    return out


class Gather:
    def __init__(self, srcs, dsts, sems, local, ahead=3, lag=1):
        self.groups = gather_groups()
        self.srcs, self.dsts, self.sems = srcs, dsts, sems
        self.ahead, self.lag = ahead, lag
        clip, frame = lax.axis_index("clip"), lax.axis_index("frame")
        self.z, self.y, self.x, self.c = clip // 2, clip % 2, frame // 2, frame % 2
        z, y, x, c = self.z, self.y, self.x, self.c
        self.zpeers = [self.dev(lax.rem(z + k, 4), y, x, c) for k in (1, 2, 3)]
        self.ypeer, self.xpeer, self.cpeer = self.dev(z, 1 - y, x, c), self.dev(z, y, 1 - x, c), self.dev(z, y, x, 1 - c)
        self.moved = {k: {} for k in ("z", "y", "x1", "x2", "c1", "c2")}
        self.step = 0
        self.local = local

    @staticmethod
    def dev(z, y, x, c):
        return {"clip": z * 2 + y, "frame": x * 2 + c}

    def peers(self):
        return self.zpeers + [self.ypeer, self.xpeer, self.cpeer]

    def span(self, g, first, count):
        _, _, _, r0, rows, unit, c0, width = self.groups[g]
        if unit:
            return pl.multiple_of(r0 + unit * first, 16), unit * count, c0, width
        return r0, rows, pl.multiple_of(512 * first, 512), 512 * count

    def src(self, g, span):
        key, name, lead = self.groups[g][:3]
        r = self.srcs[name] if lead is None else self.srcs[name].at[lead]
        return r.at[pl.ds(span[0], span[1]), pl.ds(span[2], span[3])]

    def dst(self, g, z, y, span):
        key, name, lead = self.groups[g][:3]
        cs = pl.ds(span[2], span[3])
        if name == "table":
            return self.dsts[name].at[z // 2, pl.ds(pl.multiple_of(((z % 2) * 2 + y) * 128 + span[0], 16), span[1]), cs]
        r = self.dsts[name] if lead is None else self.dsts[name].at[lead]
        per = 384 if name == "o" else 96
        return r.at[pl.ds(pl.multiple_of((z * 2 + y) * per + span[0], 16), span[1]), cs]

    def remote(self, kind, i, s, d, peer):
        return pltpu.make_async_remote_copy(
            src_ref=s,
            dst_ref=d,
            send_sem=self.sems[0].at[kind + i],
            recv_sem=self.sems[1].at[kind + i],
            device_id=peer,
            device_id_type=MESH,
        )

    def relay(self, g, kind, items, span, peer):
        return Many(
            [self.remote(22 * g + kind, i, self.dst(g, zz, yy, span), self.dst(g, zz, yy, span), peer) for i, (zz, yy) in items]
        )

    def start_z(self, g):
        two = self.span(g, 3 * self.c + self.x, 2)
        self.moved["z"][g] = Many(
            [self.remote(22 * g, k, self.src(g, two), self.dst(g, self.z, self.y, two), p) for k, p in enumerate(self.zpeers)]
        )

    def begin(self):
        for g in range(self.ahead):
            self.start_z(g)

    def others(self, first):
        return [(q, lax.rem(self.z + q, 4)) for q in range(first, 4)]

    def tick(self):
        s, lag, ng, m, y = self.step, self.lag, len(self.groups), self.moved, self.y
        if s >= ng + 3 * lag:
            return False
        self.step += 1
        if s == 0:
            for cp in self.local:
                cp.wait()
        two, one, half = (3 * self.c + self.x, 2), (3 * self.c + 2 * self.x, 1), (3 * self.c, 3)
        if s < ng:
            m["z"][s].wait_recv()
            if s + self.ahead < ng:
                self.start_z(s + self.ahead)
            m["y"][s] = self.relay(s, 3, [(q, (zz, y)) for q, zz in self.others(0)], self.span(s, *two), self.ypeer)
            m["x1"][s] = self.relay(s, 7, [(q - 1, (zz, y)) for q, zz in self.others(1)], self.span(s, *one), self.xpeer)
        g = s - lag
        if 0 <= g < ng:
            m["y"][g].wait_recv()
            m["x2"][g] = self.relay(g, 10, [(q, (zz, 1 - y)) for q, zz in self.others(0)], self.span(g, *one), self.xpeer)
            m["x1"][g].wait_recv()
            m["c1"][g] = self.relay(g, 14, [(q - 1, (zz, y)) for q, zz in self.others(1)], self.span(g, *half), self.cpeer)
        g = s - 2 * lag
        if 0 <= g < ng:
            m["x2"][g].wait_recv()
            m["c2"][g] = self.relay(g, 17, [(q, (zz, 1 - y)) for q, zz in self.others(0)], self.span(g, *half), self.cpeer)
        g = s - 3 * lag
        if 0 <= g < ng:
            m["c1"][g].wait_recv()
            m["c2"][g].wait_recv()
        return True

    def need(self, key):
        last = max(i for i, g in enumerate(self.groups) if g[0] == key)
        while self.step <= last + 3 * self.lag:
            self.tick()

    def sent(self, key):
        for g, group in enumerate(self.groups):
            for kind in self.moved.values():
                if g in kind and group[0] in (key or group[0]):
                    kind.pop(g).wait_send()

    def finish(self):
        while self.tick():
            pass
        self.sent(None)


PIECES = [(i, 1) for i in range(6)] + [(6, 4), (10, 3), (13, 3)] + [(16 + i, 1) for i in range(4)] + [(20, 4)]


def piece_slots():
    for first, count in PIECES:
        for i in range(8 * count):
            yield first + i // 8, i % 8, i // count, first + i % count


def placement():
    row, col = iota((1024, D), 0), iota((1024, D), 1)
    slot, lane = row >> 7, row & 127
    return jnp.where((col == slot * 96 + lane) & (lane < 96), 1.0, 0.0).astype(bf16)


def layer_kernel(
    gathers, idx, x_ref, g_ref, hq, hp, hi, ho, had, hnm,
    out, ig, gd, spill,
    wq, wp, wi, wo, ad, nm, nbuf, snd, rcv_a, rcv_b, big, x1, x2, tmp, o2, qkv2, a0, a1, us,
    wsem, ssem, rsem, psem, gssem, grsem, nsem,
):
    buf_g, buf_d = big.at[0], big.at[1]
    clip = lax.axis_index("clip")
    me = lax.axis_index("frame")
    nf = 4
    peers = [lax.rem(me + k, nf) for k in range(1, nf)]

    fetch = [pltpu.make_async_copy(s, d, wsem.at[9 + i]) for i, (s, d) in enumerate(((x_ref, ig), (g_ref, out)))]
    for cp in fetch:
        cp.start()
    barrier = pltpu.get_barrier_semaphore()
    groups_of = [{"clip": clip, "frame": d} for d in peers]
    loads = {}
    if gathers:
        own = pl.ds(pl.multiple_of(clip * 96, 16), 96)
        local = [
            (hq.at[0], wq.at[0, own]), (hq.at[1], wq.at[1, own]), (hp.at[0], wp.at[0, own]), (hp.at[1], wp.at[1, own]),
            (hp.at[2], wp.at[2, own]), (hi, wi.at[own]), (ho, wo.at[pl.ds(pl.multiple_of(clip * 384, 16), 384)]),
            (had, big.at[clip // 4, pl.ds(pl.multiple_of((clip % 4) * 128, 16), 128)]),
            (hnm, nbuf.at[pl.ds(pl.multiple_of(clip * 16, 16), 16)]),
        ]
        local = [pltpu.make_async_copy(s, d, wsem.at[i]) for i, (s, d) in enumerate(local)]
        for cp in local:
            cp.start()
        net = Gather(
            {"q": hq, "p": hp, "i": hi, "o": ho, "table": had},
            {"q": wq, "p": wp, "i": wi, "o": wo, "table": big},
            (gssem, grsem),
            local,
        )
        owners = [{"clip": lax.rem(clip + k, 8), "frame": me} for k in range(1, 8)]
        greet = groups_of + owners
    else:
        net = None
        for key, src, dst in (
            ("q0", hq.at[0], wq.at[0]), ("p0", hp.at[0], wp.at[0]), ("p1", hp.at[1], wp.at[1]), ("q1", hq.at[1], wq.at[1]),
            ("p2", hp.at[2], wp.at[2]), ("o", ho, wo), ("i", hi, wi), ("ad", had, ad), ("nm", hnm, nm),
        ):
            loads[key] = pltpu.make_async_copy(src, dst, wsem.at[len(loads)])
            loads[key].start()
        greet = groups_of
    for p in greet:
        pl.semaphore_signal(barrier, inc=1, device_id=p, device_id_type=MESH)
    pl.semaphore_wait(barrier, len(greet))

    def need(key):
        if net is None:
            loads[key].wait()
        else:
            net.need(key)

    def tick():
        if net is not None:
            net.tick()

    if gathers:
        net.begin()
        mine = pl.ds(pl.multiple_of(clip * 16, 16), 16)
        norms = [
            pltpu.make_async_remote_copy(
                src_ref=hnm, dst_ref=nbuf.at[mine], send_sem=nsem.at[0, k], recv_sem=nsem.at[1, k], device_id=p, device_id_type=MESH
            )
            for k, p in enumerate(owners)
        ]
        for cp in norms:
            cp.start()

    def exchange(step, src, index, rcv):
        sent = []
        for k, d in enumerate(peers):
            slot = pl.ds(k * GR, GR)
            snd[slot, :] = dg(onehot(index(d), R), src.get(), 1, 0).astype(bf16)
            cp = pltpu.make_async_remote_copy(
                src_ref=snd.at[slot],
                dst_ref=rcv.at[pl.ds(pl.multiple_of(me * GR, 16), GR)],
                send_sem=ssem.at[step, k],
                recv_sem=rsem.at[step, k],
                device_id={"clip": clip, "frame": d},
                device_id_type=MESH,
            )
            cp.start()
            sent.append(cp)
        rcv[pl.ds(pl.multiple_of(me * GR, 16), GR), :] = dg(onehot(index(me), R), src.get(), 1, 0).astype(bf16)

        def finish():
            for cp in sent:
                cp.wait_recv()
            for cp in sent:
                cp.wait_send()

        return finish

    def gain(k):
        return nm[k : k + 1, :]

    def norm(k, read, put):
        def body(rows):
            hat, _ = norm_rows(read(rows))
            put(rows, (hat * gain(k) + gain(3 + k)).astype(bf16))

        chunks(64, body)

    def rank(h, at, mask, m):
        us[m] = jnp.where(mask, dg(h.get(), ad[:, pl.ds(at, h.width)], 1, 1), 0.0).astype(bf16)

    def forward(m, h, w, width, tile, mask, emit, between=None):
        rank(h, DOWN[m], mask, m)

        def body(c):
            acc = dg(h.get(), w[:, cols(c, tile)], 1, 0)
            acc = acc + dg(us[m], ad[:, cols(UP[m] + c, tile)], 1, 0)
            emit(c, acc)

        tiles(width, tile, body, between)

    def backward(m, dz, w, width, tile, mask, emit, between=None):
        du = jnp.where(mask, dg(dz.get(), ad[:, pl.ds(UP[m], dz.width)], 1, 1), 0.0).astype(bf16)
        us[7] = du

        def body(c):
            acc = dg(dz.get(), w[cols(c, tile), :], 1, 1)
            acc = acc + dg(us[7], ad[:, cols(DOWN[m] + c, tile)], 1, 0)
            emit(c, acc)

        tiles(width, tile, body, between)

    def adapter_grads(m, h, dz):
        gd[:, pl.ds(DOWN[m], h.width)] = dg(us[7], h.get(), 0, 0).astype(gd.dtype)
        gd[:, pl.ds(UP[m], dz.width)] = dg(us[m], dz.get(), 0, 0).astype(gd.dtype)

    p_a0, p_a1 = Part(a0, 0, D), Part(a1, 0, D)
    qkv1, h1 = Part(buf_g, 0, QKV), Part(buf_g, QKV, D)
    xt, o1, m1, spare = (Part(buf_d, D * i, D) for i in range(4))
    p_o2, p_qkv2, p_g, p_d = Part(o2, 0, D), Part(qkv2, 0, QKV), Part(buf_g, 0, FF), Part(buf_d, 0, FF)

    for i, (src, dst) in enumerate(((ig, a0), (out, a1))):
        fetch[i].wait()
        for g in range(4):
            dst[pl.ds(GR * g + 192, 16), :] = jnp.zeros((16, D), bf16)
            dst[pl.ds(GR * g, NP), :] = src[g // 2, g % 2]
        if dst is a0:
            arrive = exchange(0, p_a0, to_message, rcv_a)

    mask_t = clip_mask(392)
    mask_s = clip_mask(416)
    if gathers:
        tick()
        net.need("ad")
        net.sent(["ad"])
        wanted = iota((32, 1), 0)
        wanted = jnp.where(wanted < RANK, idx[0] * RANK + wanted, idx[1] * RANK + wanted - RANK)
        pick = onehot(wanted, 128)
        for owner in range(8):
            rows = pl.ds((owner % 4) * 128, 128)
            part = dg(pick, big[owner // 4, rows, :], 1, 0).astype(bf16)
            for block, slot, of, piece in piece_slots():
                if of == owner:
                    qkv2[pl.ds(block * 32, 32), pl.ds(slot * 128, 128)] = part[:, piece * 128 : piece * 128 + 128]
        place = placement()
        joined = dg(qkv2[pl.ds(0, 768), pl.ds(0, 1024)], place, 1, 0).astype(bf16)
        for block in range(24):
            ad[:, pl.ds(block * D, D)] = joined[block * 32 : block * 32 + 32]
        for cp in norms:
            cp.wait_recv()
        for j in range(8):
            qkv2[pl.ds(0, 16), pl.ds(j * 128, 128)] = nbuf[pl.ds(16 * j, 16), :]
        nm[...] = dg(qkv2[pl.ds(0, 16), pl.ds(0, 1024)], place, 1, 0)
    else:
        need("ad")
        need("nm")
    arrive()
    for i in range(4):
        xt.put(dg(onehot(to_patches(i), R), rcv_a[...], 1, 0).astype(bf16), pl.ds(i * GR, GR))
    norm(0, lambda rows: xt.get(rows).astype(f32), lambda rows, v: h1.put(v, rows))
    need("q0")
    forward(0, h1, wq.at[0], QKV, 768, mask_t, lambda c, acc: qkv1.put(acc.astype(bf16), off=c), tick)
    temporal_loop(lambda rows, n, off, bias: attend_pair(qkv1, rows, n, off, bias, o1), tick)
    need("p0")
    forward(1, o1, wp.at[0], D, 384, mask_t, lambda c, acc: m1.put(acc.astype(bf16), off=c))
    need("p1")
    forward(2, m1, wp.at[1], D, 384, mask_t, lambda c, acc: spare.put(acc.astype(bf16), off=c))
    tick()
    arrive = exchange(1, spare, from_patches, rcv_b)
    tick()
    saves = [pltpu.make_async_copy(b, spill.at[i], psem.at[i]) for i, b in enumerate((buf_g, buf_d))]
    for cp in saves:
        cp.start()
    for cp in saves:
        cp.wait()

    need("o")
    backward(6, p_a1, wo, FF, 768, mask_s, lambda c, acc: p_d.put(acc.astype(bf16), off=c))
    us[8] = us[7]
    arrive()

    for g in range(4):
        rows = pl.ds(g * GR, GR)
        tb = dg(onehot(to_frames(g), R), rcv_b[...], 1, 0)
        x1[rows, :] = a0[rows, :].astype(f32) + tb
    norm(1, lambda rows: x1[rows, :], lambda rows, v: p_o2.put(v, rows))
    need("q1")
    forward(3, p_o2, wq.at[1], QKV, 768, mask_s, lambda c, acc: p_qkv2.put(acc.astype(bf16), off=c), tick)
    spatial_loop(lambda rows, n, off, bias: attend_pair(p_qkv2, rows, n, off, bias, p_o2), tick)
    need("p2")

    def add_spatial(c, acc):
        x2[:, cols(c, 384)] = x1[:, cols(c, 384)] + acc

    forward(4, p_o2, wp.at[2], D, 384, mask_s, add_spatial)

    norm(2, lambda rows: x2[rows, :], lambda rows, v: p_a0.put(v, rows))
    need("i")

    def activate(c, acc):
        tmp_w = acc.shape[1]
        tmp[:, pl.ds(0, tmp_w)] = acc
        @pl.loop(0, R // 32)
        def _(i):
            rows = pl.ds(pl.multiple_of(i * 32, 32), 32)
            v = tmp[rows, pl.ds(0, tmp_w)]
            phi, e = normal_parts(v)
            slope = phi + v * e * 0.3989422804014327
            p_g.put((v * phi).astype(bf16), rows, c)
            p_d.put((p_d.get(rows, c, tmp_w).astype(f32) * slope).astype(bf16), rows, c)

    forward(5, p_a0, wi, FF, 768, mask_s, activate)

    def emit_out(c, acc):
        y = (x2[:, cols(c, 384)] + acc).astype(bf16)
        for g in range(4):
            out[g // 2, g % 2, :, cols(c, 384)] = y[g * GR : g * GR + NP]

    forward(6, p_g, wo, D, 384, mask_s, emit_out)
    us[7] = us[8]
    adapter_grads(6, p_g, p_a1)

    if gathers:
        net.finish()
        for cp in norms:
            cp.wait_send()

    def emit_tmp(c, acc):
        tmp[:, cols(c, 384)] = acc

    backward(5, p_d, wi, D, 384, mask_s, emit_tmp)
    adapter_grads(5, p_a0, p_d)
    loads_back = [pltpu.make_async_copy(spill.at[i], b, psem.at[i]) for i, b in enumerate((buf_g, buf_d))]
    for cp in loads_back:
        cp.start()

    def step_two(rows):
        dx = a1[rows, :].astype(f32) + norm_back_rows(x2[rows, :], gain(2), tmp[rows, :])
        x2[rows, :] = dx
        a0[rows, :] = dx.astype(bf16)

    chunks(64, step_two)

    backward(4, p_a0, wp.at[2], D, 384, mask_s, lambda c, acc: p_a1.put(acc.astype(bf16), off=c))
    adapter_grads(4, p_o2, p_a0)
    spatial_loop(lambda rows, n, off, bias: attend_pair_back(p_qkv2, rows, n, off, bias, p_a1))
    backward(3, p_qkv2, wq.at[1], D, 384, mask_s, emit_tmp)

    def step_one(rows):
        dx = x2[rows, :] + norm_back_rows(x1[rows, :], gain(1), tmp[rows, :])
        x2[rows, :] = dx
        a0[rows, :] = dx.astype(bf16)

    chunks(64, step_one)
    arrive = exchange(2, p_a0, to_message, rcv_a)
    norm(1, lambda rows: x1[rows, :], lambda rows, v: p_a1.put(v, rows))
    adapter_grads(3, p_a1, p_qkv2)
    for cp in loads_back:
        cp.wait()
    arrive()

    for i in range(4):
        p_a0.put(dg(onehot(to_patches(i), R), rcv_a[...], 1, 0).astype(bf16), pl.ds(i * GR, GR))
    backward(2, p_a0, wp.at[1], D, 384, mask_t, lambda c, acc: p_a1.put(acc.astype(bf16), off=c))
    adapter_grads(2, m1, p_a0)
    backward(1, p_a1, wp.at[0], D, 384, mask_t, lambda c, acc: spare.put(acc.astype(bf16), off=c))
    adapter_grads(1, o1, p_a1)
    temporal_loop(lambda rows, n, off, bias: attend_pair_back(qkv1, rows, n, off, bias, spare))
    backward(0, qkv1, wq.at[0], D, 384, mask_t, emit_tmp)

    def step_zero(rows):
        dx = norm_back_rows(xt.get(rows).astype(f32), gain(0), tmp[rows, :])
        a0[rows, :] = dx.astype(bf16)

    chunks(64, step_zero)
    arrive = exchange(3, p_a0, from_patches, rcv_b)
    adapter_grads(0, h1, qkv1)
    arrive()
    for g in range(4):
        dxt = dg(onehot(to_frames(g), R), rcv_b[...], 1, 0)
        total = x2[pl.ds(g * GR, GR), :] + dxt
        ig[g // 2, g % 2] = total.astype(bf16)[:NP]


def layer(gathers, idx, x, g, hq, hp, hi, ho, ad, nm):
    vm = pl.BlockSpec(memory_space=pltpu.VMEM)
    hbm = pl.BlockSpec(memory_space=pl.ANY)
    dma = pltpu.SemaphoreType.DMA
    rows = lambda w, t=bf16: pltpu.VMEM((R, w), t)
    ng = len(gather_groups()) if gathers else 1
    return pl.pallas_call(
        functools.partial(layer_kernel, gathers),
        out_shape=[
            jax.ShapeDtypeStruct(x.shape, bf16),
            jax.ShapeDtypeStruct(x.shape, bf16),
            jax.ShapeDtypeStruct((32, ADW), bf16),
            jax.ShapeDtypeStruct((2, R, FF), bf16),
        ],
        in_specs=[pl.BlockSpec(memory_space=pltpu.SMEM)] + [hbm] * 8,
        out_specs=[vm] * 3 + [hbm],
        scratch_shapes=[
            pltpu.VMEM((2, D, QKV), bf16), pltpu.VMEM((3, D, D), bf16), pltpu.VMEM((D, FF), bf16), pltpu.VMEM((FF, D), bf16),
            pltpu.VMEM((32, ADW), bf16), pltpu.VMEM((16, D), f32), pltpu.VMEM((128, 128), bf16),
            pltpu.VMEM((3 * GR, D), bf16), rows(D), rows(D), pltpu.VMEM((2, R, FF), bf16), rows(D, f32), rows(D, f32), rows(D, f32),
            rows(D), rows(QKV), rows(D), rows(D), pltpu.VMEM((9, R, 32), bf16),
            dma((11,)), dma((4, 3)), dma((4, 3)), dma((2,)), dma((22 * ng,)), dma((22 * ng,)), dma((2, 7)),
        ],
        compiler_params=pltpu.CompilerParams(
            collective_id=1, has_side_effects=True, vmem_limit_bytes=64 * 2**20 - 2**17
        ),
        name="layer",
    )(idx, x, g, hq, hp, hi, ho, ad, nm)


def piece_widths(w):
    return [w] * 6 + [4 * w] + [3 * w] * 2 + [w] * 4 + [4 * w]


def pack_adapters(adapt_down, adapt_down_wide, adapt_up_qkv, adapt_up, adapt_up_wide):
    adapters = adapt_down_wide.shape[0]

    def flat(v):
        return v.reshape(adapters, RANK, -1)

    return jnp.concatenate(
        [
            flat(adapt_down.transpose(1, 3, 0, 2)),
            flat(adapt_down_wide.transpose(0, 2, 1)),
            flat(adapt_up_qkv.transpose(1, 2, 0, 3)),
            flat(adapt_up.transpose(1, 2, 0, 3)),
            flat(adapt_up_wide),
        ],
        axis=-1,
    )


def join_pieces(parts, w):
    joined, at = [], 0
    for width in piece_widths(w):
        piece = parts[:, :, at : at + width]
        joined.append(piece.transpose(1, 0, 2).reshape(parts.shape[1], -1))
        at += width
    return jnp.concatenate(joined, axis=-1)


def split_pieces(rows, w, owners):
    parts, at = [], 0
    for width in piece_widths(w):
        piece = rows[:, at : at + width * owners]
        parts.append(piece.reshape(rows.shape[0], owners, width).transpose(1, 0, 2))
        at += width * owners
    return jnp.concatenate(parts, axis=-1)


def per_device(
    inputs,
    out_grad,
    adapter_index,
    norm_gain,
    norm_bias,
    qkv_weight,
    proj_weight,
    mlp_in,
    mlp_out,
    adapt_down,
    adapt_down_wide,
    adapt_up_qkv,
    adapt_up,
    adapt_up_wide,
):
    owners = lax.axis_size("clip")
    adapters = adapt_down_wide.shape[0]
    clips = inputs.shape[0]
    w = norm_gain.shape[1]
    packed = pack_adapters(adapt_down, adapt_down_wide, adapt_up_qkv, adapt_up, adapt_up_wide)
    norms = jnp.concatenate([norm_gain, norm_bias], axis=0)
    if owners == 8:
        pieces = packed.reshape(adapters * RANK, 24, w)
        table = jnp.pad(pieces, ((0, 0), (0, 0), (0, 128 - w))).reshape(adapters * RANK, 24 * 128)
        own_norms = jnp.pad(norms, ((0, 10), (0, 128 - w)))
        output, input_grad, grads, _ = layer(
            True, adapter_index, inputs, out_grad, qkv_weight, proj_weight, mlp_in, mlp_out, table, own_norms
        )
    else:
        full_qkv = lax.all_gather(qkv_weight, "clip", axis=1, tiled=True)
        full_proj = lax.all_gather(proj_weight, "clip", axis=1, tiled=True)
        full_in = lax.all_gather(mlp_in, "clip", axis=0, tiled=True)
        full_out = lax.all_gather(mlp_out, "clip", axis=0, tiled=True)
        table = lax.all_gather(packed, "clip", axis=0)
        all_norms = lax.all_gather(norms, "clip", axis=0)
        nm = jnp.pad(all_norms.transpose(1, 0, 2).reshape(6, D).astype(f32), ((0, 10), (0, 0)))
        chosen = jnp.take(table, adapter_index, axis=1).reshape(owners, clips * RANK, 24 * w)
        ad = join_pieces(chosen, w)
        output, input_grad, grads, _ = layer(
            False, adapter_index, inputs, out_grad, full_qkv, full_proj, full_in, full_out, ad, nm
        )
    parts = split_pieces(grads, w, owners)
    parts = lax.all_to_all(parts, "clip", split_axis=0, concat_axis=0, tiled=True)
    every = lax.all_gather(adapter_index, "clip", axis=0, tiled=True)
    pick = (every[:, None] == jnp.arange(adapters, dtype=jnp.int32)[None, :]).astype(bf16)
    summed = jnp.einsum(
        "ca,crm->arm", pick, parts.reshape(owners * clips, RANK, 24 * w), preferred_element_type=f32
    )
    summed = lax.psum(summed.astype(bf16), "frame").astype(f32)
    return (output, input_grad) + unpack_grads(summed, w)


def unpack_grads(summed, w):
    adapters = summed.shape[0]
    down = summed[:, :, : 6 * w].reshape(adapters, RANK, 6, w).transpose(2, 0, 3, 1)
    down_wide = summed[:, :, 6 * w : 10 * w].transpose(0, 2, 1)
    up_qkv = summed[:, :, 10 * w : 16 * w].reshape(adapters, RANK, 2, 3 * w).transpose(2, 0, 1, 3)
    up = summed[:, :, 16 * w : 20 * w].reshape(adapters, RANK, 4, w).transpose(2, 0, 1, 3)
    return (down, down_wide, up_qkv, up, summed[:, :, 20 * w :])


def solution(mesh):
    return jax.shard_map(
        per_device,
        mesh=mesh,
        in_specs=(
            P("clip", "frame", None, None),
            P("clip", "frame", None, None),
            P("clip"),
            P(None, "clip"),
            P(None, "clip"),
            P(None, "clip", None),
            P(None, "clip", None),
            P("clip", None),
            P("clip", None),
            P(None, None, "clip", None),
            P(None, "clip", None),
            P(None, None, None, "clip"),
            P(None, None, None, "clip"),
            P(None, None, "clip"),
        ),
        out_specs=(
            P("clip", "frame", None, None),
            P("clip", "frame", None, None),
            P(None, None, "clip", None),
            P(None, "clip", None),
            P(None, None, None, "clip"),
            P(None, None, None, "clip"),
            P(None, None, "clip"),
        ),
        check_vma=False,
    )
```

```python
import functools
import jax
import jax.numpy as jnp
from jax import lax
from jax.experimental import pallas as pl
from jax.experimental.pallas import tpu as pltpu
from jax.sharding import PartitionSpec as P

EPS = 1e-06
MESH = pl.DeviceIdType.MESH
f32 = jnp.float32
bf16 = jnp.bfloat16
D, FF, QKV, RANK = 768, 3072, 2304, 16
NP, GR, R = 196, 208, 832
DOWN = (0, 768, 1536, 2304, 3072, 3840, 4608)
UP = (7680, 12288, 13056, 9984, 13824, 15360, 14592)
ADW = 18432
BIG = 1e30


def dg(a, b, ca, cb):
    return lax.dot_general(a, b, (((ca,), (cb,)), ((), ())), preferred_element_type=f32)


def iota(shape, d):
    return lax.broadcasted_iota(jnp.int32, shape, d)


def cols(off, w):
    return pl.ds(off if isinstance(off, int) else pl.multiple_of(off, 128), w)


def normal_parts(v):
    e = jnp.exp(-0.5 * v * v)
    t = 1.0 / (1.0 + 0.2316419 * jnp.abs(v))
    poly = t * (
        0.127414796
        + t * (-0.142248368 + t * (0.7107068705 + t * (-0.7265760135 + t * 0.5307027145)))
    )
    tail = poly * e
    return jnp.where(v >= 0, 1.0 - tail, tail), e


def onehot(col, width):
    return jnp.where(iota((col.shape[0], width), 1) == col, 1.0, 0.0).astype(bf16)


def message_rows():
    m = iota((GR, 1), 0)
    c = jnp.where(m >= 98, 1, 0)
    rest = m - 98 * c
    f = jnp.where(rest >= 49, 1, 0)
    return m < 196, c, f, rest - 49 * f


def to_message(owner):
    ok, c, f, q = message_rows()
    return jnp.where(ok, (2 * c + f) * GR + 49 * owner + q, -1)


def from_patches(owner):
    ok, c, f, q = message_rows()
    return jnp.where(ok, 392 * c + 8 * q + 2 * owner + f, -1)


def to_patches(chunk):
    t = iota((GR, 1), 0) + chunk * GR
    c = jnp.where(t >= 392, 1, 0)
    u = t - 392 * c
    q, fr = u >> 3, u & 7
    return jnp.where(t < 784, (fr >> 1) * GR + c * 98 + (fr & 1) * 49 + q, -1)


def to_frames(g):
    p = iota((GR, 1), 0)
    d = jnp.where(p >= 49, 1, 0) + jnp.where(p >= 98, 1, 0) + jnp.where(p >= 147, 1, 0)
    return jnp.where(p < NP, d * GR + (g // 2) * 98 + (g % 2) * 49 + p - 49 * d, -1)


def clip_mask(first):
    return (iota((R, 32), 0) >= first) == (iota((R, 32), 1) >= 16)


class Part:
    def __init__(self, ref, c0, width):
        self.ref, self.c0, self.width = ref, c0, width

    def get(self, rows=slice(None), off=0, width=None):
        return self.ref[rows, cols(self.c0 + off, self.width if width is None else width)]

    def put(self, val, rows=slice(None), off=0):
        self.ref[rows, cols(self.c0 + off, val.shape[1])] = val


def chunks(size, body):
    @pl.loop(0, R // size)
    def _(i):
        body(pl.ds(pl.multiple_of(i * size, size), size))


def tiles(total, tile, body, between):
    if total == tile:
        body(0)
    elif between is None:

        @pl.loop(0, total // tile)
        def _(i):
            body(i * tile)

    else:
        for c in range(0, total, tile):
            between(c)
            body(c)


def norm_rows(v):
    mean = jnp.mean(v, axis=-1, keepdims=True)
    cen = v - mean
    rstd = lax.rsqrt(jnp.mean(cen * cen, axis=-1, keepdims=True) + EPS)
    return cen * rstd, rstd


def norm_back_rows(v, gain, dh):
    hat, rstd = norm_rows(v)
    g = dh * gain
    m1 = jnp.mean(g, axis=-1, keepdims=True)
    m2 = jnp.mean(g * hat, axis=-1, keepdims=True)
    return rstd * (g - m1 - hat * m2)


def split_heads(v):
    first = iota(v.shape, 1) < 64
    zero = jnp.zeros(v.shape, bf16)
    return jnp.concatenate([jnp.where(first, v, zero), jnp.where(first, zero, v)], axis=0)


def join_heads(v):
    n = v.shape[0] // 2
    return jnp.where(iota((n, 128), 1) < 64, v[:n], v[n:])


def attend(qkv, rows, n, bias, out, pairs):
    q = [split_heads(qkv.get(rows, o, 128) * bf16(0.125)) for o in pairs]
    s = [dg(a, qkv.get(rows, D + o, 128), 1, 1) + bias for a, o in zip(q, pairs)]
    p = [jnp.exp(a - jnp.max(a, axis=1, keepdims=True)).astype(bf16) for a in s]
    ones = jnp.ones((n, 128), bf16)
    for a, o in zip(p, pairs):
        r = dg(a, jnp.concatenate([qkv.get(rows, 2 * D + o, 128), ones], axis=1), 1, 0)
        out.put(join_heads(r[:, :128] / r[:, 128:]).astype(bf16), rows, o)


def attend_back(qkv, rows, n, bias, dout, pairs, sums_by_product):
    q = [split_heads(qkv.get(rows, o, 128) * bf16(0.125)) for o in pairs]
    k = [qkv.get(rows, D + o, 128) for o in pairs]
    g = [split_heads(dout.get(rows, o, 128)) for o in pairs]
    s = [dg(a, b, 1, 1) + bias for a, b in zip(q, k)]
    dp = [dg(a, qkv.get(rows, 2 * D + o, 128), 1, 1) for a, o in zip(g, pairs)]
    p = [jnp.exp(a - jnp.max(a, axis=1, keepdims=True)) for a in s]
    if sums_by_product:
        ones = jnp.ones((n, n), bf16)
        p = [a * (1.0 / dg(a.astype(bf16), ones, 1, 0)) for a in p]
    else:
        p = [a * (1.0 / jnp.sum(a, axis=1, keepdims=True)) for a in p]
    ds = [(a * (b - jnp.sum(a * b, axis=1, keepdims=True))).astype(bf16) for a, b in zip(p, dp)]
    for i, o in enumerate(pairs):
        qkv.put((join_heads(dg(ds[i], k[i], 1, 0)) * 0.125).astype(bf16), rows, o)
        qkv.put(dg(ds[i], q[i], 0, 0).astype(bf16), rows, D + o)
        qkv.put(dg(p[i].astype(bf16), g[i], 0, 0).astype(bf16), rows, 2 * D + o)


def spatial_loop(count, body):
    bias = jnp.where(iota((1, GR), 1) < NP, 0.0, -BIG)
    steps = 6 // count

    @pl.loop(0, 4 * steps)
    def _(i):
        pairs = [((i % steps) * count + k) * 128 for k in range(count)]
        body(pl.ds(pl.multiple_of((i // steps) * GR, 16), GR), GR, bias, pairs)


def temporal_loop(body):
    pairs = range(0, D, 128)

    def bias(n):
        return jnp.where(((iota((2 * n, n), 0) & (n - 1)) >> 3) == (iota((2 * n, n), 1) >> 3), 0.0, -BIG)

    @pl.loop(0, 6)
    def _(i):
        body(pl.ds(pl.multiple_of(i * 128, 128), 128), 128, bias(128), pairs)

    body(pl.ds(768, 64), 64, bias(64), pairs)


class Many:
    def __init__(self, cps):
        self.cps = cps
        for cp in cps:
            cp.start()

    def wait_recv(self):
        for cp in self.cps:
            cp.wait_recv()

    def wait_send(self):
        for cp in self.cps:
            cp.wait_send()


def gather_groups():
    out = [(f"q0{c}", "q", 0, 0, 96, 16, c, D) for c in range(0, QKV, D)]
    out += [("p0", "p", 0, 0, 96, 16, 0, D), ("p1", "p", 1, 0, 96, 16, 0, D)]
    out += [(f"q1{c}", "q", 1, 0, 96, 16, c, D) for c in range(0, QKV, D)]
    out += [("p2", "p", 2, 0, 96, 16, 0, D)]
    out += [("o", "o", None, r, 96, 16, 0, D) for r in range(0, 384, 96)]
    out += [(f"i{c}", "i", None, 0, 96, 16, c, D) for c in range(0, FF, D)]
    return out


class Gather:
    def __init__(self, srcs, dsts, sems, local, ahead=3, lag=1):
        self.groups = gather_groups()
        self.srcs, self.dsts, self.sems = srcs, dsts, sems
        self.ahead, self.lag = ahead, lag
        clip, frame = lax.axis_index("clip"), lax.axis_index("frame")
        self.z, self.y, self.x, self.c = clip // 2, clip % 2, frame // 2, frame % 2
        z, y, x, c = self.z, self.y, self.x, self.c
        self.zpeers = [self.dev(lax.rem(z + k, 4), y, x, c) for k in (1, 2, 3)]
        self.ypeer, self.xpeer, self.cpeer = self.dev(z, 1 - y, x, c), self.dev(z, y, 1 - x, c), self.dev(z, y, x, 1 - c)
        self.moved = {k: {} for k in ("z", "y0", "y", "x1", "x2", "c1", "c2")}
        self.step = 0
        self.local = local

    @staticmethod
    def dev(z, y, x, c):
        return {"clip": z * 2 + y, "frame": x * 2 + c}

    def peers(self):
        return self.zpeers + [self.ypeer, self.xpeer, self.cpeer]

    def span(self, g, first, count):
        _, _, _, r0, rows, unit, c0, width = self.groups[g]
        return pl.multiple_of(r0 + unit * first, 16), unit * count, c0, width

    def src(self, g, span):
        key, name, lead = self.groups[g][:3]
        r = self.srcs[name] if lead is None else self.srcs[name].at[lead]
        return r.at[pl.ds(span[0], span[1]), pl.ds(span[2], span[3])]

    def dst(self, g, z, y, span):
        key, name, lead = self.groups[g][:3]
        cs = pl.ds(span[2], span[3])
        r = self.dsts[name] if lead is None else self.dsts[name].at[lead]
        per = 384 if name == "o" else 96
        return r.at[pl.ds(pl.multiple_of((z * 2 + y) * per + span[0], 16), span[1]), cs]

    def remote(self, kind, i, s, d, peer):
        return pltpu.make_async_remote_copy(
            src_ref=s,
            dst_ref=d,
            send_sem=self.sems[0].at[kind + i],
            recv_sem=self.sems[1].at[kind + i],
            device_id=peer,
            device_id_type=MESH,
        )

    def relay(self, g, kind, items, span, peer):
        return Many(
            [self.remote(22 * g + kind, i, self.dst(g, zz, yy, span), self.dst(g, zz, yy, span), peer) for i, (zz, yy) in items]
        )

    def start_z(self, g):
        two = self.span(g, 3 * self.c + self.x, 2)
        self.moved["z"][g] = Many(
            [self.remote(22 * g, k, self.src(g, two), self.dst(g, self.z, self.y, two), p) for k, p in enumerate(self.zpeers)]
        )
        self.moved["y0"][g] = Many([self.remote(22 * g, 3, self.src(g, two), self.dst(g, self.z, self.y, two), self.ypeer)])

    def begin(self):
        for g in range(self.ahead):
            self.start_z(g)

    def others(self, first):
        return [(q, lax.rem(self.z + q, 4)) for q in range(first, 4)]

    def tick(self):
        s, lag, ng, m, y = self.step, self.lag, len(self.groups), self.moved, self.y
        if s >= ng + 3 * lag:
            return False
        self.step += 1
        if s == 0:
            for cp in self.local:
                cp.wait()
        two, one, half = (3 * self.c + self.x, 2), (3 * self.c + 2 * self.x, 1), (3 * self.c, 3)
        if s < ng:
            m["z"][s].wait_recv()
            if s + self.ahead < ng:
                self.start_z(s + self.ahead)
            m["y"][s] = self.relay(s, 4, [(q - 1, (zz, y)) for q, zz in self.others(1)], self.span(s, *two), self.ypeer)
            m["x1"][s] = self.relay(s, 7, [(q - 1, (zz, y)) for q, zz in self.others(1)], self.span(s, *one), self.xpeer)
        g = s - lag
        if 0 <= g < ng:
            m["y0"][g].wait_recv()
            m["y"][g].wait_recv()
            m["x2"][g] = self.relay(g, 10, [(q, (zz, 1 - y)) for q, zz in self.others(0)], self.span(g, *one), self.xpeer)
            m["x1"][g].wait_recv()
            m["c1"][g] = self.relay(g, 14, [(q - 1, (zz, y)) for q, zz in self.others(1)], self.span(g, *half), self.cpeer)
        g = s - 2 * lag
        if 0 <= g < ng:
            m["x2"][g].wait_recv()
            m["c2"][g] = self.relay(g, 17, [(q, (zz, 1 - y)) for q, zz in self.others(0)], self.span(g, *half), self.cpeer)
        g = s - 3 * lag
        if 0 <= g < ng:
            m["c1"][g].wait_recv()
            m["c2"][g].wait_recv()
        return True

    def need(self, key):
        last = max(i for i, g in enumerate(self.groups) if g[0] == key)
        while self.step <= last + 3 * self.lag:
            self.tick()

    def finish(self):
        while self.tick():
            pass
        for kind in self.moved.values():
            for cps in kind.values():
                cps.wait_send()


PIECES = [(i, 1) for i in range(6)] + [(6, 4), (10, 3), (13, 3)] + [(16 + i, 1) for i in range(4)] + [(20, 4)]


def piece_slots():
    for first, count in PIECES:
        for i in range(8 * count):
            yield first + i // 8, i % 8, i // count, first + i % count


def placement(part):
    row = iota((256, 1), 0)
    lane = row & 127
    return onehot(jnp.where(lane < 96, (2 * part + (row >> 7)) * 96 + lane, -1), D)


def place(rows):
    total = dg(rows(0), placement(0), 1, 0)
    for part in range(1, 4):
        total = total + dg(rows(part), placement(part), 1, 0)
    return total


def pick_rows(index):
    return jnp.where(iota((256, 128), 1) == index[...], 1.0, 0.0).astype(bf16)


BATCHES = ([3, 4, 5, 6, 7, 8, 9, 13, 14, 15, 18, 19, 20, 21, 22, 23], [0, 1, 2, 10, 11, 12, 16, 17])
PLACES = {p: i for i, p in enumerate(BATCHES[0] + BATCHES[1])}


class Reduce:
    def __init__(self, batch, gd, work, stage_rows, received, result, nidx, sems):
        self.batch, self.gd, self.work, self.stage_rows = batch, gd, work, stage_rows
        self.received, self.result, self.nidx, self.sems = received, result, nidx, sems
        clip, frame = lax.axis_index("clip"), lax.axis_index("frame")
        self.clip, self.frame, self.x, self.c = clip, frame, frame // 2, frame % 2
        self.xpeer = {"clip": clip, "frame": (1 - self.x) * 2 + self.c}
        self.cpeer = {"clip": clip, "frame": self.x * 2 + 1 - self.c}
        self.width = len(BATCHES[batch]) * 32
        self.count = 0
        self.sent = []

    def lanes(self, quarter):
        return pl.ds(pl.multiple_of(2048 * self.batch + self.width * quarter, 128), self.width)

    def send(self, src, dst, peer):
        i = 16 * self.batch + self.count
        self.count += 1
        cp = pltpu.make_async_remote_copy(
            src_ref=src, dst_ref=dst, send_sem=self.sems.at[0, i], recv_sem=self.sems.at[1, i], device_id=peer, device_id_type=MESH
        )
        cp.start()
        self.sent.append(cp)
        return cp

    def add(self, first_row, quarter):
        ls = self.lanes(quarter)
        total = self.work[pl.ds(0, 256), ls].astype(f32) + self.work[pl.ds(first_row, 256), ls].astype(f32)
        self.work[pl.ds(0, 256), ls] = total.astype(bf16)

    def split(self):
        pieces = BATCHES[self.batch]
        for i, block in enumerate(pieces):
            self.stage_rows[pl.ds(32 * i, 32), :] = self.gd[:, pl.ds(block * D, D)]
        for part in range(4):
            rows = self.stage_rows[pl.ds(0, 32 * len(pieces)), :]
            parts = dg(rows, placement(part), 1, 1).astype(bf16)
            for block, slot, owner, piece in piece_slots():
                if block in pieces and slot // 2 == part:
                    i = pieces.index(block)
                    tile = parts[32 * i : 32 * i + 32, 128 * (slot % 2) : 128 * (slot % 2) + 128]
                    self.work[pl.ds(32 * owner, 32), pl.ds(128 * PLACES[piece], 128)] = tile
        self.core = []
        for xx in range(2):
            ls = self.lanes(2 * xx + 1 - self.c)
            self.core.append(self.send(self.work.at[pl.ds(0, 256), ls], self.work.at[pl.ds(256, 256), ls], self.cpeer))

    def over_x(self):
        for xx in range(2):
            self.core[xx].wait_recv()
        for xx in range(2):
            self.add(256, 2 * xx + self.c)
        ls = self.lanes(2 * (1 - self.x) + self.c)
        self.across = self.send(self.work.at[pl.ds(0, 256), ls], self.work.at[pl.ds(512, 256), ls], self.xpeer)

    def to_owners(self):
        self.across.wait_recv()
        self.add(512, self.frame)
        ls = self.lanes(self.frame)
        self.here = pl.ds(512 * self.batch, self.width)
        mine = pl.ds(pl.multiple_of(32 * self.clip, 32), 32)
        self.received[mine, self.here] = self.work[mine, ls]
        self.owned = []
        for k in range(1, 8):
            j = lax.rem(self.clip + k, 8)
            rows = pl.ds(pl.multiple_of(32 * j, 32), 32)
            self.owned.append(
                self.send(self.work.at[rows, ls], self.received.at[mine, self.here], {"clip": j, "frame": self.frame})
            )

    def by_adapter(self):
        for cp in self.owned:
            cp.wait_recv()
        ls = self.lanes(self.frame)
        self.result[:, ls] = dg(pick_rows(self.nidx), self.received[:, self.here], 0, 0).astype(bf16)
        same = self.result.at[:, ls]
        self.back = [self.send(same, same, p) for p in (self.xpeer, self.cpeer)]

    def spread(self):
        self.back[0].wait_recv()
        same = self.result.at[:, self.lanes(2 * (1 - self.x) + self.c)]
        self.last = self.send(same, same, self.cpeer)

    def finish(self):
        self.back[1].wait_recv()
        self.last.wait_recv()
        for cp in self.sent:
            cp.wait_send()


def layer_kernel(
    gathers, hidx, x_ref, g_ref, hq, hp, hi, ho, had, hnm,
    out, ig, grads, spill,
    wq, wp, wi, wo, ad, nm, nbuf, nidx, gd, received, rcv_a, rcv_b, big, x1, x2, tmp, o2, qkv2, a0, a1, us,
    wsem, ssem, rsem, psem, gssem, grsem, nsem, asem, bsem,
):
    buf_g, buf_d = big.at[0], big.at[1]

    clip = lax.axis_index("clip")
    me = lax.axis_index("frame")
    nf = 4
    peers = [lax.rem(me + k, nf) for k in range(1, nf)]

    fetch = [pltpu.make_async_copy(s, d, wsem.at[10 + i]) for i, (s, d) in enumerate(((x_ref, ig), (g_ref, out)))]
    for cp in fetch:
        cp.start()
    barrier = pltpu.get_barrier_semaphore()
    groups_of = [{"clip": clip, "frame": d} for d in peers]
    loads = {}
    if gathers:
        own = pl.ds(pl.multiple_of(clip * 96, 16), 96)
        local = [
            (hq.at[0], wq.at[0, own]), (hq.at[1], wq.at[1, own]), (hp.at[0], wp.at[0, own]), (hp.at[1], wp.at[1, own]),
            (hp.at[2], wp.at[2, own]), (hi, wi.at[own]), (ho, wo.at[pl.ds(pl.multiple_of(clip * 384, 16), 384)]),
            (had, big.at[1, pl.ds(0, 128)]), (hnm, nbuf.at[pl.ds(pl.multiple_of(clip * 16, 16), 16)]),
            (hidx, nidx.at[pl.ds(pl.multiple_of(clip * 32, 32), 32)]),
        ]
        local = [pltpu.make_async_copy(s, d, wsem.at[i]) for i, (s, d) in enumerate(local)]
        for cp in local:
            cp.start()
        net = Gather(
            {"q": hq, "p": hp, "i": hi, "o": ho},
            {"q": wq, "p": wp, "i": wi, "o": wo},
            (gssem, grsem),
            local[:7],
        )
        owners = [{"clip": lax.rem(clip + k, 8), "frame": me} for k in range(1, 8)]
        greet = groups_of + owners
    else:
        net = None
        for key, src, dst in (
            ("q0", hq.at[0], wq.at[0]), ("p0", hp.at[0], wp.at[0]), ("p1", hp.at[1], wp.at[1]), ("q1", hq.at[1], wq.at[1]),
            ("p2", hp.at[2], wp.at[2]), ("o", ho, wo), ("i", hi, wi), ("ad", had, ad), ("nm", hnm, nm),
        ):
            loads[key] = pltpu.make_async_copy(src, dst, wsem.at[len(loads)])
            loads[key].start()
        greet = groups_of
    for p in greet:
        pl.semaphore_signal(barrier, inc=1, device_id=p, device_id_type=MESH)
    pl.semaphore_wait(barrier, len(greet))

    def need(key, c=""):
        if net is not None:
            net.need(f"{key}{c}")
        elif not c:
            loads[key].wait()

    def need_tiles(key):
        def between(c):
            if c:
                tick()
            need(key, c)

        return between

    def tick():
        if net is not None:
            net.tick()

    if gathers:

        def to(peer, src, dst, sems, i):
            cp = pltpu.make_async_remote_copy(
                src_ref=src, dst_ref=dst, send_sem=sems.at[0, i], recv_sem=sems.at[1, i], device_id=peer, device_id_type=MESH
            )
            cp.start()
            return cp

        rows16 = pl.ds(pl.multiple_of(clip * 16, 16), 16)
        rows32 = pl.ds(pl.multiple_of(clip * 32, 32), 32)
        small = [to(p, hidx, nidx.at[rows32], nsem, k) for k, p in enumerate(owners)]
        small += [to(p, hnm, nbuf.at[rows16], nsem, 7 + k) for k, p in enumerate(owners)]
        net.begin()

    def exchange(step, src, index, rcv):
        sent = []
        for k, d in enumerate(peers):
            slot = pl.ds(k * GR, GR)
            o2[slot, :] = dg(onehot(index(d), R), src.get(), 1, 0).astype(bf16)
            cp = pltpu.make_async_remote_copy(
                src_ref=o2.at[slot],
                dst_ref=rcv.at[pl.ds(pl.multiple_of(me * GR, 16), GR)],
                send_sem=ssem.at[step, k],
                recv_sem=rsem.at[step, k],
                device_id={"clip": clip, "frame": d},
                device_id_type=MESH,
            )
            cp.start()
            sent.append(cp)
        rcv[pl.ds(pl.multiple_of(me * GR, 16), GR), :] = dg(onehot(index(me), R), src.get(), 1, 0).astype(bf16)

        def finish():
            for cp in sent:
                cp.wait_recv()
            for cp in sent:
                cp.wait_send()

        return finish

    def gain(k):
        return nm[k : k + 1, :]

    def norm(k, read, put):
        def body(rows):
            hat, _ = norm_rows(read(rows))
            put(rows, (hat * gain(k) + gain(3 + k)).astype(bf16))

        chunks(64, body)

    def rank(h, at, mask, m):
        us[:, pl.ds(32 * m, 32)] = jnp.where(mask, dg(h.get(), ad[:, pl.ds(at, h.width)], 1, 1), 0.0).astype(bf16)

    def forward(m, h, w, width, tile, mask, emit, between=None):
        rank(h, DOWN[m], mask, m)

        def body(c):
            acc = dg(h.get(), w[:, cols(c, tile)], 1, 0)
            acc = acc + dg(us[:, pl.ds(32 * m, 32)], ad[:, cols(UP[m] + c, tile)], 1, 0)
            emit(c, acc)

        tiles(width, tile, body, between)

    def rank_back(m, dz, mask):
        du = jnp.where(mask, dg(dz.get(), ad[:, pl.ds(UP[m], dz.width)], 1, 1), 0.0).astype(bf16)
        us[:, pl.ds(224, 32)] = du

    def backward(m, dz, w, width, tile, mask, emit, between=None):
        rank_back(m, dz, mask)
        backward_rows(m, dz, w, width, tile, emit, between)

    def backward_rows(m, dz, w, width, tile, emit, between=None):

        def body(c):
            acc = dg(dz.get(), w[cols(c, tile), :], 1, 1)
            acc = acc + dg(us[:, pl.ds(224, 32)], ad[:, cols(DOWN[m] + c, tile)], 1, 0)
            emit(c, acc)

        tiles(width, tile, body, between)

    def adapter_grads(m, h, dz):
        gd[:, pl.ds(DOWN[m], h.width)] = dg(us[:, pl.ds(224, 32)], h.get(), 0, 0).astype(gd.dtype)
        gd[:, pl.ds(UP[m], dz.width)] = dg(us[:, pl.ds(32 * m, 32)], dz.get(), 0, 0).astype(gd.dtype)

    p_a0, p_a1 = Part(a0, 0, D), Part(a1, 0, D)
    qkv1, h1 = Part(buf_g, 0, QKV), Part(buf_g, QKV, D)
    xt, o1, m1, spare = (Part(buf_d, D * i, D) for i in range(4))
    p_o2, p_qkv2, p_g, p_d = Part(o2, 0, D), Part(qkv2, 0, QKV), Part(buf_g, 0, FF), Part(buf_d, 0, FF)

    for i, (src, dst) in enumerate(((ig, a0), (out, a1))):
        fetch[i].wait()
        for g in range(4):
            dst[pl.ds(GR * g + 192, 16), :] = jnp.zeros((16, D), bf16)
            dst[pl.ds(GR * g, NP), :] = src[g // 2, g % 2]
        if dst is a0:
            arrive = exchange(0, p_a0, to_message, rcv_a)

    mask_t = clip_mask(392)
    mask_s = clip_mask(416)
    if gathers:
        for cp in local[7:]:
            cp.wait()
        for cp in small[:7]:
            cp.wait_recv()
        pick = pick_rows(nidx)
        quarter = cols(me * D, D)
        chosen = big.at[1, pl.ds(128, 256), pl.ds(0, D)]
        big[1, pl.ds(128, 256), pl.ds(0, D)] = dg(pick, big[1, pl.ds(0, 128), quarter], 1, 0).astype(bf16)
        picked = []
        for k, p in enumerate(owners):
            rows = pl.ds(pl.multiple_of(128 + 32 * p["clip"], 32), 32)
            picked.append(to(p, big.at[1, rows, pl.ds(0, D)], big.at[0, rows32, quarter], asem, k))
        big[0, rows32, quarter] = big[1, pl.ds(pl.multiple_of(128 + 32 * clip, 32), 32), pl.ds(0, D)]
        tick()
        for cp in picked:
            cp.wait_recv()

        def block_of(frame):
            return big.at[0, pl.ds(0, 256), cols(frame * D, D)]

        x, c = me // 2, me % 2
        xpeer, cpeer = {"clip": clip, "frame": (1 - x) * 2 + c}, {"clip": clip, "frame": x * 2 + 1 - c}
        picked.append(to(xpeer, block_of(me), block_of(me), asem, 7))
        picked.append(to(cpeer, block_of(me), block_of(me), asem, 8))
        tick()
        picked[7].wait_recv()
        far = (1 - x) * 2 + c
        picked.append(to(cpeer, block_of(far), block_of(far), asem, 9))
        picked[8].wait_recv()
        picked[9].wait_recv()
        for cp in picked:
            cp.wait_send()
        for owner in range(8):
            part = big[0, pl.ds(32 * owner, 32), :]
            for block, slot, of, piece in piece_slots():
                if of == owner:
                    qkv2[pl.ds(block * 32, 32), pl.ds(slot * 128, 128)] = part[:, piece * 128 : piece * 128 + 128]
        joined = place(lambda part: qkv2[pl.ds(0, 768), pl.ds(256 * part, 256)]).astype(bf16)
        for block in range(24):
            ad[:, pl.ds(block * D, D)] = joined[block * 32 : block * 32 + 32]
        for cp in small[7:]:
            cp.wait_recv()
        for j in range(8):
            qkv2[pl.ds(0, 16), pl.ds(j * 128, 128)] = nbuf[pl.ds(16 * j, 16), :]
        nm[...] = place(lambda part: qkv2[pl.ds(0, 16), pl.ds(256 * part, 256)])
    else:
        need("ad")
        need("nm")
    arrive()
    for i in range(4):
        xt.put(dg(onehot(to_patches(i), R), rcv_a[...], 1, 0).astype(bf16), pl.ds(i * GR, GR))
    tick()
    norm(0, lambda rows: xt.get(rows).astype(f32), lambda rows, v: h1.put(v, rows))
    tick()
    forward(0, h1, wq.at[0], QKV, 768, mask_t, lambda c, acc: qkv1.put(acc.astype(bf16), off=c), need_tiles("q0"))
    tick()
    temporal_loop(lambda rows, n, bias, pairs: attend(qkv1, rows, n, bias, o1, pairs))
    tick()
    need("p0")
    forward(1, o1, wp.at[0], D, 384, mask_t, lambda c, acc: m1.put(acc.astype(bf16), off=c))
    tick()
    need("p1")
    forward(2, m1, wp.at[1], D, 384, mask_t, lambda c, acc: spare.put(acc.astype(bf16), off=c))
    tick()
    arrive = exchange(1, spare, from_patches, rcv_b)
    tick()
    saves = [pltpu.make_async_copy(b, spill.at[i], psem.at[i]) for i, b in enumerate((buf_g, buf_d))]
    for cp in saves:
        cp.start()
    for cp in saves:
        cp.wait()
    tick()

    need("o")
    backward(6, p_a1, wo, FF, 768, mask_s, lambda c, acc: p_d.put(acc.astype(bf16), off=c), lambda c: tick())
    us[:, pl.ds(256, 32)] = us[:, pl.ds(224, 32)]
    tick()
    arrive()
    tick()

    for g in range(4):
        rows = pl.ds(g * GR, GR)
        tb = dg(onehot(to_frames(g), R), rcv_b[...], 1, 0)
        x1[rows, :] = a0[rows, :].astype(f32) + tb
    tick()
    norm(1, lambda rows: x1[rows, :], lambda rows, v: p_o2.put(v, rows))
    tick()
    forward(3, p_o2, wq.at[1], QKV, 768, mask_s, lambda c, acc: p_qkv2.put(acc.astype(bf16), off=c), need_tiles("q1"))
    tick()
    spatial_loop(3, lambda rows, n, bias, pairs: attend(p_qkv2, rows, n, bias, p_o2, pairs))
    tick()
    need("p2")

    def add_spatial(c, acc):
        x2[:, cols(c, 384)] = x1[:, cols(c, 384)] + acc

    forward(4, p_o2, wp.at[2], D, 384, mask_s, add_spatial)
    tick()

    norm(2, lambda rows: x2[rows, :], lambda rows, v: p_a0.put(v, rows))

    def activate(c, acc):
        tmp_w = acc.shape[1]
        tmp[:, pl.ds(0, tmp_w)] = acc
        @pl.loop(0, R // 32)
        def _(i):
            rows = pl.ds(pl.multiple_of(i * 32, 32), 32)
            v = tmp[rows, pl.ds(0, tmp_w)]
            phi, e = normal_parts(v)
            slope = phi + v * e * 0.3989422804014327
            p_g.put((v * phi).astype(bf16), rows, c)
            p_d.put((p_d.get(rows, c, tmp_w).astype(f32) * slope).astype(bf16), rows, c)

    forward(5, p_a0, wi, FF, 768, mask_s, activate, need_tiles("i"))

    def emit_out(c, acc):
        y = (x2[:, cols(c, 384)] + acc).astype(bf16)
        for g in range(4):
            out[g // 2, g % 2, :, cols(c, 384)] = y[g * GR : g * GR + NP]

    forward(6, p_g, wo, D, 384, mask_s, emit_out)
    us[:, pl.ds(224, 32)] = us[:, pl.ds(256, 32)]
    adapter_grads(6, p_g, p_a1)

    if gathers:
        net.finish()
        for cp in small:
            cp.wait_send()

    def emit_tmp(c, acc):
        tmp[:, cols(c, 384)] = acc

    backward(5, p_d, wi, D, 384, mask_s, emit_tmp)
    adapter_grads(5, p_a0, p_d)
    loads_back = [pltpu.make_async_copy(spill.at[i], b, psem.at[i]) for i, b in enumerate((buf_g, buf_d))]
    for cp in loads_back:
        cp.start()

    def step_two(rows):
        dx = a1[rows, :].astype(f32) + norm_back_rows(x2[rows, :], gain(2), tmp[rows, :])
        x2[rows, :] = dx
        a0[rows, :] = dx.astype(bf16)

    chunks(64, step_two)

    backward(4, p_a0, wp.at[2], D, 384, mask_s, lambda c, acc: p_a1.put(acc.astype(bf16), off=c))
    adapter_grads(4, p_o2, p_a0)
    spatial_loop(2, lambda rows, n, bias, pairs: attend_back(p_qkv2, rows, n, bias, p_a1, pairs, False))
    backward(3, p_qkv2, wq.at[1], D, 384, mask_s, emit_tmp)

    def step_one(rows):
        dx = x2[rows, :] + norm_back_rows(x1[rows, :], gain(1), tmp[rows, :])
        x2[rows, :] = dx
        a0[rows, :] = dx.astype(bf16)

    chunks(64, step_one)
    arrive = exchange(2, p_a0, to_message, rcv_a)
    norm(1, lambda rows: x1[rows, :], lambda rows, v: p_a1.put(v, rows))
    adapter_grads(3, p_a1, p_qkv2)
    for cp in loads_back:
        cp.wait()
    arrive()

    if gathers:
        first, second = (Reduce(i, gd, wi, wo, received, grads, nidx, bsem) for i in range(2))
        first.split()
    for i in range(4):
        p_a0.put(dg(onehot(to_patches(i), R), rcv_a[...], 1, 0).astype(bf16), pl.ds(i * GR, GR))
    backward(2, p_a0, wp.at[1], D, 384, mask_t, lambda c, acc: p_a1.put(acc.astype(bf16), off=c))
    adapter_grads(2, m1, p_a0)
    if gathers:
        first.over_x()
    backward(1, p_a1, wp.at[0], D, 384, mask_t, lambda c, acc: spare.put(acc.astype(bf16), off=c))
    adapter_grads(1, o1, p_a1)
    temporal_loop(lambda rows, n, bias, pairs: (attend_back(qkv1, rows, n, bias, spare, pairs[:3], True), attend_back(qkv1, rows, n, bias, spare, pairs[3:], True)))
    if gathers:
        first.to_owners()
    rank_back(0, qkv1, mask_t)
    adapter_grads(0, h1, qkv1)
    if gathers:
        second.split()
        first.by_adapter()
    backward_rows(0, qkv1, wq.at[0], D, 384, emit_tmp)
    if gathers:
        second.over_x()
        first.spread()

    def step_zero(rows):
        dx = norm_back_rows(xt.get(rows).astype(f32), gain(0), tmp[rows, :])
        a0[rows, :] = dx.astype(bf16)

    chunks(64, step_zero)
    if gathers:
        second.to_owners()
    arrive = exchange(3, p_a0, from_patches, rcv_b)
    if gathers:
        second.by_adapter()
        first.finish()
        second.spread()
    arrive()
    for g in range(4):
        dxt = dg(onehot(to_frames(g), R), rcv_b[...], 1, 0)
        total = x2[pl.ds(g * GR, GR), :] + dxt
        ig[g // 2, g % 2] = total.astype(bf16)[:NP]
    if gathers:
        second.finish()
    else:
        grads[...] = gd[...]


def layer(gathers, index_rows, x, g, hq, hp, hi, ho, ad, nm):
    vm = pl.BlockSpec(memory_space=pltpu.VMEM)
    hbm = pl.BlockSpec(memory_space=pl.ANY)
    dma = pltpu.SemaphoreType.DMA
    rows = lambda w, t=bf16: pltpu.VMEM((R, w), t)
    ng = len(gather_groups()) if gathers else 1
    return pl.pallas_call(
        functools.partial(layer_kernel, gathers),
        out_shape=[
            jax.ShapeDtypeStruct(x.shape, bf16),
            jax.ShapeDtypeStruct(x.shape, bf16),
            jax.ShapeDtypeStruct((128, 24 * 128) if gathers else (32, ADW), bf16),
            jax.ShapeDtypeStruct((2, R, FF), bf16),
        ],
        in_specs=[hbm] * 9,
        out_specs=[vm] * 3 + [hbm],
        scratch_shapes=[
            pltpu.VMEM((2, D, QKV), bf16), pltpu.VMEM((3, D, D), bf16), pltpu.VMEM((D, FF), bf16), pltpu.VMEM((FF, D), bf16),
            pltpu.VMEM((32, ADW), bf16), pltpu.VMEM((16, D), f32), pltpu.VMEM((128, 128), bf16),
            pltpu.VMEM((256, 128), jnp.int32), pltpu.VMEM((32, ADW), bf16), pltpu.VMEM((256, D), bf16),
            rows(D), rows(D), pltpu.VMEM((2, R, FF), bf16), rows(D, f32), rows(D, f32), rows(D, f32),
            rows(D), rows(QKV), rows(D), rows(D), rows(384),
            dma((12,)), dma((4, 3)), dma((4, 3)), dma((2,)), dma((22 * ng,)), dma((22 * ng,)), dma((2, 14)), dma((2, 10)), dma((2, 32)),
        ],
        compiler_params=pltpu.CompilerParams(
            collective_id=1, has_side_effects=True, vmem_limit_bytes=64 * 2**20 - 2**17
        ),
        name="layer",
    )(index_rows, x, g, hq, hp, hi, ho, ad, nm)


def piece_widths(w):
    return [w] * 6 + [4 * w] + [3 * w] * 2 + [w] * 4 + [4 * w]


def pack_adapters(adapt_down, adapt_down_wide, adapt_up_qkv, adapt_up, adapt_up_wide):
    adapters = adapt_down_wide.shape[0]

    def flat(v):
        return v.reshape(adapters, RANK, -1)

    return jnp.concatenate(
        [
            flat(adapt_down.transpose(1, 3, 0, 2)),
            flat(adapt_down_wide.transpose(0, 2, 1)),
            flat(adapt_up_qkv.transpose(1, 2, 0, 3)),
            flat(adapt_up.transpose(1, 2, 0, 3)),
            flat(adapt_up_wide),
        ],
        axis=-1,
    )


def join_pieces(parts, w):
    joined, at = [], 0
    for width in piece_widths(w):
        piece = parts[:, :, at : at + width]
        joined.append(piece.transpose(1, 0, 2).reshape(parts.shape[1], -1))
        at += width
    return jnp.concatenate(joined, axis=-1)


def split_pieces(rows, w, owners):
    parts, at = [], 0
    for width in piece_widths(w):
        piece = rows[:, at : at + width * owners]
        parts.append(piece.reshape(rows.shape[0], owners, width).transpose(1, 0, 2))
        at += width * owners
    return jnp.concatenate(parts, axis=-1)


def per_device(
    inputs,
    out_grad,
    adapter_index,
    norm_gain,
    norm_bias,
    qkv_weight,
    proj_weight,
    mlp_in,
    mlp_out,
    adapt_down,
    adapt_down_wide,
    adapt_up_qkv,
    adapt_up,
    adapt_up_wide,
):
    owners = lax.axis_size("clip")
    adapters = adapt_down_wide.shape[0]
    clips = inputs.shape[0]
    w = norm_gain.shape[1]
    packed = pack_adapters(adapt_down, adapt_down_wide, adapt_up_qkv, adapt_up, adapt_up_wide)
    norms = jnp.concatenate([norm_gain, norm_bias], axis=0)
    if owners == 8:
        index_rows = adapter_index[:, None] * RANK + jnp.arange(RANK, dtype=jnp.int32)[None, :]
        index_rows = jnp.broadcast_to(index_rows.reshape(clips * RANK, 1), (clips * RANK, 128))
        pieces = packed.reshape(adapters * RANK, 24, w)
        table = jnp.pad(pieces, ((0, 0), (0, 0), (0, 128 - w))).reshape(adapters * RANK, 24 * 128)
        own_norms = jnp.pad(norms, ((0, 10), (0, 128 - w)))
        output, input_grad, grads, _ = layer(
            True, index_rows, inputs, out_grad, qkv_weight, proj_weight, mlp_in, mlp_out, table, own_norms
        )
        grads = grads.reshape(adapters, RANK, 24, 128)[..., :w].astype(f32)
        summed = jnp.concatenate([grads[:, :, PLACES[p]] for p in range(24)], axis=-1)
    else:
        full_qkv = lax.all_gather(qkv_weight, "clip", axis=1, tiled=True)
        full_proj = lax.all_gather(proj_weight, "clip", axis=1, tiled=True)
        full_in = lax.all_gather(mlp_in, "clip", axis=0, tiled=True)
        full_out = lax.all_gather(mlp_out, "clip", axis=0, tiled=True)
        table = lax.all_gather(packed, "clip", axis=0)
        all_norms = lax.all_gather(norms, "clip", axis=0)
        nm = jnp.pad(all_norms.transpose(1, 0, 2).reshape(6, D).astype(f32), ((0, 10), (0, 0)))
        chosen = jnp.take(table, adapter_index, axis=1).reshape(owners, clips * RANK, 24 * w)
        ad = join_pieces(chosen, w)
        output, input_grad, grads, _ = layer(
            False, adapter_index, inputs, out_grad, full_qkv, full_proj, full_in, full_out, ad, nm
        )
        parts = split_pieces(grads, w, owners)
        parts = lax.all_to_all(parts, "clip", split_axis=0, concat_axis=0, tiled=True)
        every = lax.all_gather(adapter_index, "clip", axis=0, tiled=True)
        pick = (every[:, None] == jnp.arange(adapters, dtype=jnp.int32)[None, :]).astype(bf16)
        summed = jnp.einsum(
            "ca,crm->arm", pick, parts.reshape(owners * clips, RANK, 24 * w), preferred_element_type=f32
        )
        summed = lax.psum(summed.astype(bf16), "frame").astype(f32)
    return (output, input_grad) + unpack_grads(summed, w)


def unpack_grads(summed, w):
    adapters = summed.shape[0]
    down = summed[:, :, : 6 * w].reshape(adapters, RANK, 6, w).transpose(2, 0, 3, 1)
    down_wide = summed[:, :, 6 * w : 10 * w].transpose(0, 2, 1)
    up_qkv = summed[:, :, 10 * w : 16 * w].reshape(adapters, RANK, 2, 3 * w).transpose(2, 0, 1, 3)
    up = summed[:, :, 16 * w : 20 * w].reshape(adapters, RANK, 4, w).transpose(2, 0, 1, 3)
    return (down, down_wide, up_qkv, up, summed[:, :, 20 * w :])


def solution(mesh):
    return jax.shard_map(
        per_device,
        mesh=mesh,
        in_specs=(
            P("clip", "frame", None, None),
            P("clip", "frame", None, None),
            P("clip"),
            P(None, "clip"),
            P(None, "clip"),
            P(None, "clip", None),
            P(None, "clip", None),
            P("clip", None),
            P("clip", None),
            P(None, None, "clip", None),
            P(None, "clip", None),
            P(None, None, None, "clip"),
            P(None, None, None, "clip"),
            P(None, None, "clip"),
        ),
        out_specs=(
            P("clip", "frame", None, None),
            P("clip", "frame", None, None),
            P(None, None, "clip", None),
            P(None, "clip", None),
            P(None, None, None, "clip"),
            P(None, None, None, "clip"),
            P(None, None, "clip"),
        ),
        check_vma=False,
    )
```

```python
import functools
import jax
import jax.numpy as jnp
from jax import lax
from jax.experimental import pallas as pl
from jax.experimental.pallas import tpu as pltpu
from jax.sharding import PartitionSpec as P

EPS = 1e-06
MESH = pl.DeviceIdType.MESH
f32 = jnp.float32
bf16 = jnp.bfloat16
D, FF, QKV, RANK = 768, 3072, 2304, 16
NP, GR, R = 196, 208, 832
DOWN = (0, 768, 1536, 2304, 3072, 3840, 4608)
UP = (7680, 12288, 13056, 9984, 13824, 15360, 14592)
ADW = 18432
BIG = 1e30


def dg(a, b, ca, cb):
    return lax.dot_general(a, b, (((ca,), (cb,)), ((), ())), preferred_element_type=f32)


def iota(shape, d):
    return lax.broadcasted_iota(jnp.int32, shape, d)


def cols(off, w):
    return pl.ds(off if isinstance(off, int) else pl.multiple_of(off, 128), w)


def normal_parts(v):
    e = jnp.exp(-0.5 * v * v)
    t = 1.0 / (1.0 + 0.2316419 * jnp.abs(v))
    poly = t * (
        0.127414796
        + t * (-0.142248368 + t * (0.7107068705 + t * (-0.7265760135 + t * 0.5307027145)))
    )
    tail = poly * e
    return jnp.where(v >= 0, 1.0 - tail, tail), e


def onehot(col, width):
    return jnp.where(iota((col.shape[0], width), 1) == col, 1.0, 0.0).astype(bf16)


def message_rows():
    m = iota((GR, 1), 0)
    c = jnp.where(m >= 98, 1, 0)
    rest = m - 98 * c
    f = jnp.where(rest >= 49, 1, 0)
    return m < 196, c, f, rest - 49 * f


def to_message(owner):
    ok, c, f, q = message_rows()
    return jnp.where(ok, (2 * c + f) * GR + 49 * owner + q, -1)


def from_patches(owner):
    ok, c, f, q = message_rows()
    return jnp.where(ok, 392 * c + 8 * q + 2 * owner + f, -1)


def to_patches(chunk):
    t = iota((GR, 1), 0) + chunk * GR
    c = jnp.where(t >= 392, 1, 0)
    u = t - 392 * c
    q, fr = u >> 3, u & 7
    return jnp.where(t < 784, (fr >> 1) * GR + c * 98 + (fr & 1) * 49 + q, -1)


def to_frames(g):
    p = iota((GR, 1), 0)
    d = jnp.where(p >= 49, 1, 0) + jnp.where(p >= 98, 1, 0) + jnp.where(p >= 147, 1, 0)
    return jnp.where(p < NP, d * GR + (g // 2) * 98 + (g % 2) * 49 + p - 49 * d, -1)


def clip_mask(first):
    return (iota((R, 32), 0) >= first) == (iota((R, 32), 1) >= 16)


class Part:
    def __init__(self, ref, c0, width):
        self.ref, self.c0, self.width = ref, c0, width

    def get(self, rows=slice(None), off=0, width=None):
        return self.ref[rows, cols(self.c0 + off, self.width if width is None else width)]

    def put(self, val, rows=slice(None), off=0):
        self.ref[rows, cols(self.c0 + off, val.shape[1])] = val


def chunks(size, body):
    @pl.loop(0, R // size)
    def _(i):
        body(pl.ds(pl.multiple_of(i * size, size), size))


def tiles(total, tile, body, between):
    if total == tile:
        body(0)
    elif between is None:

        @pl.loop(0, total // tile)
        def _(i):
            body(i * tile)

    else:
        for c in range(0, total, tile):
            between(c)
            body(c)


def norm_rows(v):
    mean = jnp.mean(v, axis=-1, keepdims=True)
    cen = v - mean
    rstd = lax.rsqrt(jnp.mean(cen * cen, axis=-1, keepdims=True) + EPS)
    return cen * rstd, rstd


def norm_back_rows(v, gain, dh):
    hat, rstd = norm_rows(v)
    g = dh * gain
    m1 = jnp.mean(g, axis=-1, keepdims=True)
    m2 = jnp.mean(g * hat, axis=-1, keepdims=True)
    return rstd * (g - m1 - hat * m2)


def split_heads(v):
    first = iota(v.shape, 1) < 64
    zero = jnp.zeros(v.shape, bf16)
    return jnp.concatenate([jnp.where(first, v, zero), jnp.where(first, zero, v)], axis=0)


def join_heads(v):
    n = v.shape[0] // 2
    return jnp.where(iota((n, 128), 1) < 64, v[:n], v[n:])


def attend(qkv, rows, n, bias, out, pairs):
    q = [split_heads(qkv.get(rows, o, 128) * bf16(0.125)) for o in pairs]
    s = [dg(a, qkv.get(rows, D + o, 128), 1, 1) + bias for a, o in zip(q, pairs)]
    p = [jnp.exp(a - jnp.max(a, axis=1, keepdims=True)).astype(bf16) for a in s]
    ones = jnp.ones((n, 128), bf16)
    for a, o in zip(p, pairs):
        r = dg(a, jnp.concatenate([qkv.get(rows, 2 * D + o, 128), ones], axis=1), 1, 0)
        out.put(join_heads(r[:, :128] / r[:, 128:]).astype(bf16), rows, o)


def attend_back(qkv, rows, n, bias, dout, pairs, sums_by_product):
    q = [split_heads(qkv.get(rows, o, 128) * bf16(0.125)) for o in pairs]
    k = [qkv.get(rows, D + o, 128) for o in pairs]
    g = [split_heads(dout.get(rows, o, 128)) for o in pairs]
    s = [dg(a, b, 1, 1) + bias for a, b in zip(q, k)]
    dp = [dg(a, qkv.get(rows, 2 * D + o, 128), 1, 1) for a, o in zip(g, pairs)]
    p = [jnp.exp(a - jnp.max(a, axis=1, keepdims=True)) for a in s]
    if sums_by_product:
        ones = jnp.ones((n, n), bf16)
        p = [a * (1.0 / dg(a.astype(bf16), ones, 1, 0)) for a in p]
    else:
        p = [a * (1.0 / jnp.sum(a, axis=1, keepdims=True)) for a in p]
    ds = [(a * (b - jnp.sum(a * b, axis=1, keepdims=True))).astype(bf16) for a, b in zip(p, dp)]
    for i, o in enumerate(pairs):
        qkv.put((join_heads(dg(ds[i], k[i], 1, 0)) * 0.125).astype(bf16), rows, o)
        qkv.put(dg(ds[i], q[i], 0, 0).astype(bf16), rows, D + o)
        qkv.put(dg(p[i].astype(bf16), g[i], 0, 0).astype(bf16), rows, 2 * D + o)


def spatial_loop(count, body):
    bias = jnp.where(iota((1, GR), 1) < NP, 0.0, -BIG)
    steps = 6 // count

    @pl.loop(0, 4 * steps)
    def _(i):
        pairs = [((i % steps) * count + k) * 128 for k in range(count)]
        body(pl.ds(pl.multiple_of((i // steps) * GR, 16), GR), GR, bias, pairs)


def temporal_loop(body):
    pairs = range(0, D, 128)

    def bias(n):
        return jnp.where(((iota((2 * n, n), 0) & (n - 1)) >> 3) == (iota((2 * n, n), 1) >> 3), 0.0, -BIG)

    @pl.loop(0, 6)
    def _(i):
        body(pl.ds(pl.multiple_of(i * 128, 128), 128), 128, bias(128), pairs)

    body(pl.ds(768, 64), 64, bias(64), pairs)


class Many:
    def __init__(self, cps):
        self.cps = cps
        for cp in cps:
            cp.start()

    def wait_recv(self):
        for cp in self.cps:
            cp.wait_recv()

    def wait_send(self):
        for cp in self.cps:
            cp.wait_send()


def gather_groups():
    out = [(f"q0{c}", "q", 0, 0, 96, 16, c, D) for c in range(0, QKV, D)]
    out += [("p0", "p", 0, 0, 96, 16, 0, D), ("p1", "p", 1, 0, 96, 16, 0, D)]
    out += [(f"q1{c}", "q", 1, 0, 96, 16, c, D) for c in range(0, QKV, D)]
    out += [("p2", "p", 2, 0, 96, 16, 0, D)]
    out += [("o", "o", None, r, 96, 16, 0, D) for r in range(0, 384, 96)]
    out += [(f"i{c}", "i", None, 0, 96, 16, c, D) for c in range(0, FF, D)]
    return out


DIRECT = 0
T1, T2, T3 = 2, 2, 3


class Gather:
    def __init__(self, srcs, dsts, sems, local, ahead=3, lag=1):
        self.groups = gather_groups()
        self.srcs, self.dsts, self.sems = srcs, dsts, sems
        self.ahead, self.lag = ahead, lag
        clip, frame = lax.axis_index("clip"), lax.axis_index("frame")
        self.z, self.y, self.x, self.c = clip // 2, clip % 2, frame // 2, frame % 2
        z, y, x, c = self.z, self.y, self.x, self.c
        self.zpeers = [self.dev(lax.rem(z + k, 4), y, x, c) for k in (1, 2, 3)]
        self.ypeer, self.xpeer, self.cpeer = self.dev(z, 1 - y, x, c), self.dev(z, y, 1 - x, c), self.dev(z, y, x, 1 - c)
        self.moved = {k: {} for k in ("z", "y0", "y", "x1", "x2", "c1", "c2")}
        self.step = 0
        self.local = local

    @staticmethod
    def dev(z, y, x, c):
        return {"clip": z * 2 + y, "frame": x * 2 + c}

    def peers(self):
        return self.zpeers + [self.ypeer, self.xpeer, self.cpeer]

    def direct(self, g):
        return g < DIRECT

    def two(self, g):
        return self.span(g, 3 * self.c, 3) if self.direct(g) else self.span(g, 3 * self.c + self.x, 2)

    def span(self, g, first, count):
        _, _, _, r0, rows, unit, c0, width = self.groups[g]
        return pl.multiple_of(r0 + unit * first, 16), unit * count, c0, width

    def src(self, g, span):
        key, name, lead = self.groups[g][:3]
        r = self.srcs[name] if lead is None else self.srcs[name].at[lead]
        return r.at[pl.ds(span[0], span[1]), pl.ds(span[2], span[3])]

    def dst(self, g, z, y, span):
        key, name, lead = self.groups[g][:3]
        cs = pl.ds(span[2], span[3])
        r = self.dsts[name] if lead is None else self.dsts[name].at[lead]
        per = 384 if name == "o" else 96
        return r.at[pl.ds(pl.multiple_of((z * 2 + y) * per + span[0], 16), span[1]), cs]

    def remote(self, kind, i, s, d, peer):
        return pltpu.make_async_remote_copy(
            src_ref=s,
            dst_ref=d,
            send_sem=self.sems[0].at[kind + i],
            recv_sem=self.sems[1].at[kind + i],
            device_id=peer,
            device_id_type=MESH,
        )

    def relay(self, g, kind, items, span, peer):
        return Many(
            [self.remote(22 * g + kind, i, self.dst(g, zz, yy, span), self.dst(g, zz, yy, span), peer) for i, (zz, yy) in items]
        )

    def start_z(self, g):
        two = self.two(g)
        self.moved["z"][g] = Many(
            [self.remote(22 * g, k, self.src(g, two), self.dst(g, self.z, self.y, two), p) for k, p in enumerate(self.zpeers)]
        )
        self.moved["y0"][g] = Many([self.remote(22 * g, 3, self.src(g, two), self.dst(g, self.z, self.y, two), self.ypeer)])

    def begin(self):
        for g in range(self.ahead):
            self.start_z(g)

    def others(self, first):
        return [(q, lax.rem(self.z + q, 4)) for q in range(first, 4)]

    def tick(self):
        s, lag, ng, m, y = self.step, self.lag, len(self.groups), self.moved, self.y
        if s >= ng + 3 * lag:
            return False
        self.step += 1
        if s == 0:
            for cp in self.local:
                cp.wait()
        one, half = (3 * self.c + 2 * self.x, 1), (3 * self.c, 3)
        if s < ng:
            m["z"][s].wait_recv()
            if s + self.ahead < ng:
                self.start_z(s + self.ahead)
            m["y"][s] = self.relay(s, 4, [(q - 1, (zz, y)) for q, zz in self.others(1)], self.two(s), self.ypeer)
            if not self.direct(s):
                m["x1"][s] = self.relay(s, 7, [(q - 1, (zz, y)) for q, zz in self.others(1)], self.span(s, *one), self.xpeer)
        g = s - lag
        if 0 <= g < ng:
            m["y0"][g].wait_recv()
            m["y"][g].wait_recv()
            if not self.direct(g):
                m["x2"][g] = self.relay(g, 10, [(q, (zz, 1 - y)) for q, zz in self.others(0)], self.span(g, *one), self.xpeer)
                m["x1"][g].wait_recv()
            m["c1"][g] = self.relay(g, 14, [(q - 1, (zz, y)) for q, zz in self.others(1)], self.span(g, *half), self.cpeer)
        g = s - 2 * lag
        if 0 <= g < ng:
            if not self.direct(g):
                m["x2"][g].wait_recv()
            m["c2"][g] = self.relay(g, 17, [(q, (zz, 1 - y)) for q, zz in self.others(0)], self.span(g, *half), self.cpeer)
        g = s - 3 * lag
        if 0 <= g < ng:
            m["c1"][g].wait_recv()
            m["c2"][g].wait_recv()
        return True

    def need(self, key):
        last = max(i for i, g in enumerate(self.groups) if g[0] == key)
        while self.step <= last + 3 * self.lag:
            self.tick()

    def finish(self):
        while self.tick():
            pass
        for kind in self.moved.values():
            for cps in kind.values():
                cps.wait_send()


PIECES = [(i, 1) for i in range(6)] + [(6, 4), (10, 3), (13, 3)] + [(16 + i, 1) for i in range(4)] + [(20, 4)]


def piece_slots():
    for first, count in PIECES:
        for i in range(8 * count):
            yield first + i // 8, i % 8, i // count, first + i % count


def placement(part):
    row = iota((256, 1), 0)
    lane = row & 127
    return onehot(jnp.where(lane < 96, (2 * part + (row >> 7)) * 96 + lane, -1), D)


def place(rows):
    total = dg(rows(0), placement(0), 1, 0)
    for part in range(1, 4):
        total = total + dg(rows(part), placement(part), 1, 0)
    return total


def pick_rows(index):
    return jnp.where(iota((256, 128), 1) == index[...], 1.0, 0.0).astype(bf16)


BATCHES = ([3, 4, 5, 6, 7, 8, 9, 13, 14, 15, 18, 19, 20, 21, 22, 23], [0, 1, 2, 10, 11, 12, 16, 17])
PLACES = {p: i for i, p in enumerate(BATCHES[0] + BATCHES[1])}


class Reduce:
    def __init__(self, batch, blocks, work, received, result, nidx, sems):
        self.batch, self.blocks, self.work = batch, blocks, work
        self.received, self.result, self.nidx, self.sems = received, result, nidx, sems
        clip, frame = lax.axis_index("clip"), lax.axis_index("frame")
        self.clip, self.frame, self.x, self.c = clip, frame, frame // 2, frame % 2
        self.xpeer = {"clip": clip, "frame": (1 - self.x) * 2 + self.c}
        self.cpeer = {"clip": clip, "frame": self.x * 2 + 1 - self.c}
        self.width = len(BATCHES[batch]) * 32
        self.count = 0
        self.sent = []

    def lanes(self, quarter):
        return pl.ds(pl.multiple_of(2048 * self.batch + self.width * quarter, 128), self.width)

    def send(self, src, dst, peer):
        i = 16 * self.batch + self.count
        self.count += 1
        cp = pltpu.make_async_remote_copy(
            src_ref=src, dst_ref=dst, send_sem=self.sems.at[0, i], recv_sem=self.sems.at[1, i], device_id=peer, device_id_type=MESH
        )
        cp.start()
        self.sent.append(cp)
        return cp

    def add(self, first_row, quarter):
        ls = self.lanes(quarter)
        total = self.work[pl.ds(0, 256), ls].astype(f32) + self.work[pl.ds(first_row, 256), ls].astype(f32)
        self.work[pl.ds(0, 256), ls] = total.astype(bf16)

    def split(self):
        pieces = BATCHES[self.batch]
        for part in range(4):
            rows = self.blocks[pl.ds(512 * self.batch, 32 * len(pieces)), :]
            parts = dg(rows, placement(part), 1, 1).astype(bf16)
            for block, slot, owner, piece in piece_slots():
                if block in pieces and slot // 2 == part:
                    i = pieces.index(block)
                    tile = parts[32 * i : 32 * i + 32, 128 * (slot % 2) : 128 * (slot % 2) + 128]
                    self.work[pl.ds(32 * owner, 32), pl.ds(128 * PLACES[piece], 128)] = tile
        self.core = []
        for xx in range(2):
            ls = self.lanes(2 * xx + 1 - self.c)
            self.core.append(self.send(self.work.at[pl.ds(0, 256), ls], self.work.at[pl.ds(256, 256), ls], self.cpeer))

    def over_x(self):
        for xx in range(2):
            self.core[xx].wait_recv()
        for xx in range(2):
            self.add(256, 2 * xx + self.c)
        ls = self.lanes(2 * (1 - self.x) + self.c)
        self.across = self.send(self.work.at[pl.ds(0, 256), ls], self.work.at[pl.ds(512, 256), ls], self.xpeer)

    def to_owners(self):
        self.across.wait_recv()
        self.add(512, self.frame)
        ls = self.lanes(self.frame)
        self.here = pl.ds(512 * self.batch, self.width)
        mine = pl.ds(pl.multiple_of(32 * self.clip, 32), 32)
        self.received[mine, self.here] = self.work[mine, ls]
        self.owned = []
        for k in range(1, 8):
            j = lax.rem(self.clip + k, 8)
            rows = pl.ds(pl.multiple_of(32 * j, 32), 32)
            self.owned.append(
                self.send(self.work.at[rows, ls], self.received.at[mine, self.here], {"clip": j, "frame": self.frame})
            )

    def by_adapter(self):
        for cp in self.owned:
            cp.wait_recv()
        ls = self.lanes(self.frame)
        self.result[:, ls] = dg(pick_rows(self.nidx), self.received[:, self.here], 0, 0).astype(bf16)
        same = self.result.at[:, ls]
        self.back = [self.send(same, same, p) for p in (self.xpeer, self.cpeer)]

    def spread(self):
        self.back[0].wait_recv()
        same = self.result.at[:, self.lanes(2 * (1 - self.x) + self.c)]
        self.last = self.send(same, same, self.cpeer)

    def finish(self):
        self.back[1].wait_recv()
        self.last.wait_recv()
        for cp in self.sent:
            cp.wait_send()


def layer_kernel(
    gathers, hidx, x_ref, g_ref, hq, hp, hi, ho, had, hnm,
    out, ig, grads, spill,
    wq, wp, wi, wo, ad, nm, nbuf, nidx, received, rcv_a, rcv_b, big, x1, x2, tmp, o2, qkv2, a0, a1, us,
    wsem, ssem, rsem, psem, gssem, grsem, nsem, asem, bsem,
):
    buf_g, buf_d = big.at[0], big.at[1]

    clip = lax.axis_index("clip")
    me = lax.axis_index("frame")
    nf = 4
    peers = [lax.rem(me + k, nf) for k in range(1, nf)]

    fetch = [pltpu.make_async_copy(s, d, wsem.at[10 + i]) for i, (s, d) in enumerate(((x_ref, ig), (g_ref, out)))]
    for cp in fetch:
        cp.start()
    barrier = pltpu.get_barrier_semaphore()
    groups_of = [{"clip": clip, "frame": d} for d in peers]
    loads = {}
    if gathers:
        own = pl.ds(pl.multiple_of(clip * 96, 16), 96)
        local = [
            (hq.at[0], wq.at[0, own]), (hq.at[1], wq.at[1, own]), (hp.at[0], wp.at[0, own]), (hp.at[1], wp.at[1, own]),
            (hp.at[2], wp.at[2, own]), (hi, wi.at[own]), (ho, wo.at[pl.ds(pl.multiple_of(clip * 384, 16), 384)]),
            (had, big.at[1, pl.ds(0, 128)]), (hnm, nbuf.at[pl.ds(pl.multiple_of(clip * 16, 16), 16)]),
            (hidx, nidx.at[pl.ds(pl.multiple_of(clip * 32, 32), 32)]),
        ]
        local = [pltpu.make_async_copy(s, d, wsem.at[i]) for i, (s, d) in enumerate(local)]
        for cp in local:
            cp.start()
        net = Gather(
            {"q": hq, "p": hp, "i": hi, "o": ho},
            {"q": wq, "p": wp, "i": wi, "o": wo},
            (gssem, grsem),
            local[:7],
        )
        owners = [{"clip": lax.rem(clip + k, 8), "frame": me} for k in range(1, 8)]
        greet = groups_of + owners
    else:
        net = None
        for key, src, dst in (
            ("q0", hq.at[0], wq.at[0]), ("p0", hp.at[0], wp.at[0]), ("p1", hp.at[1], wp.at[1]), ("q1", hq.at[1], wq.at[1]),
            ("p2", hp.at[2], wp.at[2]), ("o", ho, wo), ("i", hi, wi), ("ad", had, ad), ("nm", hnm, nm),
        ):
            loads[key] = pltpu.make_async_copy(src, dst, wsem.at[len(loads)])
            loads[key].start()
        greet = groups_of
    for p in greet:
        pl.semaphore_signal(barrier, inc=1, device_id=p, device_id_type=MESH)
    pl.semaphore_wait(barrier, len(greet))

    def need(key, c=""):
        if net is not None:
            net.need(f"{key}{c}")
        elif not c:
            loads[key].wait()

    def need_tiles(key):
        def between(c):
            need(key, c)

        return between

    def tick():
        if net is not None:
            net.tick()

    if gathers:

        def to(peer, src, dst, sems, i):
            cp = pltpu.make_async_remote_copy(
                src_ref=src, dst_ref=dst, send_sem=sems.at[0, i], recv_sem=sems.at[1, i], device_id=peer, device_id_type=MESH
            )
            cp.start()
            return cp

        rows16 = pl.ds(pl.multiple_of(clip * 16, 16), 16)
        rows32 = pl.ds(pl.multiple_of(clip * 32, 32), 32)
        small = [to(p, hidx, nidx.at[rows32], nsem, k) for k, p in enumerate(owners)]
        small += [to(p, hnm, nbuf.at[rows16], nsem, 7 + k) for k, p in enumerate(owners)]
        net.begin()

    def exchange(step, src, index, rcv):
        sent = []
        for k, d in enumerate(peers):
            slot = pl.ds(k * GR, GR)
            o2[slot, :] = dg(onehot(index(d), R), src.get(), 1, 0).astype(bf16)
            cp = pltpu.make_async_remote_copy(
                src_ref=o2.at[slot],
                dst_ref=rcv.at[pl.ds(pl.multiple_of(me * GR, 16), GR)],
                send_sem=ssem.at[step, k],
                recv_sem=rsem.at[step, k],
                device_id={"clip": clip, "frame": d},
                device_id_type=MESH,
            )
            cp.start()
            sent.append(cp)
        rcv[pl.ds(pl.multiple_of(me * GR, 16), GR), :] = dg(onehot(index(me), R), src.get(), 1, 0).astype(bf16)

        def finish():
            for cp in sent:
                cp.wait_recv()
            for cp in sent:
                cp.wait_send()

        return finish

    def gain(k):
        return nm[k : k + 1, :]

    def norm(k, read, put):
        def body(rows):
            hat, _ = norm_rows(read(rows))
            put(rows, (hat * gain(k) + gain(3 + k)).astype(bf16))

        chunks(208, body)

    def rank(h, at, mask, m):
        us[:, pl.ds(32 * m, 32)] = jnp.where(mask, dg(h.get(), ad[:, pl.ds(at, h.width)], 1, 1), 0.0).astype(bf16)

    def forward(m, h, w, width, tile, mask, emit, between=None):
        rank(h, DOWN[m], mask, m)

        def body(c):
            acc = dg(h.get(), w[:, cols(c, tile)], 1, 0)
            acc = acc + dg(us[:, pl.ds(32 * m, 32)], ad[:, cols(UP[m] + c, tile)], 1, 0)
            emit(c, acc)

        tiles(width, tile, body, between)

    def rank_back(m, dz, mask):
        du = jnp.where(mask, dg(dz.get(), ad[:, pl.ds(UP[m], dz.width)], 1, 1), 0.0).astype(bf16)
        us[:, pl.ds(224, 32)] = du

    def backward(m, dz, w, width, tile, mask, emit, between=None):
        rank_back(m, dz, mask)
        backward_rows(m, dz, w, width, tile, emit, between)

    def backward_rows(m, dz, w, width, tile, emit, between=None):

        def body(c):
            acc = dg(dz.get(), w[cols(c, tile), :], 1, 1)
            acc = acc + dg(us[:, pl.ds(224, 32)], ad[:, cols(DOWN[m] + c, tile)], 1, 0)
            emit(c, acc)

        tiles(width, tile, body, between)

    def adapter_grads(m, h, dz):
        for at, side, rows in ((DOWN[m], 224, h), (UP[m], 32 * m, dz)):
            val = dg(us[:, pl.ds(side, 32)], rows.get(), 0, 0).astype(bf16)
            for k in range(rows.width // D):
                wo[pl.ds(32 * PLACES[at // D + k], 32), :] = val[:, k * D : k * D + D]

    p_a0, p_a1 = Part(a0, 0, D), Part(a1, 0, D)
    qkv1, h1 = Part(buf_g, 0, QKV), Part(buf_g, QKV, D)
    xt, o1, m1, spare = (Part(buf_d, D * i, D) for i in range(4))
    p_o2, p_qkv2, p_g, p_d = Part(o2, 0, D), Part(qkv2, 0, QKV), Part(buf_g, 0, FF), Part(buf_d, 0, FF)

    if gathers:
        for cp in local[7:]:
            cp.wait()
        for cp in small[:7]:
            cp.wait_recv()
        pick = pick_rows(nidx)
        quarter = cols(me * D, D)
        chosen = big.at[1, pl.ds(128, 256), pl.ds(0, D)]
        big[1, pl.ds(128, 256), pl.ds(0, D)] = dg(pick, big[1, pl.ds(0, 128), quarter], 1, 0).astype(bf16)
        picked = []
        for k, p in enumerate(owners):
            rows = pl.ds(pl.multiple_of(128 + 32 * p["clip"], 32), 32)
            picked.append(to(p, big.at[1, rows, pl.ds(0, D)], big.at[0, rows32, quarter], asem, k))
        big[0, rows32, quarter] = big[1, pl.ds(pl.multiple_of(128 + 32 * clip, 32), 32), pl.ds(0, D)]

    for i, (src, dst) in enumerate(((ig, a0), (out, a1))):
        fetch[i].wait()
        for g in range(4):
            dst[pl.ds(GR * g + 192, 16), :] = jnp.zeros((16, D), bf16)
            dst[pl.ds(GR * g, NP), :] = src[g // 2, g % 2]
        if dst is a0:
            arrive = exchange(0, p_a0, to_message, rcv_a)

    mask_t = clip_mask(392)
    mask_s = clip_mask(416)
    if gathers:
        tick()
        for cp in picked:
            cp.wait_recv()

        def block_of(frame):
            return big.at[0, pl.ds(0, 256), cols(frame * D, D)]

        x, c = me // 2, me % 2
        xpeer, cpeer = {"clip": clip, "frame": (1 - x) * 2 + c}, {"clip": clip, "frame": x * 2 + 1 - c}
        picked.append(to(xpeer, block_of(me), block_of(me), asem, 7))
        picked.append(to(cpeer, block_of(me), block_of(me), asem, 8))
        for _ in range(T1):
            tick()
        picked[7].wait_recv()
        far = (1 - x) * 2 + c
        picked.append(to(cpeer, block_of(far), block_of(far), asem, 9))
        picked[8].wait_recv()
        picked[9].wait_recv()
        for cp in picked:
            cp.wait_send()
        for owner in range(8):
            part = big[0, pl.ds(32 * owner, 32), :]
            for block, slot, of, piece in piece_slots():
                if of == owner:
                    qkv2[pl.ds(block * 32, 32), pl.ds(slot * 128, 128)] = part[:, piece * 128 : piece * 128 + 128]
        joined = place(lambda part: qkv2[pl.ds(0, 768), pl.ds(256 * part, 256)]).astype(bf16)
        for block in range(24):
            ad[:, pl.ds(block * D, D)] = joined[block * 32 : block * 32 + 32]
        for cp in small[7:]:
            cp.wait_recv()
        for j in range(8):
            qkv2[pl.ds(0, 16), pl.ds(j * 128, 128)] = nbuf[pl.ds(16 * j, 16), :]
        nm[...] = place(lambda part: qkv2[pl.ds(0, 16), pl.ds(256 * part, 256)])
    else:
        need("ad")
        need("nm")
    for _ in range(T2):
        tick()
    arrive()
    for i in range(4):
        xt.put(dg(onehot(to_patches(i), R), rcv_a[...], 1, 0).astype(bf16), pl.ds(i * GR, GR))
    tick()
    norm(0, lambda rows: xt.get(rows).astype(f32), lambda rows, v: h1.put(v, rows))
    tick()
    forward(0, h1, wq.at[0], QKV, 768, mask_t, lambda c, acc: qkv1.put(acc.astype(bf16), off=c), need_tiles("q0"))
    tick()
    temporal_loop(lambda rows, n, bias, pairs: attend(qkv1, rows, n, bias, o1, pairs))
    tick()
    need("p0")
    forward(1, o1, wp.at[0], D, 384, mask_t, lambda c, acc: m1.put(acc.astype(bf16), off=c))
    tick()
    need("p1")
    forward(2, m1, wp.at[1], D, 384, mask_t, lambda c, acc: spare.put(acc.astype(bf16), off=c))
    tick()
    arrive = exchange(1, spare, from_patches, rcv_b)
    tick()
    saves = [pltpu.make_async_copy(b, spill.at[i], psem.at[i]) for i, b in enumerate((buf_g, buf_d))]
    for cp in saves:
        cp.start()
    for cp in saves:
        cp.wait()
    for _ in range(T3):
        tick()
    arrive()

    for g in range(4):
        rows = pl.ds(g * GR, GR)
        tb = dg(onehot(to_frames(g), R), rcv_b[...], 1, 0)
        x1[rows, :] = a0[rows, :].astype(f32) + tb
    tick()
    norm(1, lambda rows: x1[rows, :], lambda rows, v: p_o2.put(v, rows))
    tick()
    forward(3, p_o2, wq.at[1], QKV, 768, mask_s, lambda c, acc: p_qkv2.put(acc.astype(bf16), off=c), need_tiles("q1"))
    tick()
    spatial_loop(3, lambda rows, n, bias, pairs: attend(p_qkv2, rows, n, bias, p_o2, pairs))
    tick()
    need("p2")

    def add_spatial(c, acc):
        x2[:, cols(c, 384)] = x1[:, cols(c, 384)] + acc

    forward(4, p_o2, wp.at[2], D, 384, mask_s, add_spatial)
    tick()

    need("o")
    backward(6, p_a1, wo, FF, 768, mask_s, lambda c, acc: p_d.put(acc.astype(bf16), off=c), lambda c: tick())
    us[:, pl.ds(256, 32)] = us[:, pl.ds(224, 32)]

    norm(2, lambda rows: x2[rows, :], lambda rows, v: p_a0.put(v, rows))

    def activate(c, acc):
        tmp_w = acc.shape[1]
        tmp[:, pl.ds(0, tmp_w)] = acc
        @pl.loop(0, R // 32)
        def _(i):
            rows = pl.ds(pl.multiple_of(i * 32, 32), 32)
            v = tmp[rows, pl.ds(0, tmp_w)]
            phi, e = normal_parts(v)
            slope = phi + v * e * 0.3989422804014327
            p_g.put((v * phi).astype(bf16), rows, c)
            p_d.put((p_d.get(rows, c, tmp_w).astype(f32) * slope).astype(bf16), rows, c)

    forward(5, p_a0, wi, FF, 768, mask_s, activate, need_tiles("i"))

    def emit_out(c, acc):
        y = (x2[:, cols(c, 384)] + acc).astype(bf16)
        for g in range(4):
            out[g // 2, g % 2, :, cols(c, 384)] = y[g * GR : g * GR + NP]

    forward(6, p_g, wo, D, 384, mask_s, emit_out)
    if gathers:
        net.finish()
        for cp in small:
            cp.wait_send()

    us[:, pl.ds(224, 32)] = us[:, pl.ds(256, 32)]
    adapter_grads(6, p_g, p_a1)

    def emit_tmp(c, acc):
        tmp[:, cols(c, 384)] = acc

    backward(5, p_d, wi, D, 384, mask_s, emit_tmp)
    adapter_grads(5, p_a0, p_d)
    loads_back = [pltpu.make_async_copy(spill.at[i], b, psem.at[i]) for i, b in enumerate((buf_g, buf_d))]
    for cp in loads_back:
        cp.start()

    def step_two(rows):
        dx = a1[rows, :].astype(f32) + norm_back_rows(x2[rows, :], gain(2), tmp[rows, :])
        x2[rows, :] = dx
        a0[rows, :] = dx.astype(bf16)

    chunks(208, step_two)

    backward(4, p_a0, wp.at[2], D, 384, mask_s, lambda c, acc: p_a1.put(acc.astype(bf16), off=c))
    adapter_grads(4, p_o2, p_a0)
    spatial_loop(2, lambda rows, n, bias, pairs: attend_back(p_qkv2, rows, n, bias, p_a1, pairs, False))
    backward(3, p_qkv2, wq.at[1], D, 384, mask_s, emit_tmp)

    def step_one(rows):
        dx = x2[rows, :] + norm_back_rows(x1[rows, :], gain(1), tmp[rows, :])
        x2[rows, :] = dx
        a0[rows, :] = dx.astype(bf16)

    chunks(208, step_one)
    arrive = exchange(2, p_a0, to_message, rcv_a)
    norm(1, lambda rows: x1[rows, :], lambda rows, v: p_a1.put(v, rows))
    adapter_grads(3, p_a1, p_qkv2)
    for cp in loads_back:
        cp.wait()
    arrive()

    if gathers:
        first, second = (Reduce(i, wo, wi, received, grads, nidx, bsem) for i in range(2))
        first.split()
    for i in range(4):
        p_a0.put(dg(onehot(to_patches(i), R), rcv_a[...], 1, 0).astype(bf16), pl.ds(i * GR, GR))
    backward(2, p_a0, wp.at[1], D, 384, mask_t, lambda c, acc: p_a1.put(acc.astype(bf16), off=c))
    adapter_grads(2, m1, p_a0)
    if gathers:
        first.over_x()
    backward(1, p_a1, wp.at[0], D, 384, mask_t, lambda c, acc: spare.put(acc.astype(bf16), off=c))
    adapter_grads(1, o1, p_a1)
    temporal_loop(lambda rows, n, bias, pairs: attend_back(qkv1, rows, n, bias, spare, pairs, True))
    if gathers:
        first.to_owners()
    rank_back(0, qkv1, mask_t)
    adapter_grads(0, h1, qkv1)
    if gathers:
        second.split()
        first.by_adapter()
    backward_rows(0, qkv1, wq.at[0], D, 384, emit_tmp)
    if gathers:
        second.over_x()
        first.spread()

    def step_zero(rows):
        dx = norm_back_rows(xt.get(rows).astype(f32), gain(0), tmp[rows, :])
        a0[rows, :] = dx.astype(bf16)

    chunks(208, step_zero)
    if gathers:
        second.to_owners()
    arrive = exchange(3, p_a0, from_patches, rcv_b)
    if gathers:
        second.by_adapter()
        first.finish()
        second.spread()
    arrive()
    for g in range(4):
        dxt = dg(onehot(to_frames(g), R), rcv_b[...], 1, 0)
        total = x2[pl.ds(g * GR, GR), :] + dxt
        ig[g // 2, g % 2] = total.astype(bf16)[:NP]
    if gathers:
        second.finish()
    else:
        for block in range(24):
            grads[:, pl.ds(block * D, D)] = wo[pl.ds(32 * PLACES[block], 32), :]


def layer(gathers, index_rows, x, g, hq, hp, hi, ho, ad, nm):
    vm = pl.BlockSpec(memory_space=pltpu.VMEM)
    hbm = pl.BlockSpec(memory_space=pl.ANY)
    dma = pltpu.SemaphoreType.DMA
    rows = lambda w, t=bf16: pltpu.VMEM((R, w), t)
    ng = len(gather_groups()) if gathers else 1
    return pl.pallas_call(
        functools.partial(layer_kernel, gathers),
        out_shape=[
            jax.ShapeDtypeStruct(x.shape, bf16),
            jax.ShapeDtypeStruct(x.shape, bf16),
            jax.ShapeDtypeStruct((128, 24 * 128) if gathers else (32, ADW), bf16),
            jax.ShapeDtypeStruct((2, R, FF), bf16),
        ],
        in_specs=[hbm] * 9,
        out_specs=[vm] * 3 + [hbm],
        scratch_shapes=[
            pltpu.VMEM((2, D, QKV), bf16), pltpu.VMEM((3, D, D), bf16), pltpu.VMEM((D, FF), bf16), pltpu.VMEM((FF, D), bf16),
            pltpu.VMEM((32, ADW), bf16), pltpu.VMEM((16, D), f32), pltpu.VMEM((128, 128), bf16),
            pltpu.VMEM((256, 128), jnp.int32), pltpu.VMEM((256, D), bf16),
            rows(D), rows(D), pltpu.VMEM((2, R, FF), bf16), rows(D, f32), rows(D, f32), rows(D, f32),
            rows(D), rows(QKV), rows(D), rows(D), rows(384),
            dma((12,)), dma((4, 3)), dma((4, 3)), dma((2,)), dma((22 * ng,)), dma((22 * ng,)), dma((2, 14)), dma((2, 10)), dma((2, 32)),
        ],
        compiler_params=pltpu.CompilerParams(
            collective_id=1, has_side_effects=True, vmem_limit_bytes=64 * 2**20 - 2**17
        ),
        name="layer",
    )(index_rows, x, g, hq, hp, hi, ho, ad, nm)


def piece_widths(w):
    return [w] * 6 + [4 * w] + [3 * w] * 2 + [w] * 4 + [4 * w]


def pack_adapters(adapt_down, adapt_down_wide, adapt_up_qkv, adapt_up, adapt_up_wide):
    adapters = adapt_down_wide.shape[0]

    def flat(v):
        return v.reshape(adapters, RANK, -1)

    return jnp.concatenate(
        [
            flat(adapt_down.transpose(1, 3, 0, 2)),
            flat(adapt_down_wide.transpose(0, 2, 1)),
            flat(adapt_up_qkv.transpose(1, 2, 0, 3)),
            flat(adapt_up.transpose(1, 2, 0, 3)),
            flat(adapt_up_wide),
        ],
        axis=-1,
    )


def join_pieces(parts, w):
    joined, at = [], 0
    for width in piece_widths(w):
        piece = parts[:, :, at : at + width]
        joined.append(piece.transpose(1, 0, 2).reshape(parts.shape[1], -1))
        at += width
    return jnp.concatenate(joined, axis=-1)


def split_pieces(rows, w, owners):
    parts, at = [], 0
    for width in piece_widths(w):
        piece = rows[:, at : at + width * owners]
        parts.append(piece.reshape(rows.shape[0], owners, width).transpose(1, 0, 2))
        at += width * owners
    return jnp.concatenate(parts, axis=-1)


def per_device(
    inputs,
    out_grad,
    adapter_index,
    norm_gain,
    norm_bias,
    qkv_weight,
    proj_weight,
    mlp_in,
    mlp_out,
    adapt_down,
    adapt_down_wide,
    adapt_up_qkv,
    adapt_up,
    adapt_up_wide,
):
    owners = lax.axis_size("clip")
    adapters = adapt_down_wide.shape[0]
    clips = inputs.shape[0]
    w = norm_gain.shape[1]
    packed = pack_adapters(adapt_down, adapt_down_wide, adapt_up_qkv, adapt_up, adapt_up_wide)
    norms = jnp.concatenate([norm_gain, norm_bias], axis=0)
    if owners == 8:
        index_rows = adapter_index[:, None] * RANK + jnp.arange(RANK, dtype=jnp.int32)[None, :]
        index_rows = jnp.broadcast_to(index_rows.reshape(clips * RANK, 1), (clips * RANK, 128))
        pieces = packed.reshape(adapters * RANK, 24, w)
        table = jnp.pad(pieces, ((0, 0), (0, 0), (0, 128 - w))).reshape(adapters * RANK, 24 * 128)
        own_norms = jnp.pad(norms, ((0, 10), (0, 128 - w)))
        output, input_grad, grads, _ = layer(
            True, index_rows, inputs, out_grad, qkv_weight, proj_weight, mlp_in, mlp_out, table, own_norms
        )
        grads = grads.reshape(adapters, RANK, 24, 128)[..., :w].astype(f32)
        summed = jnp.concatenate([grads[:, :, PLACES[p]] for p in range(24)], axis=-1)
    else:
        full_qkv = lax.all_gather(qkv_weight, "clip", axis=1, tiled=True)
        full_proj = lax.all_gather(proj_weight, "clip", axis=1, tiled=True)
        full_in = lax.all_gather(mlp_in, "clip", axis=0, tiled=True)
        full_out = lax.all_gather(mlp_out, "clip", axis=0, tiled=True)
        table = lax.all_gather(packed, "clip", axis=0)
        all_norms = lax.all_gather(norms, "clip", axis=0)
        nm = jnp.pad(all_norms.transpose(1, 0, 2).reshape(6, D).astype(f32), ((0, 10), (0, 0)))
        chosen = jnp.take(table, adapter_index, axis=1).reshape(owners, clips * RANK, 24 * w)
        ad = join_pieces(chosen, w)
        output, input_grad, grads, _ = layer(
            False, adapter_index, inputs, out_grad, full_qkv, full_proj, full_in, full_out, ad, nm
        )
        parts = split_pieces(grads, w, owners)
        parts = lax.all_to_all(parts, "clip", split_axis=0, concat_axis=0, tiled=True)
        every = lax.all_gather(adapter_index, "clip", axis=0, tiled=True)
        pick = (every[:, None] == jnp.arange(adapters, dtype=jnp.int32)[None, :]).astype(bf16)
        summed = jnp.einsum(
            "ca,crm->arm", pick, parts.reshape(owners * clips, RANK, 24 * w), preferred_element_type=f32
        )
        summed = lax.psum(summed.astype(bf16), "frame").astype(f32)
    return (output, input_grad) + unpack_grads(summed, w)


def unpack_grads(summed, w):
    adapters = summed.shape[0]
    down = summed[:, :, : 6 * w].reshape(adapters, RANK, 6, w).transpose(2, 0, 3, 1)
    down_wide = summed[:, :, 6 * w : 10 * w].transpose(0, 2, 1)
    up_qkv = summed[:, :, 10 * w : 16 * w].reshape(adapters, RANK, 2, 3 * w).transpose(2, 0, 1, 3)
    up = summed[:, :, 16 * w : 20 * w].reshape(adapters, RANK, 4, w).transpose(2, 0, 1, 3)
    return (down, down_wide, up_qkv, up, summed[:, :, 20 * w :])


def solution(mesh):
    return jax.shard_map(
        per_device,
        mesh=mesh,
        in_specs=(
            P("clip", "frame", None, None),
            P("clip", "frame", None, None),
            P("clip"),
            P(None, "clip"),
            P(None, "clip"),
            P(None, "clip", None),
            P(None, "clip", None),
            P("clip", None),
            P("clip", None),
            P(None, None, "clip", None),
            P(None, "clip", None),
            P(None, None, None, "clip"),
            P(None, None, None, "clip"),
            P(None, None, "clip"),
        ),
        out_specs=(
            P("clip", "frame", None, None),
            P("clip", "frame", None, None),
            P(None, None, "clip", None),
            P(None, "clip", None),
            P(None, None, None, "clip"),
            P(None, None, None, "clip"),
            P(None, None, "clip"),
        ),
        check_vma=False,
    )
```

```python
import functools
import jax
import jax.numpy as jnp
from jax import lax
from jax.experimental import pallas as pl
from jax.experimental.pallas import tpu as pltpu
from jax.sharding import PartitionSpec as P

EPS = 1e-06
MESH = pl.DeviceIdType.MESH
f32 = jnp.float32
bf16 = jnp.bfloat16
D, FF, QKV, RANK = 768, 3072, 2304, 16
NP, GR, R = 196, 208, 832
DOWN = (0, 768, 1536, 2304, 3072, 3840, 4608)
UP = (7680, 12288, 13056, 9984, 13824, 15360, 14592)
ADW = 18432
BIG = 1e30


def dg(a, b, ca, cb):
    return lax.dot_general(a, b, (((ca,), (cb,)), ((), ())), preferred_element_type=f32)


def iota(shape, d):
    return lax.broadcasted_iota(jnp.int32, shape, d)


def cols(off, w):
    return pl.ds(off if isinstance(off, int) else pl.multiple_of(off, 128), w)


def normal_parts(v):
    e = jnp.exp(-0.5 * v * v)
    t = 1.0 / (1.0 + 0.2316419 * jnp.abs(v))
    poly = t * (
        0.127414796
        + t * (-0.142248368 + t * (0.7107068705 + t * (-0.7265760135 + t * 0.5307027145)))
    )
    tail = poly * e
    return jnp.where(v >= 0, 1.0 - tail, tail), e


def onehot(col, width):
    return jnp.where(iota((col.shape[0], width), 1) == col, 1.0, 0.0).astype(bf16)


def message_rows():
    m = iota((GR, 1), 0)
    c = jnp.where(m >= 98, 1, 0)
    rest = m - 98 * c
    f = jnp.where(rest >= 49, 1, 0)
    return m < 196, c, f, rest - 49 * f


def to_message(owner):
    ok, c, f, q = message_rows()
    return jnp.where(ok, (2 * c + f) * GR + 49 * owner + q, -1)


def from_patches(owner):
    ok, c, f, q = message_rows()
    return jnp.where(ok, 392 * c + 8 * q + 2 * owner + f, -1)


def to_patches(chunk):
    t = iota((GR, 1), 0) + chunk * GR
    c = jnp.where(t >= 392, 1, 0)
    u = t - 392 * c
    q, fr = u >> 3, u & 7
    return jnp.where(t < 784, (fr >> 1) * GR + c * 98 + (fr & 1) * 49 + q, -1)


def to_frames(g):
    p = iota((GR, 1), 0)
    d = jnp.where(p >= 49, 1, 0) + jnp.where(p >= 98, 1, 0) + jnp.where(p >= 147, 1, 0)
    return jnp.where(p < NP, d * GR + (g // 2) * 98 + (g % 2) * 49 + p - 49 * d, -1)


def clip_mask(first):
    return (iota((R, 32), 0) >= first) == (iota((R, 32), 1) >= 16)


class Part:
    def __init__(self, ref, c0, width):
        self.ref, self.c0, self.width = ref, c0, width

    def get(self, rows=slice(None), off=0, width=None):
        return self.ref[rows, cols(self.c0 + off, self.width if width is None else width)]

    def put(self, val, rows=slice(None), off=0):
        self.ref[rows, cols(self.c0 + off, val.shape[1])] = val


def chunks(size, body):
    @pl.loop(0, R // size)
    def _(i):
        body(pl.ds(pl.multiple_of(i * size, size), size))


def tiles(total, tile, body, between):
    if total == tile:
        body(0)
    elif between is None:

        @pl.loop(0, total // tile)
        def _(i):
            body(i * tile)

    else:
        for c in range(0, total, tile):
            between(c)
            body(c)


def norm_rows(v):
    mean = jnp.mean(v, axis=-1, keepdims=True)
    cen = v - mean
    rstd = lax.rsqrt(jnp.mean(cen * cen, axis=-1, keepdims=True) + EPS)
    return cen * rstd, rstd


def norm_back_rows(v, gain, dh):
    hat, rstd = norm_rows(v)
    g = dh * gain
    m1 = jnp.mean(g, axis=-1, keepdims=True)
    m2 = jnp.mean(g * hat, axis=-1, keepdims=True)
    return rstd * (g - m1 - hat * m2)


def split_heads(v):
    first = iota(v.shape, 1) < 64
    zero = jnp.zeros(v.shape, bf16)
    return jnp.concatenate([jnp.where(first, v, zero), jnp.where(first, zero, v)], axis=0)


def join_heads(v):
    n = v.shape[0] // 2
    return jnp.where(iota((n, 128), 1) < 64, v[:n], v[n:])


def attend(qkv, rows, n, bias, out, pairs):
    q = [split_heads(qkv.get(rows, o, 128) * bf16(0.125)) for o in pairs]
    s = [dg(a, qkv.get(rows, D + o, 128), 1, 1) + bias for a, o in zip(q, pairs)]
    p = [jnp.exp(a - jnp.max(a, axis=1, keepdims=True)).astype(bf16) for a in s]
    ones = jnp.ones((n, 128), bf16)
    for a, o in zip(p, pairs):
        r = dg(a, jnp.concatenate([qkv.get(rows, 2 * D + o, 128), ones], axis=1), 1, 0)
        out.put(join_heads(r[:, :128] / r[:, 128:]).astype(bf16), rows, o)


def attend_back(qkv, rows, n, bias, dout, pairs, sums_by_product):
    q = [split_heads(qkv.get(rows, o, 128) * bf16(0.125)) for o in pairs]
    k = [qkv.get(rows, D + o, 128) for o in pairs]
    g = [split_heads(dout.get(rows, o, 128)) for o in pairs]
    s = [dg(a, b, 1, 1) + bias for a, b in zip(q, k)]
    dp = [dg(a, qkv.get(rows, 2 * D + o, 128), 1, 1) for a, o in zip(g, pairs)]
    p = [jnp.exp(a - jnp.max(a, axis=1, keepdims=True)) for a in s]
    if sums_by_product:
        ones = jnp.ones((n, n), bf16)
        p = [a * (1.0 / dg(a.astype(bf16), ones, 1, 0)) for a in p]
    else:
        p = [a * (1.0 / jnp.sum(a, axis=1, keepdims=True)) for a in p]
    ds = [(a * (b - jnp.sum(a * b, axis=1, keepdims=True))).astype(bf16) for a, b in zip(p, dp)]
    for i, o in enumerate(pairs):
        qkv.put((join_heads(dg(ds[i], k[i], 1, 0)) * 0.125).astype(bf16), rows, o)
        qkv.put(dg(ds[i], q[i], 0, 0).astype(bf16), rows, D + o)
        qkv.put(dg(p[i].astype(bf16), g[i], 0, 0).astype(bf16), rows, 2 * D + o)


def spatial_loop(count, body):
    bias = jnp.where(iota((1, GR), 1) < NP, 0.0, -BIG)
    steps = 6 // count

    @pl.loop(0, 4 * steps)
    def _(i):
        pairs = [((i % steps) * count + k) * 128 for k in range(count)]
        body(pl.ds(pl.multiple_of((i // steps) * GR, 16), GR), GR, bias, pairs)


def temporal_loop(body):
    pairs = range(0, D, 128)

    def bias(n):
        return jnp.where(((iota((2 * n, n), 0) & (n - 1)) >> 3) == (iota((2 * n, n), 1) >> 3), 0.0, -BIG)

    @pl.loop(0, 6)
    def _(i):
        body(pl.ds(pl.multiple_of(i * 128, 128), 128), 128, bias(128), pairs)

    body(pl.ds(768, 64), 64, bias(64), pairs)


class Many:
    def __init__(self, cps):
        self.cps = cps
        for cp in cps:
            cp.start()

    def wait_recv(self):
        for cp in self.cps:
            cp.wait_recv()

    def wait_send(self):
        for cp in self.cps:
            cp.wait_send()


def gather_groups():
    out = [(f"q0{c}", "q", 0, 0, 96, 16, c, D) for c in range(0, QKV, D)]
    out += [("p0", "p", 0, 0, 96, 16, 0, D), ("p1", "p", 1, 0, 96, 16, 0, D)]
    out += [(f"q1{c}", "q", 1, 0, 96, 16, c, D) for c in range(0, QKV, D)]
    out += [("p2", "p", 2, 0, 96, 16, 0, D)]
    out += [("o", "o", None, r, 96, 16, 0, D) for r in range(0, 384, 96)]
    out += [(f"i{c}", "i", None, 0, 96, 16, c, D) for c in range(0, FF, D)]
    return out


DIRECT = 0
T1, T2, T3 = 2, 2, 3


class Gather:
    def __init__(self, srcs, dsts, sems, local, ahead=2, lag=1):
        self.groups = gather_groups()
        self.srcs, self.dsts, self.sems = srcs, dsts, sems
        self.ahead, self.lag = ahead, lag
        clip, frame = lax.axis_index("clip"), lax.axis_index("frame")
        self.z, self.y, self.x, self.c = clip // 2, clip % 2, frame // 2, frame % 2
        z, y, x, c = self.z, self.y, self.x, self.c
        self.zpeers = [self.dev(lax.rem(z + k, 4), y, x, c) for k in (1, 2, 3)]
        self.ypeer, self.xpeer, self.cpeer = self.dev(z, 1 - y, x, c), self.dev(z, y, 1 - x, c), self.dev(z, y, x, 1 - c)
        self.moved = {k: {} for k in ("z", "y0", "y", "x1", "x2", "c1", "c2")}
        self.step = 0
        self.local = local

    @staticmethod
    def dev(z, y, x, c):
        return {"clip": z * 2 + y, "frame": x * 2 + c}

    def peers(self):
        return self.zpeers + [self.ypeer, self.xpeer, self.cpeer]

    def direct(self, g):
        return g < DIRECT

    def two(self, g):
        return self.span(g, 3 * self.c, 3) if self.direct(g) else self.span(g, 3 * self.c + self.x, 2)

    def span(self, g, first, count):
        _, _, _, r0, rows, unit, c0, width = self.groups[g]
        return pl.multiple_of(r0 + unit * first, 16), unit * count, c0, width

    def src(self, g, span):
        key, name, lead = self.groups[g][:3]
        r = self.srcs[name] if lead is None else self.srcs[name].at[lead]
        return r.at[pl.ds(span[0], span[1]), pl.ds(span[2], span[3])]

    def dst(self, g, z, y, span):
        key, name, lead = self.groups[g][:3]
        cs = pl.ds(span[2], span[3])
        r = self.dsts[name] if lead is None else self.dsts[name].at[lead]
        per = 384 if name == "o" else 96
        return r.at[pl.ds(pl.multiple_of((z * 2 + y) * per + span[0], 16), span[1]), cs]

    def remote(self, kind, i, s, d, peer):
        return pltpu.make_async_remote_copy(
            src_ref=s,
            dst_ref=d,
            send_sem=self.sems[0].at[kind + i],
            recv_sem=self.sems[1].at[kind + i],
            device_id=peer,
            device_id_type=MESH,
        )

    def relay(self, g, kind, items, span, peer):
        return Many(
            [self.remote(22 * g + kind, i, self.dst(g, zz, yy, span), self.dst(g, zz, yy, span), peer) for i, (zz, yy) in items]
        )

    def start_z(self, g):
        two = self.two(g)
        self.moved["z"][g] = Many(
            [self.remote(22 * g, k, self.src(g, two), self.dst(g, self.z, self.y, two), p) for k, p in enumerate(self.zpeers)]
        )
        self.moved["y0"][g] = Many([self.remote(22 * g, 3, self.src(g, two), self.dst(g, self.z, self.y, two), self.ypeer)])

    def begin(self):
        for g in range(self.ahead):
            self.start_z(g)

    def others(self, first):
        return [(q, lax.rem(self.z + q, 4)) for q in range(first, 4)]

    def tick(self):
        s, lag, ng, m, y = self.step, self.lag, len(self.groups), self.moved, self.y
        if s >= ng + 3 * lag:
            return False
        self.step += 1
        if s == 0:
            for cp in self.local:
                cp.wait()
        one, half = (3 * self.c + 2 * self.x, 1), (3 * self.c, 3)
        if s < ng:
            m["z"][s].wait_recv()
            if s + self.ahead < ng:
                self.start_z(s + self.ahead)
            m["y"][s] = self.relay(s, 4, [(q - 1, (zz, y)) for q, zz in self.others(1)], self.two(s), self.ypeer)
            if not self.direct(s):
                m["x1"][s] = self.relay(s, 7, [(q - 1, (zz, y)) for q, zz in self.others(1)], self.span(s, *one), self.xpeer)
        g = s - lag
        if 0 <= g < ng:
            m["y0"][g].wait_recv()
            m["y"][g].wait_recv()
            if not self.direct(g):
                m["x2"][g] = self.relay(g, 10, [(q, (zz, 1 - y)) for q, zz in self.others(0)], self.span(g, *one), self.xpeer)
                m["x1"][g].wait_recv()
            m["c1"][g] = self.relay(g, 14, [(q - 1, (zz, y)) for q, zz in self.others(1)], self.span(g, *half), self.cpeer)
        g = s - 2 * lag
        if 0 <= g < ng:
            if not self.direct(g):
                m["x2"][g].wait_recv()
            m["c2"][g] = self.relay(g, 17, [(q, (zz, 1 - y)) for q, zz in self.others(0)], self.span(g, *half), self.cpeer)
        g = s - 3 * lag
        if 0 <= g < ng:
            m["c1"][g].wait_recv()
            m["c2"][g].wait_recv()
        return True

    def need(self, key):
        last = max(i for i, g in enumerate(self.groups) if g[0] == key)
        while self.step <= last + 3 * self.lag:
            self.tick()

    def finish(self):
        while self.tick():
            pass
        for kind in self.moved.values():
            for cps in kind.values():
                cps.wait_send()


PIECES = [(i, 1) for i in range(6)] + [(6, 4), (10, 3), (13, 3)] + [(16 + i, 1) for i in range(4)] + [(20, 4)]


def piece_slots():
    for first, count in PIECES:
        for i in range(8 * count):
            yield first + i // 8, i % 8, i // count, first + i % count


def placement(part):
    row = iota((256, 1), 0)
    lane = row & 127
    return onehot(jnp.where(lane < 96, (2 * part + (row >> 7)) * 96 + lane, -1), D)


def place(rows):
    total = dg(rows(0), placement(0), 1, 0)
    for part in range(1, 4):
        total = total + dg(rows(part), placement(part), 1, 0)
    return total


def pick_rows(index):
    return jnp.where(iota((256, 128), 1) == index[...], 1.0, 0.0).astype(bf16)


BATCHES = ([3, 4, 5, 6, 7, 8, 9, 13, 14, 15, 18, 19, 20, 21, 22, 23], [0, 1, 2, 10, 11, 12, 16, 17])
PLACES = {p: i for i, p in enumerate(BATCHES[0] + BATCHES[1])}


class Reduce:
    def __init__(self, batch, blocks, work, received, result, nidx, sems):
        self.batch, self.blocks, self.work = batch, blocks, work
        self.received, self.result, self.nidx, self.sems = received, result, nidx, sems
        clip, frame = lax.axis_index("clip"), lax.axis_index("frame")
        self.clip, self.frame, self.x, self.c = clip, frame, frame // 2, frame % 2
        self.xpeer = {"clip": clip, "frame": (1 - self.x) * 2 + self.c}
        self.cpeer = {"clip": clip, "frame": self.x * 2 + 1 - self.c}
        self.width = len(BATCHES[batch]) * 32
        self.count = 0
        self.sent = []

    def lanes(self, quarter):
        return pl.ds(pl.multiple_of(2048 * self.batch + self.width * quarter, 128), self.width)

    def send(self, src, dst, peer):
        i = 16 * self.batch + self.count
        self.count += 1
        cp = pltpu.make_async_remote_copy(
            src_ref=src, dst_ref=dst, send_sem=self.sems.at[0, i], recv_sem=self.sems.at[1, i], device_id=peer, device_id_type=MESH
        )
        cp.start()
        self.sent.append(cp)
        return cp

    def add(self, first_row, quarter):
        ls = self.lanes(quarter)
        total = self.work[pl.ds(0, 256), ls].astype(f32) + self.work[pl.ds(first_row, 256), ls].astype(f32)
        self.work[pl.ds(0, 256), ls] = total.astype(bf16)

    def split(self):
        pieces = BATCHES[self.batch]
        for part in range(4):
            rows = self.blocks[pl.ds(512 * self.batch, 32 * len(pieces)), :]
            parts = dg(rows, placement(part), 1, 1).astype(bf16)
            for block, slot, owner, piece in piece_slots():
                if block in pieces and slot // 2 == part:
                    i = pieces.index(block)
                    tile = parts[32 * i : 32 * i + 32, 128 * (slot % 2) : 128 * (slot % 2) + 128]
                    self.work[pl.ds(32 * owner, 32), pl.ds(128 * PLACES[piece], 128)] = tile

    def over_cores(self):
        self.core = []
        for xx in range(2):
            ls = self.lanes(2 * xx + 1 - self.c)
            self.core.append(self.send(self.work.at[pl.ds(0, 256), ls], self.work.at[pl.ds(256, 256), ls], self.cpeer))

    def over_x(self):
        for xx in range(2):
            self.core[xx].wait_recv()
        for xx in range(2):
            self.add(256, 2 * xx + self.c)
        ls = self.lanes(2 * (1 - self.x) + self.c)
        self.across = self.send(self.work.at[pl.ds(0, 256), ls], self.work.at[pl.ds(512, 256), ls], self.xpeer)

    def to_owners(self):
        self.across.wait_recv()
        self.add(512, self.frame)
        ls = self.lanes(self.frame)
        self.here = pl.ds(512 * self.batch, self.width)
        mine = pl.ds(pl.multiple_of(32 * self.clip, 32), 32)
        self.received[mine, self.here] = self.work[mine, ls]
        self.owned = []
        for k in range(1, 8):
            j = lax.rem(self.clip + k, 8)
            rows = pl.ds(pl.multiple_of(32 * j, 32), 32)
            self.owned.append(
                self.send(self.work.at[rows, ls], self.received.at[mine, self.here], {"clip": j, "frame": self.frame})
            )

    def by_adapter(self):
        for cp in self.owned:
            cp.wait_recv()
        ls = self.lanes(self.frame)
        self.result[:, ls] = dg(pick_rows(self.nidx), self.received[:, self.here], 0, 0).astype(bf16)
        same = self.result.at[:, ls]
        self.back = [self.send(same, same, p) for p in (self.xpeer, self.cpeer)]

    def spread(self):
        self.back[0].wait_recv()
        same = self.result.at[:, self.lanes(2 * (1 - self.x) + self.c)]
        self.last = self.send(same, same, self.cpeer)

    def finish(self):
        self.back[1].wait_recv()
        self.last.wait_recv()
        for cp in self.sent:
            cp.wait_send()


def layer_kernel(
    gathers, hidx, x_ref, g_ref, hq, hp, hi, ho, had, hnm,
    out, ig, grads, spill,
    wq, wp, wi, wo, ad, nm, nbuf, nidx, received, rcv_a, rcv_b, big, x1, x2, tmp, o2, qkv2, a0, a1, us,
    wsem, ssem, rsem, psem, gssem, grsem, nsem, asem, bsem,
):
    buf_g, buf_d = big.at[0], big.at[1]

    clip = lax.axis_index("clip")
    me = lax.axis_index("frame")
    nf = 4
    peers = [lax.rem(me + k, nf) for k in range(1, nf)]

    fetch = [pltpu.make_async_copy(s, d, wsem.at[10 + i]) for i, (s, d) in enumerate(((x_ref, ig), (g_ref, out)))]
    for cp in fetch:
        cp.start()
    barrier = pltpu.get_barrier_semaphore()
    groups_of = [{"clip": clip, "frame": d} for d in peers]
    loads = {}
    if gathers:
        own = pl.ds(pl.multiple_of(clip * 96, 16), 96)
        local = [
            (hq.at[0], wq.at[0, own]), (hq.at[1], wq.at[1, own]), (hp.at[0], wp.at[0, own]), (hp.at[1], wp.at[1, own]),
            (hp.at[2], wp.at[2, own]), (hi, wi.at[own]), (ho, wo.at[pl.ds(pl.multiple_of(clip * 384, 16), 384)]),
            (had.at[:, cols(me * D, D)], big.at[0, pl.ds(256, 128), pl.ds(D, D)]), (hnm, nbuf.at[pl.ds(pl.multiple_of(clip * 16, 16), 16)]),
            (hidx, nidx.at[pl.ds(pl.multiple_of(clip * 32, 32), 32)]),
        ]
        local = [pltpu.make_async_copy(s, d, wsem.at[i]) for i, (s, d) in enumerate(local)]
        for cp in local:
            cp.start()
        net = Gather(
            {"q": hq, "p": hp, "i": hi, "o": ho},
            {"q": wq, "p": wp, "i": wi, "o": wo},
            (gssem, grsem),
            local[:7],
        )
        owners = [{"clip": lax.rem(clip + k, 8), "frame": me} for k in range(1, 8)]
        greet = groups_of + owners
    else:
        net = None
        for key, src, dst in (
            ("q0", hq.at[0], wq.at[0]), ("p0", hp.at[0], wp.at[0]), ("p1", hp.at[1], wp.at[1]), ("q1", hq.at[1], wq.at[1]),
            ("p2", hp.at[2], wp.at[2]), ("o", ho, wo), ("i", hi, wi), ("ad", had, ad), ("nm", hnm, nm),
        ):
            loads[key] = pltpu.make_async_copy(src, dst, wsem.at[len(loads)])
            loads[key].start()
        greet = groups_of
    for p in greet:
        pl.semaphore_signal(barrier, inc=1, device_id=p, device_id_type=MESH)
    pl.semaphore_wait(barrier, len(greet))

    def need(key, c=""):
        if net is not None:
            net.need(f"{key}{c}")
        elif not c:
            loads[key].wait()

    def need_tiles(key):
        def between(c):
            need(key, c)

        return between

    def tick():
        if net is not None:
            net.tick()

    if gathers:

        def to(peer, src, dst, sems, i):
            cp = pltpu.make_async_remote_copy(
                src_ref=src, dst_ref=dst, send_sem=sems.at[0, i], recv_sem=sems.at[1, i], device_id=peer, device_id_type=MESH
            )
            cp.start()
            return cp

        rows16 = pl.ds(pl.multiple_of(clip * 16, 16), 16)
        rows32 = pl.ds(pl.multiple_of(clip * 32, 32), 32)
        small = [to(p, hidx, nidx.at[rows32], nsem, k) for k, p in enumerate(owners)]
        small += [to(p, hnm, nbuf.at[rows16], nsem, 7 + k) for k, p in enumerate(owners)]
        net.begin()

    def exchange(step, src, index, rcv):
        sent = []
        for k, d in enumerate(peers):
            slot = pl.ds(k * GR, GR)
            o2[slot, :] = dg(onehot(index(d), R), src.get(), 1, 0).astype(bf16)
            cp = pltpu.make_async_remote_copy(
                src_ref=o2.at[slot],
                dst_ref=rcv.at[pl.ds(pl.multiple_of(me * GR, 16), GR)],
                send_sem=ssem.at[step, k],
                recv_sem=rsem.at[step, k],
                device_id={"clip": clip, "frame": d},
                device_id_type=MESH,
            )
            cp.start()
            sent.append(cp)
        rcv[pl.ds(pl.multiple_of(me * GR, 16), GR), :] = dg(onehot(index(me), R), src.get(), 1, 0).astype(bf16)

        def finish():
            for cp in sent:
                cp.wait_recv()
            for cp in sent:
                cp.wait_send()

        return finish

    def gain(k):
        return nm[k : k + 1, :]

    def norm(k, read, put):
        def body(rows):
            hat, _ = norm_rows(read(rows))
            put(rows, (hat * gain(k) + gain(3 + k)).astype(bf16))

        chunks(208, body)

    def rank(h, at, mask, m):
        us[:, pl.ds(32 * m, 32)] = jnp.where(mask, dg(h.get(), ad[:, pl.ds(at, h.width)], 1, 1), 0.0).astype(bf16)

    def forward(m, h, w, width, tile, mask, emit, between=None):
        rank(h, DOWN[m], mask, m)

        def body(c):
            acc = dg(h.get(), w[:, cols(c, tile)], 1, 0)
            acc = acc + dg(us[:, pl.ds(32 * m, 32)], ad[:, cols(UP[m] + c, tile)], 1, 0)
            emit(c, acc)

        tiles(width, tile, body, between)

    def rank_back(m, dz, mask):
        du = jnp.where(mask, dg(dz.get(), ad[:, pl.ds(UP[m], dz.width)], 1, 1), 0.0).astype(bf16)
        us[:, pl.ds(224, 32)] = du

    def backward(m, dz, w, width, tile, mask, emit, between=None):
        rank_back(m, dz, mask)
        backward_rows(m, dz, w, width, tile, emit, between)

    def backward_rows(m, dz, w, width, tile, emit, between=None):

        def body(c):
            acc = dg(dz.get(), w[cols(c, tile), :], 1, 1)
            acc = acc + dg(us[:, pl.ds(224, 32)], ad[:, cols(DOWN[m] + c, tile)], 1, 0)
            emit(c, acc)

        tiles(width, tile, body, between)

    def adapter_grads(m, h, dz):
        for at, side, rows in ((DOWN[m], 224, h), (UP[m], 32 * m, dz)):
            val = dg(us[:, pl.ds(side, 32)], rows.get(), 0, 0).astype(bf16)
            for k in range(rows.width // D):
                wo[pl.ds(32 * PLACES[at // D + k], 32), :] = val[:, k * D : k * D + D]

    p_a0, p_a1 = Part(a0, 0, D), Part(a1, 0, D)
    qkv1, h1 = Part(buf_g, 0, QKV), Part(buf_g, QKV, D)
    xt, o1, m1, spare = (Part(buf_d, D * i, D) for i in range(4))
    p_o2, p_qkv2, p_g, p_d = Part(o2, 0, D), Part(qkv2, 0, QKV), Part(buf_g, 0, FF), Part(buf_d, 0, FF)

    if gathers:
        def quarter_at(frame):
            if isinstance(frame, int):
                return 256 * (frame % 3), D * (frame // 3)
            return pl.multiple_of(256 * lax.rem(frame, 3), 32), pl.multiple_of(D * (frame // 3), 128)

        def quarter(frame, row, rows):
            r0, c0 = quarter_at(frame)
            return pl.ds(pl.multiple_of(r0 + row, 32), rows), pl.ds(c0, D)

        for cp in local[7:]:
            cp.wait()
        for cp in small[:7]:
            cp.wait_recv()
        side = pl.ds(D, D)
        big[0, pl.ds(384, 256), side] = dg(pick_rows(nidx), big[0, pl.ds(256, 128), side], 1, 0).astype(bf16)
        picked = []
        landing = quarter(me, 32 * clip, 32)
        for k, p in enumerate(owners):
            rows = pl.ds(pl.multiple_of(384 + 32 * p["clip"], 32), 32)
            picked.append(to(p, big.at[0, rows, side], big.at[(0,) + landing], asem, k))
        big[(0,) + landing] = big[0, pl.ds(pl.multiple_of(384 + 32 * clip, 32), 32), side]

    for i, (src, dst) in enumerate(((ig, a0), (out, a1))):
        fetch[i].wait()
        for g in range(4):
            dst[pl.ds(GR * g + 192, 16), :] = jnp.zeros((16, D), bf16)
            dst[pl.ds(GR * g, NP), :] = src[g // 2, g % 2]
        if dst is a0:
            arrive = exchange(0, p_a0, to_message, rcv_a)

    mask_t = clip_mask(392)
    mask_s = clip_mask(416)
    if gathers:
        tick()
        for cp in picked:
            cp.wait_recv()

        def block_of(frame):
            return big.at[(0,) + quarter(frame, 0, 256)]

        x, c = me // 2, me % 2
        xpeer, cpeer = {"clip": clip, "frame": (1 - x) * 2 + c}, {"clip": clip, "frame": x * 2 + 1 - c}
        picked.append(to(xpeer, block_of(me), block_of(me), asem, 7))
        picked.append(to(cpeer, block_of(me), block_of(me), asem, 8))
        for cp in small[7:]:
            cp.wait_recv()
        for j in range(8):
            qkv2[pl.ds(0, 16), pl.ds(j * 128, 128)] = nbuf[pl.ds(16 * j, 16), :]
        nm[...] = place(lambda part: qkv2[pl.ds(0, 16), pl.ds(256 * part, 256)])
    else:
        need("ad")
        need("nm")
    for _ in range(T1):
        tick()
    arrive()
    for i in range(4):
        xt.put(dg(onehot(to_patches(i), R), rcv_a[...], 1, 0).astype(bf16), pl.ds(i * GR, GR))
    norm(0, lambda rows: xt.get(rows).astype(f32), lambda rows, v: h1.put(v, rows))
    if gathers:
        picked[7].wait_recv()
        far = (1 - x) * 2 + c
        picked.append(to(cpeer, block_of(far), block_of(far), asem, 9))
        for _ in range(T2):
            tick()
        picked[8].wait_recv()
        picked[9].wait_recv()
        for cp in picked:
            cp.wait_send()
        for block, slot, owner, piece in piece_slots():
            r0, c0 = quarter_at(piece // 6)
            part = big[0, pl.ds(r0 + 32 * owner, 32), pl.ds(c0 + piece % 6 * 128, 128)]
            qkv2[pl.ds(block * 32, 32), pl.ds(slot * 128, 128)] = part
        joined = place(lambda part: qkv2[pl.ds(0, 768), pl.ds(256 * part, 256)]).astype(bf16)
        for block in range(24):
            ad[:, pl.ds(block * D, D)] = joined[block * 32 : block * 32 + 32]
    tick()
    forward(0, h1, wq.at[0], QKV, 768, mask_t, lambda c, acc: qkv1.put(acc.astype(bf16), off=c), need_tiles("q0"))
    tick()
    temporal_loop(lambda rows, n, bias, pairs: attend(qkv1, rows, n, bias, o1, pairs))
    tick()
    need("p0")
    forward(1, o1, wp.at[0], D, 384, mask_t, lambda c, acc: m1.put(acc.astype(bf16), off=c))
    tick()
    need("p1")
    forward(2, m1, wp.at[1], D, 384, mask_t, lambda c, acc: spare.put(acc.astype(bf16), off=c))
    tick()
    arrive = exchange(1, spare, from_patches, rcv_b)
    tick()
    saves = [pltpu.make_async_copy(b, spill.at[i], psem.at[i]) for i, b in enumerate((buf_g, buf_d))]
    for cp in saves:
        cp.start()
    for cp in saves:
        cp.wait()
    for _ in range(T3):
        tick()
    arrive()

    for g in range(4):
        rows = pl.ds(g * GR, GR)
        tb = dg(onehot(to_frames(g), R), rcv_b[...], 1, 0)
        x1[rows, :] = a0[rows, :].astype(f32) + tb
    tick()
    norm(1, lambda rows: x1[rows, :], lambda rows, v: p_o2.put(v, rows))
    tick()
    forward(3, p_o2, wq.at[1], QKV, 768, mask_s, lambda c, acc: p_qkv2.put(acc.astype(bf16), off=c), need_tiles("q1"))
    tick()
    spatial_loop(3, lambda rows, n, bias, pairs: attend(p_qkv2, rows, n, bias, p_o2, pairs))
    tick()
    need("p2")

    def add_spatial(c, acc):
        x2[:, cols(c, 384)] = x1[:, cols(c, 384)] + acc

    forward(4, p_o2, wp.at[2], D, 384, mask_s, add_spatial)
    tick()

    need("o")
    backward(6, p_a1, wo, FF, 768, mask_s, lambda c, acc: p_d.put(acc.astype(bf16), off=c), lambda c: tick())
    us[:, pl.ds(256, 32)] = us[:, pl.ds(224, 32)]

    norm(2, lambda rows: x2[rows, :], lambda rows, v: p_a0.put(v, rows))

    def activate(c, acc):
        tmp_w = acc.shape[1]
        tmp[:, pl.ds(0, tmp_w)] = acc
        @pl.loop(0, R // 32)
        def _(i):
            rows = pl.ds(pl.multiple_of(i * 32, 32), 32)
            v = tmp[rows, pl.ds(0, tmp_w)]
            phi, e = normal_parts(v)
            slope = phi + v * e * 0.3989422804014327
            p_g.put((v * phi).astype(bf16), rows, c)
            p_d.put((p_d.get(rows, c, tmp_w).astype(f32) * slope).astype(bf16), rows, c)

    forward(5, p_a0, wi, FF, 768, mask_s, activate, need_tiles("i"))

    def emit_out(c, acc):
        y = (x2[:, cols(c, 384)] + acc).astype(bf16)
        for g in range(4):
            out[g // 2, g % 2, :, cols(c, 384)] = y[g * GR : g * GR + NP]

    forward(6, p_g, wo, D, 384, mask_s, emit_out)
    if gathers:
        net.finish()
        for cp in small:
            cp.wait_send()

    us[:, pl.ds(224, 32)] = us[:, pl.ds(256, 32)]
    adapter_grads(6, p_g, p_a1)

    def emit_tmp(c, acc):
        tmp[:, cols(c, 384)] = acc

    backward(5, p_d, wi, D, 384, mask_s, emit_tmp)
    adapter_grads(5, p_a0, p_d)
    loads_back = [pltpu.make_async_copy(spill.at[i], b, psem.at[i]) for i, b in enumerate((buf_g, buf_d))]
    for cp in loads_back:
        cp.start()

    def step_two(rows):
        dx = a1[rows, :].astype(f32) + norm_back_rows(x2[rows, :], gain(2), tmp[rows, :])
        x2[rows, :] = dx
        a0[rows, :] = dx.astype(bf16)

    chunks(208, step_two)

    backward(4, p_a0, wp.at[2], D, 384, mask_s, lambda c, acc: p_a1.put(acc.astype(bf16), off=c))
    adapter_grads(4, p_o2, p_a0)
    spatial_loop(2, lambda rows, n, bias, pairs: attend_back(p_qkv2, rows, n, bias, p_a1, pairs, False))
    backward(3, p_qkv2, wq.at[1], D, 384, mask_s, emit_tmp)

    def step_one(rows):
        dx = x2[rows, :] + norm_back_rows(x1[rows, :], gain(1), tmp[rows, :])
        x2[rows, :] = dx
        a0[rows, :] = dx.astype(bf16)

    chunks(208, step_one)
    arrive = exchange(2, p_a0, to_message, rcv_a)
    norm(1, lambda rows: x1[rows, :], lambda rows, v: p_a1.put(v, rows))
    adapter_grads(3, p_a1, p_qkv2)
    if gathers:
        first, second = (Reduce(i, wo, wi, received, grads, nidx, bsem) for i in range(2))
        first.split()
    for cp in loads_back:
        cp.wait()
    arrive()

    if gathers:
        first.over_cores()
    for i in range(4):
        p_a0.put(dg(onehot(to_patches(i), R), rcv_a[...], 1, 0).astype(bf16), pl.ds(i * GR, GR))
    backward(2, p_a0, wp.at[1], D, 384, mask_t, lambda c, acc: p_a1.put(acc.astype(bf16), off=c))
    adapter_grads(2, m1, p_a0)
    if gathers:
        first.over_x()
    backward(1, p_a1, wp.at[0], D, 384, mask_t, lambda c, acc: spare.put(acc.astype(bf16), off=c))
    adapter_grads(1, o1, p_a1)
    temporal_loop(lambda rows, n, bias, pairs: attend_back(qkv1, rows, n, bias, spare, pairs, True))
    if gathers:
        first.to_owners()
    rank_back(0, qkv1, mask_t)
    adapter_grads(0, h1, qkv1)
    if gathers:
        second.split()
        second.over_cores()
        first.by_adapter()
    backward_rows(0, qkv1, wq.at[0], D, 384, emit_tmp)
    if gathers:
        second.over_x()
        first.spread()

    def step_zero(rows):
        dx = norm_back_rows(xt.get(rows).astype(f32), gain(0), tmp[rows, :])
        a0[rows, :] = dx.astype(bf16)

    chunks(208, step_zero)
    if gathers:
        second.to_owners()
    arrive = exchange(3, p_a0, from_patches, rcv_b)
    if gathers:
        second.by_adapter()
        first.finish()
        second.spread()
    arrive()
    for g in range(4):
        dxt = dg(onehot(to_frames(g), R), rcv_b[...], 1, 0)
        total = x2[pl.ds(g * GR, GR), :] + dxt
        ig[g // 2, g % 2] = total.astype(bf16)[:NP]
    if gathers:
        second.finish()
    else:
        for block in range(24):
            grads[:, pl.ds(block * D, D)] = wo[pl.ds(32 * PLACES[block], 32), :]


def layer(gathers, index_rows, x, g, hq, hp, hi, ho, ad, nm):
    vm = pl.BlockSpec(memory_space=pltpu.VMEM)
    hbm = pl.BlockSpec(memory_space=pl.ANY)
    dma = pltpu.SemaphoreType.DMA
    rows = lambda w, t=bf16: pltpu.VMEM((R, w), t)
    ng = len(gather_groups()) if gathers else 1
    return pl.pallas_call(
        functools.partial(layer_kernel, gathers),
        out_shape=[
            jax.ShapeDtypeStruct(x.shape, bf16),
            jax.ShapeDtypeStruct(x.shape, bf16),
            jax.ShapeDtypeStruct((128, 24 * 128) if gathers else (32, ADW), bf16),
            jax.ShapeDtypeStruct((2, R, FF), bf16),
        ],
        in_specs=[hbm] * 9,
        out_specs=[vm] * 3 + [hbm],
        scratch_shapes=[
            pltpu.VMEM((2, D, QKV), bf16), pltpu.VMEM((3, D, D), bf16), pltpu.VMEM((D, FF), bf16), pltpu.VMEM((FF, D), bf16),
            pltpu.VMEM((32, ADW), bf16), pltpu.VMEM((16, D), f32), pltpu.VMEM((128, 128), bf16),
            pltpu.VMEM((256, 128), jnp.int32), pltpu.VMEM((256, D), bf16),
            rows(D), rows(D), pltpu.VMEM((2, R, FF), bf16), rows(D, f32), rows(D, f32), rows(D, f32),
            rows(D), rows(QKV), rows(D), rows(D), rows(384),
            dma((12,)), dma((4, 3)), dma((4, 3)), dma((2,)), dma((22 * ng,)), dma((22 * ng,)), dma((2, 14)), dma((2, 10)), dma((2, 32)),
        ],
        compiler_params=pltpu.CompilerParams(
            collective_id=1, has_side_effects=True, vmem_limit_bytes=64 * 2**20 - 2**17
        ),
        name="layer",
    )(index_rows, x, g, hq, hp, hi, ho, ad, nm)


def piece_widths(w):
    return [w] * 6 + [4 * w] + [3 * w] * 2 + [w] * 4 + [4 * w]


def pack_adapters(adapt_down, adapt_down_wide, adapt_up_qkv, adapt_up, adapt_up_wide):
    adapters = adapt_down_wide.shape[0]

    def flat(v):
        return v.reshape(adapters, RANK, -1)

    return jnp.concatenate(
        [
            flat(adapt_down.transpose(1, 3, 0, 2)),
            flat(adapt_down_wide.transpose(0, 2, 1)),
            flat(adapt_up_qkv.transpose(1, 2, 0, 3)),
            flat(adapt_up.transpose(1, 2, 0, 3)),
            flat(adapt_up_wide),
        ],
        axis=-1,
    )


def join_pieces(parts, w):
    joined, at = [], 0
    for width in piece_widths(w):
        piece = parts[:, :, at : at + width]
        joined.append(piece.transpose(1, 0, 2).reshape(parts.shape[1], -1))
        at += width
    return jnp.concatenate(joined, axis=-1)


def split_pieces(rows, w, owners):
    parts, at = [], 0
    for width in piece_widths(w):
        piece = rows[:, at : at + width * owners]
        parts.append(piece.reshape(rows.shape[0], owners, width).transpose(1, 0, 2))
        at += width * owners
    return jnp.concatenate(parts, axis=-1)


def per_device(
    inputs,
    out_grad,
    adapter_index,
    norm_gain,
    norm_bias,
    qkv_weight,
    proj_weight,
    mlp_in,
    mlp_out,
    adapt_down,
    adapt_down_wide,
    adapt_up_qkv,
    adapt_up,
    adapt_up_wide,
):
    owners = lax.axis_size("clip")
    adapters = adapt_down_wide.shape[0]
    clips = inputs.shape[0]
    w = norm_gain.shape[1]
    packed = pack_adapters(adapt_down, adapt_down_wide, adapt_up_qkv, adapt_up, adapt_up_wide)
    norms = jnp.concatenate([norm_gain, norm_bias], axis=0)
    if owners == 8:
        index_rows = adapter_index[:, None] * RANK + jnp.arange(RANK, dtype=jnp.int32)[None, :]
        index_rows = jnp.broadcast_to(index_rows.reshape(clips * RANK, 1), (clips * RANK, 128))
        pieces = packed.reshape(adapters * RANK, 24, w)
        table = jnp.pad(pieces, ((0, 0), (0, 0), (0, 128 - w))).reshape(adapters * RANK, 24 * 128)
        own_norms = jnp.pad(norms, ((0, 10), (0, 128 - w)))
        output, input_grad, grads, _ = layer(
            True, index_rows, inputs, out_grad, qkv_weight, proj_weight, mlp_in, mlp_out, table, own_norms
        )
        grads = grads.reshape(adapters, RANK, 24, 128)[..., :w].astype(f32)
        summed = jnp.concatenate([grads[:, :, PLACES[p]] for p in range(24)], axis=-1)
    else:
        full_qkv = lax.all_gather(qkv_weight, "clip", axis=1, tiled=True)
        full_proj = lax.all_gather(proj_weight, "clip", axis=1, tiled=True)
        full_in = lax.all_gather(mlp_in, "clip", axis=0, tiled=True)
        full_out = lax.all_gather(mlp_out, "clip", axis=0, tiled=True)
        table = lax.all_gather(packed, "clip", axis=0)
        all_norms = lax.all_gather(norms, "clip", axis=0)
        nm = jnp.pad(all_norms.transpose(1, 0, 2).reshape(6, D).astype(f32), ((0, 10), (0, 0)))
        chosen = jnp.take(table, adapter_index, axis=1).reshape(owners, clips * RANK, 24 * w)
        ad = join_pieces(chosen, w)
        output, input_grad, grads, _ = layer(
            False, adapter_index, inputs, out_grad, full_qkv, full_proj, full_in, full_out, ad, nm
        )
        parts = split_pieces(grads, w, owners)
        parts = lax.all_to_all(parts, "clip", split_axis=0, concat_axis=0, tiled=True)
        every = lax.all_gather(adapter_index, "clip", axis=0, tiled=True)
        pick = (every[:, None] == jnp.arange(adapters, dtype=jnp.int32)[None, :]).astype(bf16)
        summed = jnp.einsum(
            "ca,crm->arm", pick, parts.reshape(owners * clips, RANK, 24 * w), preferred_element_type=f32
        )
        summed = lax.psum(summed.astype(bf16), "frame").astype(f32)
    return (output, input_grad) + unpack_grads(summed, w)


def unpack_grads(summed, w):
    adapters = summed.shape[0]
    down = summed[:, :, : 6 * w].reshape(adapters, RANK, 6, w).transpose(2, 0, 3, 1)
    down_wide = summed[:, :, 6 * w : 10 * w].transpose(0, 2, 1)
    up_qkv = summed[:, :, 10 * w : 16 * w].reshape(adapters, RANK, 2, 3 * w).transpose(2, 0, 1, 3)
    up = summed[:, :, 16 * w : 20 * w].reshape(adapters, RANK, 4, w).transpose(2, 0, 1, 3)
    return (down, down_wide, up_qkv, up, summed[:, :, 20 * w :])


def solution(mesh):
    return jax.shard_map(
        per_device,
        mesh=mesh,
        in_specs=(
            P("clip", "frame", None, None),
            P("clip", "frame", None, None),
            P("clip"),
            P(None, "clip"),
            P(None, "clip"),
            P(None, "clip", None),
            P(None, "clip", None),
            P("clip", None),
            P("clip", None),
            P(None, None, "clip", None),
            P(None, "clip", None),
            P(None, None, None, "clip"),
            P(None, None, None, "clip"),
            P(None, None, "clip"),
        ),
        out_specs=(
            P("clip", "frame", None, None),
            P("clip", "frame", None, None),
            P(None, None, "clip", None),
            P(None, "clip", None),
            P(None, None, None, "clip"),
            P(None, None, None, "clip"),
            P(None, None, "clip"),
        ),
        check_vma=False,
    )
```

```python
import functools
import jax
import jax.numpy as jnp
from jax import lax
from jax.experimental import pallas as pl
from jax.experimental.pallas import tpu as pltpu
from jax.sharding import PartitionSpec as P

EPS = 1e-06
MESH = pl.DeviceIdType.MESH
f32 = jnp.float32
bf16 = jnp.bfloat16
D, FF, QKV, RANK = 768, 3072, 2304, 16
NP, GR, R = 196, 208, 832
DOWN = (0, 768, 1536, 2304, 3072, 3840, 4608)
UP = (7680, 12288, 13056, 9984, 13824, 15360, 14592)
ADW = 18432
BIG = 1e30


def dg(a, b, ca, cb):
    return lax.dot_general(a, b, (((ca,), (cb,)), ((), ())), preferred_element_type=f32)


def iota(shape, d):
    return lax.broadcasted_iota(jnp.int32, shape, d)


def cols(off, w):
    return pl.ds(off if isinstance(off, int) else pl.multiple_of(off, 128), w)


def normal_parts(v):
    e = jnp.exp(-0.5 * v * v)
    t = 1.0 / (1.0 + 0.2316419 * jnp.abs(v))
    poly = t * (
        0.127414796
        + t * (-0.142248368 + t * (0.7107068705 + t * (-0.7265760135 + t * 0.5307027145)))
    )
    tail = poly * e
    return jnp.where(v >= 0, 1.0 - tail, tail), e


def onehot(col, width):
    return jnp.where(iota((col.shape[0], width), 1) == col, 1.0, 0.0).astype(bf16)


def message_rows():
    m = iota((GR, 1), 0)
    c = jnp.where(m >= 98, 1, 0)
    rest = m - 98 * c
    f = jnp.where(rest >= 49, 1, 0)
    return m < 196, c, f, rest - 49 * f


def to_message(owner):
    ok, c, f, q = message_rows()
    return jnp.where(ok, (2 * c + f) * GR + 49 * owner + q, -1)


def from_patches(owner):
    ok, c, f, q = message_rows()
    return jnp.where(ok, 392 * c + 8 * q + 2 * owner + f, -1)


def to_patches(chunk):
    t = iota((GR, 1), 0) + chunk * GR
    c = jnp.where(t >= 392, 1, 0)
    u = t - 392 * c
    q, fr = u >> 3, u & 7
    return jnp.where(t < 784, (fr >> 1) * GR + c * 98 + (fr & 1) * 49 + q, -1)


def to_frames(g):
    p = iota((GR, 1), 0)
    d = jnp.where(p >= 49, 1, 0) + jnp.where(p >= 98, 1, 0) + jnp.where(p >= 147, 1, 0)
    return jnp.where(p < NP, d * GR + (g // 2) * 98 + (g % 2) * 49 + p - 49 * d, -1)


def clip_mask(first):
    return (iota((R, 32), 0) >= first) == (iota((R, 32), 1) >= 16)


class Part:
    def __init__(self, ref, c0, width):
        self.ref, self.c0, self.width = ref, c0, width

    def get(self, rows=slice(None), off=0, width=None):
        return self.ref[rows, cols(self.c0 + off, self.width if width is None else width)]

    def put(self, val, rows=slice(None), off=0):
        self.ref[rows, cols(self.c0 + off, val.shape[1])] = val


def chunks(size, body):
    @pl.loop(0, R // size)
    def _(i):
        body(pl.ds(pl.multiple_of(i * size, size), size))


def tiles(total, tile, body, between):
    if total == tile:
        body(0)
    elif between is None:

        @pl.loop(0, total // tile)
        def _(i):
            body(i * tile)

    else:
        for c in range(0, total, tile):
            between(c)
            body(c)


def norm_rows(v):
    mean = jnp.mean(v, axis=-1, keepdims=True)
    cen = v - mean
    rstd = lax.rsqrt(jnp.mean(cen * cen, axis=-1, keepdims=True) + EPS)
    return cen * rstd, rstd


def norm_back_rows(v, gain, dh):
    hat, rstd = norm_rows(v)
    g = dh * gain
    m1 = jnp.mean(g, axis=-1, keepdims=True)
    m2 = jnp.mean(g * hat, axis=-1, keepdims=True)
    return rstd * (g - m1 - hat * m2)


def split_heads(v):
    first = iota(v.shape, 1) < 64
    zero = jnp.zeros(v.shape, bf16)
    return jnp.concatenate([jnp.where(first, v, zero), jnp.where(first, zero, v)], axis=0)


def join_heads(v):
    n = v.shape[0] // 2
    return jnp.where(iota((n, 128), 1) < 64, v[:n], v[n:])


def attend(qkv, rows, n, bias, out, pairs):
    q = [split_heads(qkv.get(rows, o, 128) * bf16(0.125)) for o in pairs]
    s = [dg(a, qkv.get(rows, D + o, 128), 1, 1) + bias for a, o in zip(q, pairs)]
    p = [jnp.exp(a - jnp.max(a, axis=1, keepdims=True)).astype(bf16) for a in s]
    ones = jnp.ones((n, 128), bf16)
    for a, o in zip(p, pairs):
        r = dg(a, jnp.concatenate([qkv.get(rows, 2 * D + o, 128), ones], axis=1), 1, 0)
        out.put(join_heads(r[:, :128] / r[:, 128:]).astype(bf16), rows, o)


def attend_back(qkv, rows, n, bias, dout, pairs, sums_by_product):
    q = [split_heads(qkv.get(rows, o, 128) * bf16(0.125)) for o in pairs]
    k = [qkv.get(rows, D + o, 128) for o in pairs]
    g = [split_heads(dout.get(rows, o, 128)) for o in pairs]
    s = [dg(a, b, 1, 1) + bias for a, b in zip(q, k)]
    dp = [dg(a, qkv.get(rows, 2 * D + o, 128), 1, 1) for a, o in zip(g, pairs)]
    p = [jnp.exp(a - jnp.max(a, axis=1, keepdims=True)) for a in s]
    if sums_by_product:
        ones = jnp.ones((n, n), bf16)
        p = [a * (1.0 / dg(a.astype(bf16), ones, 1, 0)) for a in p]
    else:
        p = [a * (1.0 / jnp.sum(a, axis=1, keepdims=True)) for a in p]
    ds = [(a * (b - jnp.sum(a * b, axis=1, keepdims=True))).astype(bf16) for a, b in zip(p, dp)]
    for i, o in enumerate(pairs):
        qkv.put((join_heads(dg(ds[i], k[i], 1, 0)) * 0.125).astype(bf16), rows, o)
        qkv.put(dg(ds[i], q[i], 0, 0).astype(bf16), rows, D + o)
        qkv.put(dg(p[i].astype(bf16), g[i], 0, 0).astype(bf16), rows, 2 * D + o)


def spatial_loop(count, body):
    bias = jnp.where(iota((1, GR), 1) < NP, 0.0, -BIG)
    steps = 6 // count

    @pl.loop(0, 4 * steps)
    def _(i):
        pairs = [((i % steps) * count + k) * 128 for k in range(count)]
        body(pl.ds(pl.multiple_of((i // steps) * GR, 16), GR), GR, bias, pairs)


def temporal_loop(body):
    pairs = range(0, D, 128)

    def bias(n):
        return jnp.where(((iota((2 * n, n), 0) & (n - 1)) >> 3) == (iota((2 * n, n), 1) >> 3), 0.0, -BIG)

    @pl.loop(0, 6)
    def _(i):
        body(pl.ds(pl.multiple_of(i * 128, 128), 128), 128, bias(128), pairs)

    body(pl.ds(768, 64), 64, bias(64), pairs)


class Many:
    def __init__(self, cps):
        self.cps = cps
        for cp in cps:
            cp.start()

    def wait_recv(self):
        for cp in self.cps:
            cp.wait_recv()

    def wait_send(self):
        for cp in self.cps:
            cp.wait_send()


def gather_groups():
    out = [(f"q0{c}", "q", 0, 0, 96, 16, c, D) for c in range(0, QKV, D)]
    out += [("p0", "p", 0, 0, 96, 16, 0, D), ("p1", "p", 1, 0, 96, 16, 0, D)]
    out += [(f"q1{c}", "q", 1, 0, 96, 16, c, D) for c in range(0, QKV, D)]
    out += [("p2", "p", 2, 0, 96, 16, 0, D)]
    out += [("o", "o", None, r, 96, 16, 0, D) for r in range(0, 384, 96)]
    out += [(f"i{c}", "i", None, 0, 96, 16, c, D) for c in range(0, FF, D)]
    return out


DIRECT = 0
T1, T2, T3 = 2, 2, 3


class Gather:
    def __init__(self, srcs, dsts, sems, local, ahead=2, lag=1):
        self.groups = gather_groups()
        self.srcs, self.dsts, self.sems = srcs, dsts, sems
        self.ahead, self.lag = ahead, lag
        clip, frame = lax.axis_index("clip"), lax.axis_index("frame")
        self.z, self.y, self.x, self.c = clip // 2, clip % 2, frame // 2, frame % 2
        z, y, x, c = self.z, self.y, self.x, self.c
        self.zpeers = [self.dev(lax.rem(z + k, 4), y, x, c) for k in (1, 2, 3)]
        self.ypeer, self.xpeer, self.cpeer = self.dev(z, 1 - y, x, c), self.dev(z, y, 1 - x, c), self.dev(z, y, x, 1 - c)
        self.moved = {k: {} for k in ("z", "y0", "y", "x1", "x2", "c1", "c2")}
        self.step = 0
        self.local = local

    @staticmethod
    def dev(z, y, x, c):
        return {"clip": z * 2 + y, "frame": x * 2 + c}

    def peers(self):
        return self.zpeers + [self.ypeer, self.xpeer, self.cpeer]

    def direct(self, g):
        return g < DIRECT

    def two(self, g):
        return self.span(g, 3 * self.c, 3) if self.direct(g) else self.span(g, 3 * self.c + self.x, 2)

    def span(self, g, first, count):
        _, _, _, r0, rows, unit, c0, width = self.groups[g]
        return pl.multiple_of(r0 + unit * first, 16), unit * count, c0, width

    def src(self, g, span):
        key, name, lead = self.groups[g][:3]
        r = self.srcs[name] if lead is None else self.srcs[name].at[lead]
        return r.at[pl.ds(span[0], span[1]), pl.ds(span[2], span[3])]

    def dst(self, g, z, y, span):
        key, name, lead = self.groups[g][:3]
        cs = pl.ds(span[2], span[3])
        r = self.dsts[name] if lead is None else self.dsts[name].at[lead]
        per = 384 if name == "o" else 96
        return r.at[pl.ds(pl.multiple_of((z * 2 + y) * per + span[0], 16), span[1]), cs]

    def remote(self, kind, i, s, d, peer):
        return pltpu.make_async_remote_copy(
            src_ref=s,
            dst_ref=d,
            send_sem=self.sems[0].at[kind + i],
            recv_sem=self.sems[1].at[kind + i],
            device_id=peer,
            device_id_type=MESH,
        )

    def relay(self, g, kind, items, span, peer):
        return Many(
            [self.remote(22 * g + kind, i, self.dst(g, zz, yy, span), self.dst(g, zz, yy, span), peer) for i, (zz, yy) in items]
        )

    def start_z(self, g):
        two = self.two(g)
        self.moved["z"][g] = Many(
            [self.remote(22 * g, k, self.src(g, two), self.dst(g, self.z, self.y, two), p) for k, p in enumerate(self.zpeers)]
        )
        self.moved["y0"][g] = Many([self.remote(22 * g, 3, self.src(g, two), self.dst(g, self.z, self.y, two), self.ypeer)])

    def begin(self):
        for g in range(self.ahead):
            self.start_z(g)

    def others(self, first):
        return [(q, lax.rem(self.z + q, 4)) for q in range(first, 4)]

    def tick(self):
        s, lag, ng, m, y = self.step, self.lag, len(self.groups), self.moved, self.y
        if s >= ng + 3 * lag:
            return False
        self.step += 1
        if s == 0:
            for cp in self.local:
                cp.wait()
        one, half = (3 * self.c + 2 * self.x, 1), (3 * self.c, 3)
        if s < ng:
            m["z"][s].wait_recv()
            if s + self.ahead < ng:
                self.start_z(s + self.ahead)
            m["y"][s] = self.relay(s, 4, [(q - 1, (zz, y)) for q, zz in self.others(1)], self.two(s), self.ypeer)
            if not self.direct(s):
                m["x1"][s] = self.relay(s, 7, [(q - 1, (zz, y)) for q, zz in self.others(1)], self.span(s, *one), self.xpeer)
        g = s - lag
        if 0 <= g < ng:
            m["y0"][g].wait_recv()
            m["y"][g].wait_recv()
            if not self.direct(g):
                m["x2"][g] = self.relay(g, 10, [(q, (zz, 1 - y)) for q, zz in self.others(0)], self.span(g, *one), self.xpeer)
                m["x1"][g].wait_recv()
            m["c1"][g] = self.relay(g, 14, [(q - 1, (zz, y)) for q, zz in self.others(1)], self.span(g, *half), self.cpeer)
        g = s - 2 * lag
        if 0 <= g < ng:
            if not self.direct(g):
                m["x2"][g].wait_recv()
            m["c2"][g] = self.relay(g, 17, [(q, (zz, 1 - y)) for q, zz in self.others(0)], self.span(g, *half), self.cpeer)
        g = s - 3 * lag
        if 0 <= g < ng:
            m["c1"][g].wait_recv()
            m["c2"][g].wait_recv()
        return True

    def need(self, key):
        last = max(i for i, g in enumerate(self.groups) if g[0] == key)
        while self.step <= last + 3 * self.lag:
            self.tick()

    def finish(self):
        while self.tick():
            pass
        for kind in self.moved.values():
            for cps in kind.values():
                cps.wait_send()


PIECES = [(i, 1) for i in range(6)] + [(6, 4), (10, 3), (13, 3)] + [(16 + i, 1) for i in range(4)] + [(20, 4)]


def piece_slots():
    for first, count in PIECES:
        for i in range(8 * count):
            yield first + i // 8, i % 8, i // count, first + i % count


def placement(part):
    row = iota((256, 1), 0)
    lane = row & 127
    return onehot(jnp.where(lane < 96, (2 * part + (row >> 7)) * 96 + lane, -1), D)


def place(rows):
    total = dg(rows(0), placement(0), 1, 0)
    for part in range(1, 4):
        total = total + dg(rows(part), placement(part), 1, 0)
    return total


def pick_rows(index):
    return jnp.where(iota((256, 128), 1) == index[...], 1.0, 0.0).astype(bf16)


BATCHES = ([3, 4, 5, 6, 7, 8, 9, 13, 14, 15, 18, 19, 20, 21, 22, 23], [0, 1, 2, 10, 11, 12, 16, 17])
PLACES = {p: i for i, p in enumerate(BATCHES[0] + BATCHES[1])}


class Reduce:
    def __init__(self, batch, blocks, work, received, result, nidx, sems):
        self.batch, self.blocks, self.work = batch, blocks, work
        self.received, self.result, self.nidx, self.sems = received, result, nidx, sems
        clip, frame = lax.axis_index("clip"), lax.axis_index("frame")
        self.clip, self.frame, self.x, self.c = clip, frame, frame // 2, frame % 2
        self.xpeer = {"clip": clip, "frame": (1 - self.x) * 2 + self.c}
        self.cpeer = {"clip": clip, "frame": self.x * 2 + 1 - self.c}
        self.width = len(BATCHES[batch]) * 32
        self.count = 0
        self.sent = []

    def lanes(self, quarter):
        return pl.ds(pl.multiple_of(2048 * self.batch + self.width * quarter, 128), self.width)

    def send(self, src, dst, peer):
        i = 16 * self.batch + self.count
        self.count += 1
        cp = pltpu.make_async_remote_copy(
            src_ref=src, dst_ref=dst, send_sem=self.sems.at[0, i], recv_sem=self.sems.at[1, i], device_id=peer, device_id_type=MESH
        )
        cp.start()
        self.sent.append(cp)
        return cp

    def add(self, first_row, quarter):
        ls = self.lanes(quarter)
        total = self.work[pl.ds(0, 256), ls].astype(f32) + self.work[pl.ds(first_row, 256), ls].astype(f32)
        self.work[pl.ds(0, 256), ls] = total.astype(bf16)

    def split(self):
        pieces = BATCHES[self.batch]
        for part in range(4):
            rows = self.blocks[pl.ds(512 * self.batch, 32 * len(pieces)), :]
            parts = dg(rows, placement(part), 1, 1).astype(bf16)
            for block, slot, owner, piece in piece_slots():
                if block in pieces and slot // 2 == part:
                    i = pieces.index(block)
                    tile = parts[32 * i : 32 * i + 32, 128 * (slot % 2) : 128 * (slot % 2) + 128]
                    self.work[pl.ds(32 * owner, 32), pl.ds(128 * PLACES[piece], 128)] = tile

    def over_cores(self):
        self.core = []
        for xx in range(2):
            ls = self.lanes(2 * xx + 1 - self.c)
            self.core.append(self.send(self.work.at[pl.ds(0, 256), ls], self.work.at[pl.ds(256, 256), ls], self.cpeer))

    def over_x(self):
        for xx in range(2):
            self.core[xx].wait_recv()
        for xx in range(2):
            self.add(256, 2 * xx + self.c)
        ls = self.lanes(2 * (1 - self.x) + self.c)
        self.across = self.send(self.work.at[pl.ds(0, 256), ls], self.work.at[pl.ds(512, 256), ls], self.xpeer)

    def to_owners(self):
        self.across.wait_recv()
        self.add(512, self.frame)
        ls = self.lanes(self.frame)
        self.here = pl.ds(512 * self.batch, self.width)
        mine = pl.ds(pl.multiple_of(32 * self.clip, 32), 32)
        self.received[mine, self.here] = self.work[mine, ls]
        self.owned = []
        for k in range(1, 8):
            j = lax.rem(self.clip + k, 8)
            rows = pl.ds(pl.multiple_of(32 * j, 32), 32)
            self.owned.append(
                self.send(self.work.at[rows, ls], self.received.at[mine, self.here], {"clip": j, "frame": self.frame})
            )

    def by_adapter(self):
        for cp in self.owned:
            cp.wait_recv()
        ls = self.lanes(self.frame)
        self.result[:, ls] = dg(pick_rows(self.nidx), self.received[:, self.here], 0, 0).astype(bf16)
        same = self.result.at[:, ls]
        self.back = [self.send(same, same, p) for p in (self.xpeer, self.cpeer)]

    def spread(self):
        self.back[0].wait_recv()
        same = self.result.at[:, self.lanes(2 * (1 - self.x) + self.c)]
        self.last = self.send(same, same, self.cpeer)

    def finish(self):
        self.back[1].wait_recv()
        self.last.wait_recv()
        for cp in self.sent:
            cp.wait_send()


def layer_kernel(
    gathers, hidx, x_ref, g_ref, hq, hp, hi, ho, had, hnm,
    out, ig, grads, spill,
    wq, wp, wi, wo, ad, nm, nbuf, nidx, received, rcv_a, rcv_b, big, x1, x2, tmp, o2, qkv2, a0, a1, us,
    wsem, ssem, rsem, psem, gssem, grsem, nsem, asem, bsem,
):
    buf_g, buf_d = big.at[0], big.at[1]

    clip = lax.axis_index("clip")
    me = lax.axis_index("frame")
    nf = 4
    peers = [lax.rem(me + k, nf) for k in range(1, nf)]

    fetch = [pltpu.make_async_copy(s, d, wsem.at[10 + i]) for i, (s, d) in enumerate(((x_ref, ig), (g_ref, out)))]
    for cp in fetch:
        cp.start()
    barrier = pltpu.get_barrier_semaphore()
    groups_of = [{"clip": clip, "frame": d} for d in peers]
    loads = {}
    if gathers:
        own = pl.ds(pl.multiple_of(clip * 96, 16), 96)
        local = [
            (hq.at[0], wq.at[0, own]), (hq.at[1], wq.at[1, own]), (hp.at[0], wp.at[0, own]), (hp.at[1], wp.at[1, own]),
            (hp.at[2], wp.at[2, own]), (hi, wi.at[own]), (ho, wo.at[pl.ds(pl.multiple_of(clip * 384, 16), 384)]),
            (had.at[:, cols(me * D, D)], big.at[0, pl.ds(256, 128), pl.ds(D, D)]), (hnm, nbuf.at[pl.ds(pl.multiple_of(clip * 16, 16), 16)]),
            (hidx, nidx.at[pl.ds(pl.multiple_of(clip * 32, 32), 32)]),
        ]
        local = [pltpu.make_async_copy(s, d, wsem.at[i]) for i, (s, d) in enumerate(local)]
        for cp in local:
            cp.start()
        net = Gather(
            {"q": hq, "p": hp, "i": hi, "o": ho},
            {"q": wq, "p": wp, "i": wi, "o": wo},
            (gssem, grsem),
            local[:7],
        )
        owners = [{"clip": lax.rem(clip + k, 8), "frame": me} for k in range(1, 8)]
        greet = groups_of + owners
    else:
        net = None
        for key, src, dst in (
            ("q0", hq.at[0], wq.at[0]), ("p0", hp.at[0], wp.at[0]), ("p1", hp.at[1], wp.at[1]), ("q1", hq.at[1], wq.at[1]),
            ("p2", hp.at[2], wp.at[2]), ("o", ho, wo), ("i", hi, wi), ("ad", had, ad), ("nm", hnm, nm),
        ):
            loads[key] = pltpu.make_async_copy(src, dst, wsem.at[len(loads)])
            loads[key].start()
        greet = groups_of
    for p in greet:
        pl.semaphore_signal(barrier, inc=1, device_id=p, device_id_type=MESH)
    pl.semaphore_wait(barrier, len(greet))

    def need(key, c=""):
        if net is not None:
            net.need(f"{key}{c}")
        elif not c:
            loads[key].wait()

    def need_tiles(key):
        def between(c):
            need(key, c)

        return between

    def tick():
        if net is not None:
            net.tick()

    if gathers:

        def to(peer, src, dst, sems, i):
            cp = pltpu.make_async_remote_copy(
                src_ref=src, dst_ref=dst, send_sem=sems.at[0, i], recv_sem=sems.at[1, i], device_id=peer, device_id_type=MESH
            )
            cp.start()
            return cp

        rows16 = pl.ds(pl.multiple_of(clip * 16, 16), 16)
        rows32 = pl.ds(pl.multiple_of(clip * 32, 32), 32)
        small = [to(p, hidx, nidx.at[rows32], nsem, k) for k, p in enumerate(owners)]
        small += [to(p, hnm, nbuf.at[rows16], nsem, 7 + k) for k, p in enumerate(owners)]
        net.begin()

    def exchange(step, src, index, rcv):
        sent = []
        for k, d in enumerate(peers):
            slot = pl.ds(k * GR, GR)
            o2[slot, :] = dg(onehot(index(d), R), src.get(), 1, 0).astype(bf16)
            cp = pltpu.make_async_remote_copy(
                src_ref=o2.at[slot],
                dst_ref=rcv.at[pl.ds(pl.multiple_of(me * GR, 16), GR)],
                send_sem=ssem.at[step, k],
                recv_sem=rsem.at[step, k],
                device_id={"clip": clip, "frame": d},
                device_id_type=MESH,
            )
            cp.start()
            sent.append(cp)
        rcv[pl.ds(pl.multiple_of(me * GR, 16), GR), :] = dg(onehot(index(me), R), src.get(), 1, 0).astype(bf16)

        def finish():
            for cp in sent:
                cp.wait_recv()
            for cp in sent:
                cp.wait_send()

        return finish

    def gain(k):
        return nm[k : k + 1, :]

    def norm(k, read, put):
        def body(rows):
            hat, _ = norm_rows(read(rows))
            put(rows, (hat * gain(k) + gain(3 + k)).astype(bf16))

        chunks(208, body)

    def rank(h, at, mask, m):
        us[:, pl.ds(32 * m, 32)] = jnp.where(mask, dg(h.get(), ad[:, pl.ds(at, h.width)], 1, 1), 0.0).astype(bf16)

    def forward(m, h, w, width, tile, mask, emit, between=None):
        rank(h, DOWN[m], mask, m)

        def body(c):
            acc = dg(h.get(), w[:, cols(c, tile)], 1, 0)
            acc = acc + dg(us[:, pl.ds(32 * m, 32)], ad[:, cols(UP[m] + c, tile)], 1, 0)
            emit(c, acc)

        tiles(width, tile, body, between)

    def rank_back(m, dz, mask):
        du = jnp.where(mask, dg(dz.get(), ad[:, pl.ds(UP[m], dz.width)], 1, 1), 0.0).astype(bf16)
        us[:, pl.ds(224, 32)] = du

    def backward(m, dz, w, width, tile, mask, emit, between=None):
        rank_back(m, dz, mask)
        backward_rows(m, dz, w, width, tile, emit, between)

    def backward_rows(m, dz, w, width, tile, emit, between=None):

        def body(c):
            acc = dg(dz.get(), w[cols(c, tile), :], 1, 1)
            acc = acc + dg(us[:, pl.ds(224, 32)], ad[:, cols(DOWN[m] + c, tile)], 1, 0)
            emit(c, acc)

        tiles(width, tile, body, between)

    def adapter_grads(m, h, dz):
        for at, side, rows in ((DOWN[m], 224, h), (UP[m], 32 * m, dz)):
            val = dg(us[:, pl.ds(side, 32)], rows.get(), 0, 0).astype(bf16)
            for k in range(rows.width // D):
                wo[pl.ds(32 * PLACES[at // D + k], 32), :] = val[:, k * D : k * D + D]

    p_a0, p_a1 = Part(a0, 0, D), Part(a1, 0, D)
    qkv1, h1 = Part(buf_g, 0, QKV), Part(buf_g, QKV, D)
    xt, o1, m1, spare = (Part(buf_d, D * i, D) for i in range(4))
    p_o2, p_qkv2, p_g, p_d = Part(o2, 0, D), Part(qkv2, 0, QKV), Part(buf_g, 0, FF), Part(buf_d, 0, FF)

    if gathers:
        def quarter_at(frame):
            if isinstance(frame, int):
                return 256 * (frame % 3), D * (frame // 3)
            return pl.multiple_of(256 * lax.rem(frame, 3), 32), pl.multiple_of(D * (frame // 3), 128)

        def quarter(frame, row, rows):
            r0, c0 = quarter_at(frame)
            return pl.ds(pl.multiple_of(r0 + row, 32), rows), pl.ds(c0, D)

        for cp in local[7:]:
            cp.wait()
        for cp in small[:7]:
            cp.wait_recv()
        side = pl.ds(D, D)
        big[0, pl.ds(384, 256), side] = dg(pick_rows(nidx), big[0, pl.ds(256, 128), side], 1, 0).astype(bf16)
        picked = []
        landing = quarter(me, 32 * clip, 32)
        for k, p in enumerate(owners):
            rows = pl.ds(pl.multiple_of(384 + 32 * p["clip"], 32), 32)
            picked.append(to(p, big.at[0, rows, side], big.at[(0,) + landing], asem, k))
        big[(0,) + landing] = big[0, pl.ds(pl.multiple_of(384 + 32 * clip, 32), 32), side]

    for i, (src, dst) in enumerate(((ig, a0), (out, a1))):
        fetch[i].wait()
        for g in range(4):
            dst[pl.ds(GR * g + 192, 16), :] = jnp.zeros((16, D), bf16)
            dst[pl.ds(GR * g, NP), :] = src[g // 2, g % 2]
        if dst is a0:
            arrive = exchange(0, p_a0, to_message, rcv_a)

    mask_t = clip_mask(392)
    mask_s = clip_mask(416)
    if gathers:
        tick()
        for cp in picked:
            cp.wait_recv()

        def block_of(frame):
            return big.at[(0,) + quarter(frame, 0, 256)]

        x, c = me // 2, me % 2
        xpeer, cpeer = {"clip": clip, "frame": (1 - x) * 2 + c}, {"clip": clip, "frame": x * 2 + 1 - c}
        picked.append(to(xpeer, block_of(me), block_of(me), asem, 7))
        picked.append(to(cpeer, block_of(me), block_of(me), asem, 8))
        for cp in small[7:]:
            cp.wait_recv()
        for j in range(8):
            qkv2[pl.ds(0, 16), pl.ds(j * 128, 128)] = nbuf[pl.ds(16 * j, 16), :]
        nm[...] = place(lambda part: qkv2[pl.ds(0, 16), pl.ds(256 * part, 256)])
    else:
        need("ad")
        need("nm")
    for _ in range(T1):
        tick()
    arrive()
    for i in range(4):
        xt.put(dg(onehot(to_patches(i), R), rcv_a[...], 1, 0).astype(bf16), pl.ds(i * GR, GR))
    norm(0, lambda rows: xt.get(rows).astype(f32), lambda rows, v: h1.put(v, rows))
    if gathers:
        picked[7].wait_recv()
        far = (1 - x) * 2 + c
        picked.append(to(cpeer, block_of(far), block_of(far), asem, 9))
        for _ in range(T2):
            tick()
        picked[8].wait_recv()
        picked[9].wait_recv()
        for cp in picked:
            cp.wait_send()
        for block, slot, owner, piece in piece_slots():
            r0, c0 = quarter_at(piece // 6)
            part = big[0, pl.ds(r0 + 32 * owner, 32), pl.ds(c0 + piece % 6 * 128, 128)]
            qkv2[pl.ds(block * 32, 32), pl.ds(slot * 128, 128)] = part
        joined = place(lambda part: qkv2[pl.ds(0, 768), pl.ds(256 * part, 256)]).astype(bf16)
        for block in range(24):
            ad[:, pl.ds(block * D, D)] = joined[block * 32 : block * 32 + 32]
    tick()
    forward(0, h1, wq.at[0], QKV, 768, mask_t, lambda c, acc: qkv1.put(acc.astype(bf16), off=c), need_tiles("q0"))
    tick()
    temporal_loop(lambda rows, n, bias, pairs: attend(qkv1, rows, n, bias, o1, pairs))
    tick()
    need("p0")
    forward(1, o1, wp.at[0], D, 256, mask_t, lambda c, acc: m1.put(acc.astype(bf16), off=c))
    tick()
    need("p1")
    forward(2, m1, wp.at[1], D, 256, mask_t, lambda c, acc: spare.put(acc.astype(bf16), off=c))
    tick()
    arrive = exchange(1, spare, from_patches, rcv_b)
    tick()
    saves = [pltpu.make_async_copy(b, spill.at[i], psem.at[i]) for i, b in enumerate((buf_g, buf_d))]
    for cp in saves:
        cp.start()
    for cp in saves:
        cp.wait()
    for _ in range(T3):
        tick()
    arrive()

    for g in range(4):
        rows = pl.ds(g * GR, GR)
        tb = dg(onehot(to_frames(g), R), rcv_b[...], 1, 0)
        x1[rows, :] = a0[rows, :].astype(f32) + tb
    tick()
    norm(1, lambda rows: x1[rows, :], lambda rows, v: p_o2.put(v, rows))
    tick()
    forward(3, p_o2, wq.at[1], QKV, 768, mask_s, lambda c, acc: p_qkv2.put(acc.astype(bf16), off=c), need_tiles("q1"))
    tick()
    spatial_loop(3, lambda rows, n, bias, pairs: attend(p_qkv2, rows, n, bias, p_o2, pairs))
    tick()
    need("p2")

    def add_spatial(c, acc):
        x2[:, cols(c, 256)] = x1[:, cols(c, 256)] + acc

    forward(4, p_o2, wp.at[2], D, 256, mask_s, add_spatial)
    tick()

    need("o")
    backward(6, p_a1, wo, FF, 768, mask_s, lambda c, acc: p_d.put(acc.astype(bf16), off=c), lambda c: tick())
    us[:, pl.ds(256, 32)] = us[:, pl.ds(224, 32)]

    norm(2, lambda rows: x2[rows, :], lambda rows, v: p_a0.put(v, rows))

    def activate(c, acc):
        tmp_w = acc.shape[1]
        tmp[:, pl.ds(0, tmp_w)] = acc
        @pl.loop(0, R // 32)
        def _(i):
            rows = pl.ds(pl.multiple_of(i * 32, 32), 32)
            v = tmp[rows, pl.ds(0, tmp_w)]
            phi, e = normal_parts(v)
            slope = phi + v * e * 0.3989422804014327
            p_g.put((v * phi).astype(bf16), rows, c)
            p_d.put((p_d.get(rows, c, tmp_w).astype(f32) * slope).astype(bf16), rows, c)

    forward(5, p_a0, wi, FF, 768, mask_s, activate, need_tiles("i"))

    def emit_out(c, acc):
        y = (x2[:, cols(c, 256)] + acc).astype(bf16)
        for g in range(4):
            out[g // 2, g % 2, :, cols(c, 256)] = y[g * GR : g * GR + NP]

    forward(6, p_g, wo, D, 256, mask_s, emit_out)
    if gathers:
        net.finish()
        for cp in small:
            cp.wait_send()

    us[:, pl.ds(224, 32)] = us[:, pl.ds(256, 32)]
    adapter_grads(6, p_g, p_a1)

    def emit_tmp(c, acc):
        tmp[:, cols(c, 256)] = acc

    backward(5, p_d, wi, D, 256, mask_s, emit_tmp)
    adapter_grads(5, p_a0, p_d)
    loads_back = [pltpu.make_async_copy(spill.at[i], b, psem.at[i]) for i, b in enumerate((buf_g, buf_d))]
    for cp in loads_back:
        cp.start()

    def step_two(rows):
        dx = a1[rows, :].astype(f32) + norm_back_rows(x2[rows, :], gain(2), tmp[rows, :])
        x2[rows, :] = dx
        a0[rows, :] = dx.astype(bf16)

    chunks(208, step_two)

    backward(4, p_a0, wp.at[2], D, 256, mask_s, lambda c, acc: p_a1.put(acc.astype(bf16), off=c))
    adapter_grads(4, p_o2, p_a0)
    spatial_loop(2, lambda rows, n, bias, pairs: attend_back(p_qkv2, rows, n, bias, p_a1, pairs, False))
    backward(3, p_qkv2, wq.at[1], D, 256, mask_s, emit_tmp)

    def step_one(rows):
        dx = x2[rows, :] + norm_back_rows(x1[rows, :], gain(1), tmp[rows, :])
        x2[rows, :] = dx
        a0[rows, :] = dx.astype(bf16)

    chunks(208, step_one)
    arrive = exchange(2, p_a0, to_message, rcv_a)
    norm(1, lambda rows: x1[rows, :], lambda rows, v: p_a1.put(v, rows))
    adapter_grads(3, p_a1, p_qkv2)
    if gathers:
        first, second = (Reduce(i, wo, wi, received, grads, nidx, bsem) for i in range(2))
        first.split()
    for cp in loads_back:
        cp.wait()
    arrive()

    if gathers:
        first.over_cores()
    for i in range(4):
        p_a0.put(dg(onehot(to_patches(i), R), rcv_a[...], 1, 0).astype(bf16), pl.ds(i * GR, GR))
    backward(2, p_a0, wp.at[1], D, 256, mask_t, lambda c, acc: p_a1.put(acc.astype(bf16), off=c))
    adapter_grads(2, m1, p_a0)
    if gathers:
        first.over_x()
    backward(1, p_a1, wp.at[0], D, 256, mask_t, lambda c, acc: spare.put(acc.astype(bf16), off=c))
    adapter_grads(1, o1, p_a1)
    temporal_loop(lambda rows, n, bias, pairs: attend_back(qkv1, rows, n, bias, spare, pairs, True))
    if gathers:
        first.to_owners()
    rank_back(0, qkv1, mask_t)
    adapter_grads(0, h1, qkv1)
    if gathers:
        second.split()
        second.over_cores()
        first.by_adapter()
    backward_rows(0, qkv1, wq.at[0], D, 256, emit_tmp)
    if gathers:
        second.over_x()
        first.spread()

    def step_zero(rows):
        dx = norm_back_rows(xt.get(rows).astype(f32), gain(0), tmp[rows, :])
        a0[rows, :] = dx.astype(bf16)

    chunks(208, step_zero)
    if gathers:
        second.to_owners()
    arrive = exchange(3, p_a0, from_patches, rcv_b)
    if gathers:
        second.by_adapter()
        first.finish()
        second.spread()
    arrive()
    for g in range(4):
        dxt = dg(onehot(to_frames(g), R), rcv_b[...], 1, 0)
        total = x2[pl.ds(g * GR, GR), :] + dxt
        ig[g // 2, g % 2] = total.astype(bf16)[:NP]
    if gathers:
        second.finish()
    else:
        for block in range(24):
            grads[:, pl.ds(block * D, D)] = wo[pl.ds(32 * PLACES[block], 32), :]


def layer(gathers, index_rows, x, g, hq, hp, hi, ho, ad, nm):
    vm = pl.BlockSpec(memory_space=pltpu.VMEM)
    hbm = pl.BlockSpec(memory_space=pl.ANY)
    dma = pltpu.SemaphoreType.DMA
    rows = lambda w, t=bf16: pltpu.VMEM((R, w), t)
    ng = len(gather_groups()) if gathers else 1
    return pl.pallas_call(
        functools.partial(layer_kernel, gathers),
        out_shape=[
            jax.ShapeDtypeStruct(x.shape, bf16),
            jax.ShapeDtypeStruct(x.shape, bf16),
            jax.ShapeDtypeStruct((128, 24 * 128) if gathers else (32, ADW), bf16),
            jax.ShapeDtypeStruct((2, R, FF), bf16),
        ],
        in_specs=[hbm] * 9,
        out_specs=[vm] * 3 + [hbm],
        scratch_shapes=[
            pltpu.VMEM((2, D, QKV), bf16), pltpu.VMEM((3, D, D), bf16), pltpu.VMEM((D, FF), bf16), pltpu.VMEM((FF, D), bf16),
            pltpu.VMEM((32, ADW), bf16), pltpu.VMEM((16, D), f32), pltpu.VMEM((128, 128), bf16),
            pltpu.VMEM((256, 128), jnp.int32), pltpu.VMEM((256, D), bf16),
            rows(D), rows(D), pltpu.VMEM((2, R, FF), bf16), rows(D, f32), rows(D, f32), rows(D, f32),
            rows(D), rows(QKV), rows(D), rows(D), rows(384),
            dma((12,)), dma((4, 3)), dma((4, 3)), dma((2,)), dma((22 * ng,)), dma((22 * ng,)), dma((2, 14)), dma((2, 10)), dma((2, 32)),
        ],
        compiler_params=pltpu.CompilerParams(
            collective_id=1, has_side_effects=True, vmem_limit_bytes=64 * 2**20 - 2**17
        ),
        name="layer",
    )(index_rows, x, g, hq, hp, hi, ho, ad, nm)


def piece_widths(w):
    return [w] * 6 + [4 * w] + [3 * w] * 2 + [w] * 4 + [4 * w]


def pack_adapters(adapt_down, adapt_down_wide, adapt_up_qkv, adapt_up, adapt_up_wide):
    adapters = adapt_down_wide.shape[0]

    def flat(v):
        return v.reshape(adapters, RANK, -1)

    return jnp.concatenate(
        [
            flat(adapt_down.transpose(1, 3, 0, 2)),
            flat(adapt_down_wide.transpose(0, 2, 1)),
            flat(adapt_up_qkv.transpose(1, 2, 0, 3)),
            flat(adapt_up.transpose(1, 2, 0, 3)),
            flat(adapt_up_wide),
        ],
        axis=-1,
    )


def join_pieces(parts, w):
    joined, at = [], 0
    for width in piece_widths(w):
        piece = parts[:, :, at : at + width]
        joined.append(piece.transpose(1, 0, 2).reshape(parts.shape[1], -1))
        at += width
    return jnp.concatenate(joined, axis=-1)


def split_pieces(rows, w, owners):
    parts, at = [], 0
    for width in piece_widths(w):
        piece = rows[:, at : at + width * owners]
        parts.append(piece.reshape(rows.shape[0], owners, width).transpose(1, 0, 2))
        at += width * owners
    return jnp.concatenate(parts, axis=-1)


def per_device(
    inputs,
    out_grad,
    adapter_index,
    norm_gain,
    norm_bias,
    qkv_weight,
    proj_weight,
    mlp_in,
    mlp_out,
    adapt_down,
    adapt_down_wide,
    adapt_up_qkv,
    adapt_up,
    adapt_up_wide,
):
    owners = lax.axis_size("clip")
    adapters = adapt_down_wide.shape[0]
    clips = inputs.shape[0]
    w = norm_gain.shape[1]
    packed = pack_adapters(adapt_down, adapt_down_wide, adapt_up_qkv, adapt_up, adapt_up_wide)
    norms = jnp.concatenate([norm_gain, norm_bias], axis=0)
    if owners == 8:
        index_rows = adapter_index[:, None] * RANK + jnp.arange(RANK, dtype=jnp.int32)[None, :]
        index_rows = jnp.broadcast_to(index_rows.reshape(clips * RANK, 1), (clips * RANK, 128))
        pieces = packed.reshape(adapters * RANK, 24, w)
        table = jnp.pad(pieces, ((0, 0), (0, 0), (0, 128 - w))).reshape(adapters * RANK, 24 * 128)
        own_norms = jnp.pad(norms, ((0, 10), (0, 128 - w)))
        output, input_grad, grads, _ = layer(
            True, index_rows, inputs, out_grad, qkv_weight, proj_weight, mlp_in, mlp_out, table, own_norms
        )
        grads = grads.reshape(adapters, RANK, 24, 128)[..., :w].astype(f32)
        summed = jnp.concatenate([grads[:, :, PLACES[p]] for p in range(24)], axis=-1)
    else:
        full_qkv = lax.all_gather(qkv_weight, "clip", axis=1, tiled=True)
        full_proj = lax.all_gather(proj_weight, "clip", axis=1, tiled=True)
        full_in = lax.all_gather(mlp_in, "clip", axis=0, tiled=True)
        full_out = lax.all_gather(mlp_out, "clip", axis=0, tiled=True)
        table = lax.all_gather(packed, "clip", axis=0)
        all_norms = lax.all_gather(norms, "clip", axis=0)
        nm = jnp.pad(all_norms.transpose(1, 0, 2).reshape(6, D).astype(f32), ((0, 10), (0, 0)))
        chosen = jnp.take(table, adapter_index, axis=1).reshape(owners, clips * RANK, 24 * w)
        ad = join_pieces(chosen, w)
        output, input_grad, grads, _ = layer(
            False, adapter_index, inputs, out_grad, full_qkv, full_proj, full_in, full_out, ad, nm
        )
        parts = split_pieces(grads, w, owners)
        parts = lax.all_to_all(parts, "clip", split_axis=0, concat_axis=0, tiled=True)
        every = lax.all_gather(adapter_index, "clip", axis=0, tiled=True)
        pick = (every[:, None] == jnp.arange(adapters, dtype=jnp.int32)[None, :]).astype(bf16)
        summed = jnp.einsum(
            "ca,crm->arm", pick, parts.reshape(owners * clips, RANK, 24 * w), preferred_element_type=f32
        )
        summed = lax.psum(summed.astype(bf16), "frame").astype(f32)
    return (output, input_grad) + unpack_grads(summed, w)


def unpack_grads(summed, w):
    adapters = summed.shape[0]
    down = summed[:, :, : 6 * w].reshape(adapters, RANK, 6, w).transpose(2, 0, 3, 1)
    down_wide = summed[:, :, 6 * w : 10 * w].transpose(0, 2, 1)
    up_qkv = summed[:, :, 10 * w : 16 * w].reshape(adapters, RANK, 2, 3 * w).transpose(2, 0, 1, 3)
    up = summed[:, :, 16 * w : 20 * w].reshape(adapters, RANK, 4, w).transpose(2, 0, 1, 3)
    return (down, down_wide, up_qkv, up, summed[:, :, 20 * w :])


def solution(mesh):
    return jax.shard_map(
        per_device,
        mesh=mesh,
        in_specs=(
            P("clip", "frame", None, None),
            P("clip", "frame", None, None),
            P("clip"),
            P(None, "clip"),
            P(None, "clip"),
            P(None, "clip", None),
            P(None, "clip", None),
            P("clip", None),
            P("clip", None),
            P(None, None, "clip", None),
            P(None, "clip", None),
            P(None, None, None, "clip"),
            P(None, None, None, "clip"),
            P(None, None, "clip"),
        ),
        out_specs=(
            P("clip", "frame", None, None),
            P("clip", "frame", None, None),
            P(None, None, "clip", None),
            P(None, "clip", None),
            P(None, None, None, "clip"),
            P(None, None, None, "clip"),
            P(None, None, "clip"),
        ),
        check_vma=False,
    )
```
